128 devices in a mesh: dp: 16 (over z, y), ctx: 2 (over x_hi), tp: 4 (over x_lo, core).
Axes of the slice: x: 4 (x_hi: 2, x_lo: 2; x = x_hi * 2 + x_lo), y: 4, z: 4, core: 2. Of those that a mesh axis runs over, the one named last changes fastest.
Arguments:
- stream: bfloat16 [16, 2048, 768], P('dp', 'ctx'), may hold values from -6 to 6
- norm_gain: bfloat16 [768], P('dp'), may hold values from 0.5 to 1.5
- w_gate: bfloat16 [768, 1536], P('dp', 'tp'), may hold values from -0.21875 to 0.21875
- w_value: bfloat16 [768, 1536], P('dp', 'tp'), may hold values from -0.21875 to 0.21875
- w_step: bfloat16 [768, 24], P('dp', 'tp'), may hold values from -0.21875 to 0.21875
- w_state: bfloat16 [768, 256], P('dp'), may hold values from -0.21875 to 0.21875
- w_out: bfloat16 [1536, 768], P('tp', 'dp'), may hold values from -0.15625 to 0.15625
- conv_value: float32 [4, 1536], P(None, 'tp'), may hold values from -3 to 3
- conv_value_bias: float32 [1536], P('tp'), may hold values from -3 to 3
- conv_state: float32 [4, 256], replicated, may hold values from -3 to 3
- conv_state_bias: float32 [256], replicated, may hold values from -3 to 3
- step_bias: float32 [24], P('tp'), may hold values from -5 to -1
- decay_log: float32 [24], P('tp'), may hold values from -5 to 0.5
- skip_gain: float32 [24], P('tp'), may hold values from 0.5 to 1.5
- inner_gain: float32 [1536], P('tp'), may hold values from 0.5 to 1.5
- cotangent: bfloat16 [16, 2048, 768], P('dp', 'ctx'), may hold values from -6 to 6
Outputs:
- mixed_out: bfloat16 [16, 2048, 768], P('dp', 'ctx')
- d_stream: float32 [16, 2048, 768], P('dp', 'ctx')
- grad_norm_gain: float32 [768], P('dp')
- grad_w_gate: float32 [768, 1536], P('dp', 'tp')
- grad_w_value: float32 [768, 1536], P('dp', 'tp')
- grad_w_step: float32 [768, 24], P('dp', 'tp')
- grad_w_state: float32 [768, 256], P('dp')
- grad_w_out: float32 [1536, 768], P('tp', 'dp')
- grad_conv_value: float32 [4, 1536], P(None, 'tp')
- grad_conv_value_bias: float32 [1536], P('tp')
- grad_conv_state: float32 [4, 256], replicated
- grad_conv_state_bias: float32 [256], replicated
- grad_step_bias: float32 [24], P('tp')
- grad_decay_log: float32 [24], P('tp')
- grad_skip_gain: float32 [24], P('tp')
- grad_inner_gain: float32 [1536], P('tp')
The draws below stay inside these ranges and needn't reach their ends.
All inputs are finite; a program needn't handle non-finite values.
Results may differ from the reference program's by a relative error of at most 0.0095.
The reference program's roundings to bfloat16 on the way count: a program that leaves them out, or rounds other values in their place, can miss the bound.
Values may be sent and summed in bfloat16 or wider, within the bound.
A program may use at most 128 MiB of HBM per device.

```python
import jax
import jax.numpy as jnp
from jax import lax

D = 768
HEADS = 24
HEAD = 64
STATE = 128
CONV = 4
GROUP = 256
SEQ = 2048
INNER = 1536
BATCH = 16


def steps_of(rng, dims, cuts, least, largest):
    factor_of, own = 1.0, jax.random.fold_in(rng, 6)
    for dim, blocks in cuts:
        steps = jnp.exp(jax.random.uniform(jax.random.fold_in(own, dim), (blocks,), jnp.float32, least / len(cuts), largest / len(cuts)))
        factor_of = factor_of * jnp.repeat(steps, dims[dim] // blocks).reshape([-1 if axis == dim else 1 for axis in range(len(dims))])
    return factor_of


def scatter_about(own_key, extent, deviation, bound, shards=(), kind=jnp.bfloat16):
    array = jax.random.normal(own_key, extent, jnp.float32) * deviation
    if len(shards) > 0:
        array = steps_of(own_key, extent, shards, -0.22, 0.18) * array
    return jnp.clip(array, min=-bound, max=bound).astype(kind)


def setup_inputs(seed: int = 0) -> dict:
    key_of = jax.random.split(jax.random.key(seed), 17)
    return {
        "stream": scatter_about(key_of[0], (BATCH, SEQ, D), 1.0, 6.0, ((0, 16), (1, 2))),
        "norm_gain": jnp.clip(1.0 + 0.1 * jax.random.normal(key_of[1], (D,), jnp.float32), 0.5, 1.5).astype(jnp.bfloat16),
        "w_gate": scatter_about(key_of[2], (D, INNER), D ** -0.5, 0.21875, ((0, 16), (1, 4))),
        "w_value": scatter_about(key_of[3], (D, INNER), D ** -0.5, 0.21875, ((0, 16), (1, 4))),
        "w_step": scatter_about(key_of[4], (D, HEADS), D ** -0.5, 0.21875, ((0, 16), (1, 4))),
        "w_state": scatter_about(key_of[5], (D, 2 * STATE), D ** -0.5, 0.21875, ((0, 16),)),
        "w_out": scatter_about(key_of[6], (INNER, D), INNER ** -0.5, 0.15625, ((0, 4), (1, 16))),
        "conv_value": scatter_about(key_of[7], (CONV, INNER), CONV ** -0.5, 3.0, ((1, 4),), jnp.float32),
        "conv_value_bias": scatter_about(key_of[8], (INNER,), 0.5, 3.0, ((0, 4),), jnp.float32),
        "conv_state": scatter_about(key_of[9], (CONV, 2 * STATE), CONV ** -0.5, 3.0, (), jnp.float32),
        "conv_state_bias": scatter_about(key_of[10], (2 * STATE,), 0.5, 3.0, (), jnp.float32),
        "step_bias": jnp.clip(-5.0 + 4.0 * jax.random.uniform(key_of[11], (HEADS,), jnp.float32) ** steps_of(key_of[11], (HEADS,), ((0, 4),), -0.2, 0.2), -5.0, -1.0),
        "decay_log": jnp.clip(-5.0 + 5.5 * jax.random.uniform(key_of[12], (HEADS,), jnp.float32) ** steps_of(key_of[12], (HEADS,), ((0, 4),), -0.2, 0.2), -5.0, 0.5),
        "skip_gain": jnp.clip(0.5 + 1.0 * jax.random.uniform(key_of[13], (HEADS,), jnp.float32) ** steps_of(key_of[13], (HEADS,), ((0, 4),), -0.2, 0.2), 0.5, 1.5),
        "inner_gain": jnp.clip(1.0 + 0.1 * jax.random.normal(key_of[14], (INNER,), jnp.float32), 0.5, 1.5),
        "cotangent": scatter_about(key_of[15], (BATCH, SEQ, D), 1.0, 6.0, ((0, 16), (1, 2))),
    }


EPS = 1e-05
HIGH = lax.Precision.HIGHEST

@jax.custom_vjp
def low(v):
    return lax.optimization_barrier(v.astype(jnp.bfloat16)).astype(jnp.float32)

@jax.custom_vjp
def low_back(v):
    return v

def low_keep(v):
    return (low(v), None)

def low_pass(kept, grad):
    return (grad,)

def back_keep(v):
    return (v, None)

def back_low(kept, grad):
    return (low(grad),)
low.defvjp(low_keep, low_pass)
low_back.defvjp(back_keep, back_low)

def group_step(state_in, pieces):
    values, keys_low, reads_low, step_val, log_rate = pieces
    cum_log = jnp.cumsum(log_rate, axis=0)
    cum_heads = cum_log.T
    lower_mask = jnp.arange(GROUP)[:, None] >= jnp.arange(GROUP)[None, :]
    spread = jnp.where(lower_mask[None], cum_heads[:, :, None] - cum_heads[:, None, :], -1e+30)
    decays = jnp.exp(spread)
    inner_prod = jnp.dot(reads_low, keys_low.T, precision=HIGH)
    weights = low(inner_prod[None] * decays * step_val.T[:, None, :])
    local_out = jnp.einsum('hts,shp->thp', weights, values, precision=HIGH)
    carried_pre = low_back(jnp.einsum('tn,hpn->thp', reads_low, low(state_in), precision=HIGH))
    carried_out = jnp.exp(cum_log)[:, :, None] * carried_pre
    last_cum = cum_log[-1]
    scales = step_val * jnp.exp(last_cum[None] - cum_log)
    weighted = low(values * scales[:, :, None])
    fresh_state = low_back(jnp.einsum('shp,sn->hpn', weighted, keys_low, precision=HIGH))
    state_out = jnp.exp(last_cum)[:, None, None] * state_in + fresh_state
    return (state_out, local_out + carried_out)

def block_forward(stream, norm_gain, w_gate, w_value, w_step, w_state, w_out, conv_value, conv_value_bias, conv_state, conv_state_bias, step_bias, decay_log, skip_gain, inner_gain):
    length = stream.shape[0]
    scale_zero = lax.rsqrt(lax.optimization_barrier(jnp.mean(stream * stream, axis=-1, keepdims=True)) + EPS)
    normed = low(stream * scale_zero * norm_gain)
    gate_out = low_back(jnp.dot(normed, w_gate, precision=HIGH))
    value_pre = low_back(low(jnp.dot(normed, w_value, precision=HIGH)))
    state_pre = low_back(low(jnp.dot(normed, w_state, precision=HIGH)))
    step_raw = low_back(jnp.dot(normed, w_step, precision=HIGH))
    conv_input = jnp.concatenate([value_pre, state_pre], axis=1)
    kernel = jnp.concatenate([conv_value, conv_state], axis=1)
    kernel_bias = jnp.concatenate([conv_value_bias, conv_state_bias])
    padded = jnp.pad(conv_input, ((CONV - 1, 0), (0, 0)))
    conv_sum = kernel_bias + sum((kernel[offset] * padded[offset:offset + length] for offset in range(CONV)))
    activated = jax.nn.silu(conv_sum)
    values = low(activated[:, :INNER]).reshape(length, HEADS, HEAD)
    keys_low = low(activated[:, INNER:INNER + STATE])
    reads_low = low(activated[:, INNER + STATE:])
    step_val = jax.nn.softplus(step_raw + step_bias)
    log_rate = -jnp.exp(decay_log) * step_val
    blocks = length // GROUP
    pieces = (values.reshape(blocks, GROUP, HEADS, HEAD), keys_low.reshape(blocks, GROUP, STATE), reads_low.reshape(blocks, GROUP, STATE), step_val.reshape(blocks, GROUP, HEADS), log_rate.reshape(blocks, GROUP, HEADS))
    zero_state = jnp.zeros((HEADS, HEAD, STATE), jnp.float32)
    unused, group_outs = lax.scan(jax.checkpoint(group_step), zero_state, pieces)
    ssd_out = group_outs.reshape(length, HEADS, HEAD) + skip_gain[None, :, None] * values
    ssd_out = low_back(ssd_out.reshape(length, INNER))
    gated = ssd_out * jax.nn.silu(gate_out)
    scale_one = lax.rsqrt(lax.optimization_barrier(jnp.mean(gated * gated, axis=-1, keepdims=True)) + EPS)
    normal_out = low(gated * scale_one * inner_gain)
    return stream + jnp.dot(normal_out, w_out, precision=HIGH)

def add_pair(left_val, right_val):
    return left_val + right_val

def reference(stream, norm_gain, w_gate, w_value, w_step, w_state, w_out, conv_value, conv_value_bias, conv_state, conv_state_bias, step_bias, decay_log, skip_gain, inner_gain, cotangent):
    weights_f = tuple((param.astype(jnp.float32) for param in (norm_gain, w_gate, w_value, w_step, w_state, w_out, conv_value, conv_value_bias, conv_state, conv_state_bias, step_bias, decay_log, skip_gain, inner_gain)))

    def one_sequence(totals_in, pair_in):
        sequence, cot_seq = pair_in
        output, pullback = jax.vjp(block_forward, sequence.astype(jnp.float32), *weights_f)
        grads = pullback(cot_seq.astype(jnp.float32))
        totals_out = jax.tree.map(add_pair, totals_in, tuple(grads[1:]))
        return (totals_out, (output.astype(jnp.bfloat16), grads[0]))
    zero_grads = tuple((jnp.zeros_like(param) for param in weights_f))
    totals, outputs = lax.scan(one_sequence, zero_grads, (stream, cotangent))
    return (outputs[0], outputs[1], totals[0], totals[1], totals[2], totals[3], totals[4], totals[5], totals[6], totals[7], totals[8], totals[9], totals[10], totals[11], totals[12], totals[13])
```

```python
import jax
import jax.numpy as jnp
from jax import lax
from jax.experimental import pallas as pl
from jax.experimental.pallas import tpu as pltpu
from jax.sharding import PartitionSpec as P

D = 768
HEAD = 64
STATE = 128
CONV = 4
GROUP = 256
INNER = 1536


EPS = 1e-05
HIGH = lax.Precision.HIGHEST


MESH = pl.DeviceIdType.MESH
VM = pl.BlockSpec(memory_space=pltpu.VMEM)
ANY = pl.BlockSpec(memory_space=pl.ANY)
DP = 16
ROWS = 48
WIDE = 1536
DMA = pltpu.SemaphoreType.DMA


def params(ident, limit=32):
    return pltpu.CompilerParams(
        collective_id=ident, has_side_effects=True, vmem_limit_bytes=limit * 1024 * 1024
    )


def remote(source, target, send, recv, **where):
    return pltpu.make_async_remote_copy(
        src_ref=source,
        dst_ref=target,
        send_sem=send,
        recv_sem=recv,
        device_id=where,
        device_id_type=MESH,
    )


def greet(peers):
    barrier = pltpu.get_barrier_semaphore()
    for where in peers:
        pl.semaphore_signal(barrier, inc=1, device_id=where, device_id_type=MESH)
    pl.semaphore_wait(barrier, len(peers))


def dp_ring():
    me = lax.axis_index("dp")
    return me, [lax.rem(me + hop, DP) for hop in range(1, DP)]


def gather_kernel(shard, edge, full, edge_in, send, recv, edge_send, edge_recv, own):
    me, others = dp_ring()
    partner = 1 - lax.axis_index("ctx")
    greet([{"dp": peer} for peer in others] + [{"ctx": partner}])
    mine = pl.ds(pl.multiple_of(me * ROWS, 16), ROWS)
    copies = [remote(edge, edge_in, edge_send, edge_recv, ctx=partner)]
    copies += [
        remote(shard, full.at[mine], send.at[hop], recv.at[hop], dp=peer)
        for hop, peer in enumerate(others)
    ]
    for copy in copies:
        copy.start()
    keep = pltpu.make_async_copy(shard, full.at[mine], own)
    keep.start()
    keep.wait()
    for copy in copies:
        copy.wait()


def gather_weights(shard, edge):
    return pl.pallas_call(
        gather_kernel,
        out_shape=(
            jax.ShapeDtypeStruct((DP * ROWS, WIDE), shard.dtype),
            jax.ShapeDtypeStruct(edge.shape, edge.dtype),
        ),
        in_specs=[VM, VM],
        out_specs=(VM, VM),
        scratch_shapes=[DMA((DP - 1,)), DMA((DP - 1,)), DMA, DMA, DMA],
        compiler_params=params(1),
    )(shard, edge)


def scatter_kernel(
    grads, small, out, small_out, held, small_held, total, arrived, total_in, arrived_in,
    send, recv, small_send, small_recv, pair_send, pair_recv, own
):
    me, others = dp_ring()
    partner = 1 - lax.axis_index("ctx")
    greet([{"dp": peer} for peer in others] + [{"ctx": partner}])
    copies = []
    for hop, peer in enumerate(others):
        rows = pl.ds(pl.multiple_of(peer * ROWS, 16), ROWS)
        copies.append(remote(grads.at[rows], held.at[me], send.at[hop], recv.at[hop], dp=peer))
        copies.append(
            remote(small, small_held.at[me], small_send.at[hop], small_recv.at[hop], dp=peer)
        )
    for copy in copies:
        copy.start()
    rows = pl.ds(pl.multiple_of(me * ROWS, 16), ROWS)
    keeps = [
        pltpu.make_async_copy(grads.at[rows], held.at[me], own.at[0]),
        pltpu.make_async_copy(small, small_held.at[me], own.at[1]),
    ]
    for keep in keeps:
        keep.start()
    for keep in keeps:
        keep.wait()
    for copy in copies:
        copy.wait()
    total[...] = jnp.zeros_like(total)
    arrived[...] = jnp.zeros_like(arrived)

    def add(index, carry):
        total[...] += held[index].astype(jnp.float32)
        arrived[...] += small_held[index]
        return carry

    lax.fori_loop(0, DP, add, 0)
    pairs = [
        remote(total, total_in, pair_send.at[0], pair_recv.at[0], ctx=partner),
        remote(arrived, arrived_in, pair_send.at[1], pair_recv.at[1], ctx=partner),
    ]
    for copy in pairs:
        copy.start()
    for copy in pairs:
        copy.wait()
    out[...] = total[...] + total_in[...]
    small_out[...] = arrived[...] + arrived_in[...]


def scatter_grads(grads, small):
    block = (ROWS, WIDE)
    f32 = jnp.float32
    return pl.pallas_call(
        scatter_kernel,
        out_shape=(
            jax.ShapeDtypeStruct(block, f32),
            jax.ShapeDtypeStruct(small.shape, f32),
        ),
        in_specs=[VM, VM],
        out_specs=(VM, VM),
        scratch_shapes=[
            pltpu.VMEM((DP, *block), grads.dtype),
            pltpu.VMEM((DP, *small.shape), f32),
            pltpu.VMEM(block, f32),
            pltpu.VMEM(small.shape, f32),
            pltpu.VMEM(block, f32),
            pltpu.VMEM(small.shape, f32),
            DMA((DP - 1,)),
            DMA((DP - 1,)),
            DMA((DP - 1,)),
            DMA((DP - 1,)),
            DMA((2,)),
            DMA((2,)),
            DMA((2,)),
        ],
        compiler_params=params(2),
    )(grads, small)


def swap_kernel(mine, other, send, recv):
    partner = 1 - lax.axis_index("ctx")
    greet([{"ctx": partner}])
    copy = remote(mine, other, send, recv, ctx=partner)
    copy.start()
    copy.wait()


def swap_ctx(value, ident):
    return pl.pallas_call(
        swap_kernel,
        out_shape=jax.ShapeDtypeStruct(value.shape, value.dtype),
        in_specs=[VM],
        out_specs=VM,
        scratch_shapes=[DMA, DMA],
        compiler_params=params(ident),
    )(value)


def sum_all_kernel(part, out, held, send, recv):
    me = lax.axis_index("tp")
    others = [lax.rem(me + hop, 4) for hop in range(1, 4)]
    greet([{"tp": peer} for peer in others])
    copies = [
        remote(part, held.at[me], send.at[hop], recv.at[hop], tp=peer)
        for hop, peer in enumerate(others)
    ]
    for copy in copies:
        copy.start()
    held[me] = part[...]
    for copy in copies:
        copy.wait()
    out[...] = (held[0] + held[1]) + (held[2] + held[3])


def sum_all(part, ident):
    return pl.pallas_call(
        sum_all_kernel,
        out_shape=jax.ShapeDtypeStruct(part.shape, part.dtype),
        in_specs=[VM],
        out_specs=VM,
        scratch_shapes=[pltpu.VMEM((4, *part.shape), part.dtype), DMA((3,)), DMA((3,))],
        compiler_params=params(ident),
    )(part)


def tp_sum_kernel(part, base, out, half_in, quarter_out, quarter_in, send, recv):
    me = lax.axis_index("tp")
    core, chip = lax.rem(me, 2), lax.div(me, 2)
    twin, across = me + 1 - 2 * core, me + 2 - 4 * chip
    greet([{"tp": twin}, {"tp": across}])
    size = part.shape[0] // 4

    def quarter(c, h):
        return pl.ds(pl.multiple_of((2 * c + h) * size, size), size)

    keep, give = quarter(core, chip), quarter(core, 1 - chip)
    for_twin = [quarter(1 - core, 1 - chip), quarter(1 - core, chip)]
    first = [
        remote(part.at[rows], half_in.at[place], send.at[place], recv.at[place], tp=twin)
        for place, rows in enumerate(for_twin)
    ]
    for copy in first:
        copy.start()
    f32 = jnp.float32
    first[0].wait()
    quarter_out[...] = (part[give].astype(f32) + half_in[0].astype(f32)).astype(part.dtype)
    over = remote(quarter_out, quarter_in, send.at[2], recv.at[2], tp=across)
    over.start()
    first[1].wait()
    over.wait()
    total = part[keep].astype(f32) + half_in[1].astype(f32) + quarter_in[...].astype(f32)
    if base is not None:
        total = total + base[keep].astype(f32)
    out[keep] = total.astype(out.dtype)
    back = remote(out.at[keep], out.at[keep], send.at[3], recv.at[3], tp=across)
    beside = remote(out.at[keep], out.at[keep], send.at[4], recv.at[4], tp=twin)
    back.start()
    beside.start()
    back.wait()
    relay = remote(out.at[give], out.at[give], send.at[5], recv.at[5], tp=twin)
    relay.start()
    beside.wait()
    relay.wait()


def tp_sum_bare(part, out, *rest):
    tp_sum_kernel(part, None, out, *rest)


def tp_sum(part, base, ident):
    rows, columns = part.shape
    operands = (part,) if base is None else (part, base)
    return pl.pallas_call(
        tp_sum_bare if base is None else tp_sum_kernel,
        out_shape=jax.ShapeDtypeStruct(part.shape, part.dtype),
        in_specs=[VM] * len(operands),
        out_specs=VM,
        scratch_shapes=[
            pltpu.VMEM((2, rows // 4, columns), part.dtype),
            pltpu.VMEM((rows // 4, columns), part.dtype),
            pltpu.VMEM((rows // 4, columns), part.dtype),
            DMA((6,)),
            DMA((6,)),
        ],
        compiler_params=params(ident),
    )(*operands)


def matmul(left, right):
    return jnp.dot(left, right, preferred_element_type=jnp.float32)


def back_matmul(grad_rows, weight):
    return lax.dot_general(
        grad_rows, weight, (((1,), (1,)), ((), ())), preferred_element_type=jnp.float32
    )


def silu_grad(pre_act):
    sigmoid_val = jax.nn.sigmoid(pre_act)
    return sigmoid_val * (1.0 + pre_act * (1.0 - sigmoid_val))


def chain(entering, decay, fresh, order):
    carry, inputs = entering, {}
    for block in order:
        inputs[block] = carry
        carry = decay[block][:, None, None] * carry + fresh[block]
    return carry, jnp.stack([inputs[block] for block in sorted(inputs)])


def per_device(
    stream,
    norm_gain,
    w_gate,
    w_value,
    w_step,
    w_state,
    w_out,
    conv_value,
    conv_value_bias,
    conv_state,
    conv_state_bias,
    step_bias,
    decay_log,
    skip_gain,
    inner_gain,
    cotangent,
):
    tokens = stream.shape[1]
    local_heads = step_bias.shape[0]
    local_inner = inner_gain.shape[0]
    blocks = tokens // GROUP
    bfloat = jnp.bfloat16
    f32 = jnp.float32
    ctx = lax.axis_index("ctx")
    tp = lax.axis_index("tp")
    mix = local_inner + 2 * STATE
    thin = mix + local_inner
    shard = jnp.concatenate(
        [
            w_value,
            w_state,
            w_gate,
            w_step,
            norm_gain[:, None],
            jnp.zeros((ROWS, 128 - local_heads - 1), bfloat),
            w_out.T,
        ],
        axis=1,
    )
    full, edge = gather_weights(shard, stream[0, tokens - 16 :])
    projection = full[:, : thin + 128]
    out_t = full[:, thin + 128 :]
    gain_zero = full[:, thin + local_heads].astype(f32)[None]
    source = stream[0].astype(f32)

    def normalise(rows):
        scale = lax.rsqrt(jnp.mean(rows * rows, axis=-1, keepdims=True) + EPS)
        return scale, (rows * scale * gain_zero).astype(bfloat)

    scale_zero, normed = normalise(source)
    projected = matmul(normed, projection)
    conv_input = projected[:, :mix].astype(bfloat)
    gate_out = projected[:, mix:thin]
    step_raw = projected[:, thin : thin + local_heads]
    edge_normed = normalise(edge.astype(f32))[1]
    edge_rows = matmul(edge_normed, full[:, :mix])[13:]
    edge_rows = jnp.where(ctx == 0, 0.0, edge_rows).astype(bfloat)
    padded = jnp.concatenate([edge_rows, conv_input], axis=0).astype(f32)
    kernel = jnp.concatenate([conv_value, conv_state], axis=1)
    kernel_bias = jnp.concatenate([conv_value_bias, conv_state_bias])
    conv_sum = kernel_bias + sum(
        (kernel[offset] * padded[offset : offset + tokens] for offset in range(CONV))
    )
    activated = jax.nn.silu(conv_sum)
    values = activated[:, :local_inner].astype(bfloat).reshape(blocks, GROUP, local_heads, HEAD)
    keys_low = (
        activated[:, local_inner : local_inner + STATE].astype(bfloat).reshape(blocks, GROUP, STATE)
    )
    reads_low = activated[:, local_inner + STATE :].astype(bfloat).reshape(blocks, GROUP, STATE)
    step_val = jax.nn.softplus(step_raw + step_bias)
    decay_rate = jnp.exp(decay_log)
    log_rate = -decay_rate * step_val
    step_blocks = step_val.reshape(blocks, GROUP, local_heads).transpose(0, 2, 1)
    lower_mask = jnp.arange(GROUP)[:, None] >= jnp.arange(GROUP)[None, :]
    lower_ones = lower_mask.astype(f32)
    cum_log = jnp.einsum(
        "ts,csh->cht", lower_ones, log_rate.reshape(blocks, GROUP, local_heads), precision=HIGH
    )
    last_cum = cum_log[:, :, -1]
    decays = jnp.exp(jnp.where(lower_mask, cum_log[:, :, :, None] - cum_log[:, :, None, :], -1e30))
    inner_prod = jnp.einsum("ctn,csn->cts", reads_low, keys_low, preferred_element_type=f32)
    weights = inner_prod[:, None] * decays * step_blocks[:, :, None, :]
    weights_low = weights.astype(bfloat)
    local_out = jnp.einsum("chts,cshp->cthp", weights_low, values, preferred_element_type=f32)
    scales = step_blocks * jnp.exp(last_cum[:, :, None] - cum_log)
    scales_t = scales.transpose(0, 2, 1)
    values_f = values.astype(f32)
    weighted = (values_f * scales_t[..., None]).astype(bfloat)
    fresh_state = jnp.einsum("cshp,csn->chpn", weighted, keys_low, preferred_element_type=f32)
    block_decay = jnp.exp(last_cum)
    zero_state = jnp.zeros((local_heads, HEAD, STATE), f32)
    forward, backward = range(blocks), range(blocks - 1, -1, -1)
    device_state = chain(zero_state, block_decay, fresh_state, forward)[0]
    entering = jnp.where(ctx == 1, swap_ctx(device_state, 3), 0.0)
    states_in = chain(entering, block_decay, fresh_state, forward)[1]
    states_low = states_in.astype(bfloat)
    carried_pre = jnp.einsum("ctn,chpn->cthp", reads_low, states_low, preferred_element_type=f32)
    exp_cum = jnp.exp(cum_log).transpose(0, 2, 1)
    ssd_heads = (
        local_out + exp_cum[..., None] * carried_pre + skip_gain[None, None, :, None] * values_f
    )
    ssd_out = ssd_heads.reshape(tokens, local_inner)
    gate_act = jax.nn.silu(gate_out)
    gated = ssd_out * gate_act
    upstream = cotangent[0]
    grad_normal = matmul(upstream, out_t)
    scaled_grad = grad_normal * inner_gain
    sums = jnp.stack([jnp.sum(gated * gated, axis=1), jnp.sum(scaled_grad * gated, axis=1)])
    sums = sum_all(sums.reshape(2 * tokens // 128, 128), 4).reshape(2, tokens)
    square_sum, cross_sum = sums[0], sums[1]
    scale_one = lax.rsqrt(square_sum / INNER + EPS)[:, None]
    normal_out = (gated * scale_one * inner_gain).astype(bfloat)
    branch = back_matmul(normal_out, out_t).astype(bfloat)
    mixed_out = tp_sum(branch, stream[0], 5)[None]
    grad_w_out = matmul(upstream.T, normal_out)
    grad_inner_gain = jnp.sum(grad_normal * gated * scale_one, axis=0)
    grad_gated = (
        scale_one * scaled_grad
        - gated * (scale_one * scale_one * scale_one) * (cross_sum / INNER)[:, None]
    )
    grad_ssd = (grad_gated * gate_act).astype(bfloat)
    grad_gate = (grad_gated * ssd_out * silu_grad(gate_out)).astype(bfloat)
    grad_heads = grad_ssd.reshape(blocks, GROUP, local_heads, HEAD)
    grad_heads_f = grad_heads.astype(f32)
    grad_skip_gain = jnp.sum(grad_heads_f * values_f, axis=(0, 1, 3))
    grad_values = skip_gain[None, None, :, None] * grad_heads_f
    grad_weights = jnp.einsum("cthp,cshp->chts", grad_heads, values, preferred_element_type=f32)
    grad_values = grad_values + jnp.einsum(
        "chts,cthp->cshp", weights_low, grad_heads, preferred_element_type=f32
    )
    product = grad_weights * weights
    grad_cum = jnp.sum(product, axis=3) - jnp.sum(product, axis=2)
    grad_step = jnp.sum(grad_weights * inner_prod[:, None] * decays, axis=2)
    grad_inner = jnp.sum(grad_weights * decays * step_blocks[:, :, None, :], axis=1)
    grad_exp = grad_heads_f * exp_cum[..., None]
    grad_carried = grad_exp.astype(bfloat)
    grad_cum = grad_cum + jnp.sum(grad_exp * carried_pre, axis=3).transpose(0, 2, 1)
    grad_reads = jnp.einsum("cthp,chpn->ctn", grad_carried, states_low, preferred_element_type=f32)
    grad_state_read = jnp.einsum(
        "cthp,ctn->chpn", grad_carried, reads_low, preferred_element_type=f32
    )
    local_in = chain(zero_state, block_decay, grad_state_read, backward)[0]
    arriving = jnp.where(ctx == 0, swap_ctx(local_in, 6), 0.0)
    grad_state_out = chain(arriving, block_decay, grad_state_read, backward)[1]
    grad_last = jnp.sum(grad_state_out * states_in, axis=(2, 3)) * block_decay
    grad_fresh = grad_state_out.astype(bfloat)
    grad_weighted = jnp.einsum("csn,chpn->cshp", keys_low, grad_fresh, preferred_element_type=f32)
    grad_keys = jnp.einsum("cshp,chpn->csn", weighted, grad_fresh, preferred_element_type=f32)
    grad_values = grad_values + grad_weighted * scales_t[..., None]
    grad_scales = jnp.sum(grad_weighted * values_f, axis=3).transpose(0, 2, 1)
    grad_step = grad_step + grad_scales * jnp.exp(last_cum[:, :, None] - cum_log)
    spill_term = grad_scales * scales
    grad_last = grad_last + jnp.sum(spill_term, axis=2)
    last_flag = (jnp.arange(GROUP) == GROUP - 1).astype(f32)
    grad_cum = grad_cum - spill_term + grad_last[:, :, None] * last_flag
    keys_f = keys_low.astype(f32)
    reads_f = reads_low.astype(f32)
    grad_reads = grad_reads + jnp.einsum("cts,csn->ctn", grad_inner, keys_f, precision=HIGH)
    grad_keys = grad_keys + jnp.einsum("cts,ctn->csn", grad_inner, reads_f, precision=HIGH)
    grad_rate = jnp.einsum("ts,cht->chs", lower_ones, grad_cum, precision=HIGH)
    grad_step = grad_step - decay_rate[None, :, None] * grad_rate
    grad_decay_log = -decay_rate * jnp.sum(grad_rate * step_blocks, axis=(0, 2))
    grad_step_pre = grad_step.transpose(0, 2, 1).reshape(tokens, local_heads) * jax.nn.sigmoid(
        step_raw + step_bias
    )
    grad_step_bias = jnp.sum(grad_step_pre, axis=0)
    grad_step_low = grad_step_pre.astype(bfloat)
    state_grads = jnp.concatenate(
        [grad_keys.reshape(tokens, STATE), grad_reads.reshape(tokens, STATE)], axis=1
    )
    state_grads = sum_all(state_grads, 7)
    grad_act = jnp.concatenate([grad_values.reshape(tokens, local_inner), state_grads], axis=1)
    grad_conv = grad_act * silu_grad(conv_sum)
    grad_padded = sum(
        (
            jnp.pad(kernel[offset] * grad_conv, ((offset, CONV - 1 - offset), (0, 0)))
            for offset in range(CONV)
        )
    )
    incoming = swap_ctx(grad_padded[:8], 8)[: CONV - 1]
    incoming = jnp.where(ctx == 0, incoming, 0.0)
    grad_input = grad_padded[CONV - 1 :] + jnp.pad(incoming, ((tokens - (CONV - 1), 0), (0, 0)))
    grad_kernel = jnp.stack(
        [jnp.sum(grad_conv * padded[offset : offset + tokens], axis=0) for offset in range(CONV)]
    )
    grad_kernel_bias = jnp.sum(grad_conv, axis=0)
    grad_step_wide = jnp.pad(grad_step_low, ((0, 0), (0, 128 - local_heads)))
    grad_mix = grad_input.astype(bfloat)
    all_grads = jnp.concatenate([grad_mix, grad_gate, grad_step_wide], axis=1)
    grad_w = matmul(normed.T, all_grads)
    mine = (jnp.arange(tokens) // (tokens // 4) == tp)[:, None]
    state_mine = jnp.where(mine, grad_mix[:, local_inner:], 0)
    once = jnp.concatenate([grad_mix[:, :local_inner], state_mine, all_grads[:, mix:]], axis=1)
    grad_normed = tp_sum(back_matmul(once, projection).astype(bfloat), None, 9).astype(f32)
    grad_norm_gain = jnp.sum(grad_normed * source * scale_zero, axis=0)
    scaled_zero = grad_normed * gain_zero
    grad_source = scale_zero * scaled_zero - source * (scale_zero * scale_zero * scale_zero) * (
        jnp.sum(scaled_zero * source, axis=1, keepdims=True) / D
    )
    d_stream = (upstream.astype(f32) + grad_source)[None]
    packed = jnp.concatenate(
        [
            grad_w[:, : thin + local_heads],
            grad_norm_gain[:, None],
            grad_w[:, thin + local_heads + 1 :],
            grad_w_out,
        ],
        axis=1,
    ).astype(bfloat)
    heads_row = jnp.concatenate([grad_step_bias, grad_decay_log, grad_skip_gain])
    small = jnp.concatenate(
        [
            grad_kernel[:, :local_inner],
            grad_kernel_bias[None, :local_inner],
            grad_inner_gain[None],
            jnp.pad(grad_kernel[:, local_inner:], ((0, 0), (0, local_inner - 2 * STATE))),
            jnp.pad(grad_kernel_bias[None, local_inner:], ((0, 0), (0, local_inner - 2 * STATE))),
            jnp.pad(heads_row[None], ((0, 4), (0, local_inner - 3 * local_heads))),
        ],
        axis=0,
    )
    owned, totals = scatter_grads(packed, small)
    return (
        mixed_out,
        d_stream,
        owned[:, thin + local_heads],
        owned[:, mix:thin],
        owned[:, :local_inner],
        owned[:, thin : thin + local_heads],
        owned[:, local_inner:mix],
        owned[:, thin + 128 :].T,
        totals[:4, :local_inner],
        totals[4],
        totals[6:10, : 2 * STATE],
        totals[10, : 2 * STATE],
        totals[11, :local_heads],
        totals[11, local_heads : 2 * local_heads],
        totals[11, 2 * local_heads : 3 * local_heads],
        totals[5],
    )


def solution(mesh):
    in_specs = (
        P("dp", "ctx", None),
        P("dp"),
        P("dp", "tp"),
        P("dp", "tp"),
        P("dp", "tp"),
        P("dp", None),
        P("tp", "dp"),
        P(None, "tp"),
        P("tp"),
        P(),
        P(),
        P("tp"),
        P("tp"),
        P("tp"),
        P("tp"),
        P("dp", "ctx", None),
    )
    out_specs = (
        P("dp", "ctx", None),
        P("dp", "ctx", None),
        P("dp"),
        P("dp", "tp"),
        P("dp", "tp"),
        P("dp", "tp"),
        P("dp", None),
        P("tp", "dp"),
        P(None, "tp"),
        P("tp"),
        P(),
        P(),
        P("tp"),
        P("tp"),
        P("tp"),
        P("tp"),
    )
    return jax.shard_map(
        per_device, mesh=mesh, in_specs=in_specs, out_specs=out_specs, check_vma=False
    )
```

```python
import jax
import jax.numpy as jnp
from jax import lax
from jax.experimental import pallas as pl
from jax.experimental.pallas import tpu as pltpu
from jax.sharding import PartitionSpec as P

D = 768
HEAD = 64
STATE = 128
CONV = 4
GROUP = 256
INNER = 1536


EPS = 1e-05
HIGH = lax.Precision.HIGHEST


MESH = pl.DeviceIdType.MESH
VM = pl.BlockSpec(memory_space=pltpu.VMEM)
SIDE = 4
ROWS = 48
WIDE = 1536
DMA = pltpu.SemaphoreType.DMA
F32 = jnp.float32
BF16 = jnp.bfloat16


def params(ident, limit=40):
    return pltpu.CompilerParams(
        collective_id=ident, has_side_effects=True, vmem_limit_bytes=limit * 1024 * 1024
    )


def remote(source, target, send, recv, where):
    return pltpu.make_async_remote_copy(
        src_ref=source,
        dst_ref=target,
        send_sem=send,
        recv_sem=recv,
        device_id=where,
        device_id_type=MESH,
    )


def greet(peers):
    barrier = pltpu.get_barrier_semaphore()
    for where in peers:
        pl.semaphore_signal(barrier, inc=1, device_id=where, device_id_type=MESH)
    pl.semaphore_wait(barrier, len(peers))


def place():
    me = lax.axis_index("dp")
    z, y = lax.div(me, SIDE), lax.rem(me, SIDE)

    def along_y(hop):
        return {"dp": z * SIDE + lax.rem(y + hop, SIDE)}

    def along_z(hop):
        return {"dp": lax.rem(z + hop, SIDE) * SIDE + y}

    return z, y, along_y, along_z


def ahead(position, hop):
    return lax.rem(position + hop, SIDE)


class RingGather:
    def __init__(self, block, source, position, along, send, recv, first):
        self.block, self.position, self.along = block, position, along
        self.send, self.recv, self.first = send, recv, first
        self.direct = [
            self.copy(source(0), position, 0, 0, 1),
            self.copy(source(1), position, 1, 1, 3),
            self.copy(source(1), position, 1, 2, 1),
            self.copy(source(0), position, 0, 3, 3),
        ]
        for item in self.direct:
            item.start()

    def copy(self, source, position, sub, slot, hop):
        slot = self.first + slot
        return remote(
            source,
            self.block(position, sub),
            self.send.at[slot],
            self.recv.at[slot],
            self.along(hop),
        )

    def relay(self):
        left, right = ahead(self.position, 3), ahead(self.position, 1)
        self.direct[0].wait_recv()
        one = self.copy(self.block(left, 0), left, 0, 4, 1)
        one.start()
        self.direct[1].wait_recv()
        two = self.copy(self.block(right, 1), right, 1, 5, 3)
        two.start()
        self.relayed = [one, two]

    def finish(self):
        for item in self.direct[2:] + self.relayed:
            item.wait_recv()
        for item in self.direct + self.relayed:
            item.wait_send()


def gather_kernel(shard, edge, full, edge_in, send, recv, own):
    z, y, along_y, along_z = place()
    partner = {"ctx": 1 - lax.axis_index("ctx")}
    greet([along_y(1), along_y(3), along_z(1), along_z(3), partner])
    quarter = WIDE // 4

    def columns(sub):
        return pl.ds(sub * quarter, quarter)

    halo = remote(edge, edge_in, send.at[24], recv.at[24], partner)
    first_y = RingGather(
        lambda at, sub: full.at[z, at, :, columns(sub)],
        lambda sub: shard.at[:, columns(sub)],
        y, along_y, send, recv, 0,
    )
    first_z = RingGather(
        lambda at, sub: full.at[at, y, :, columns(2 + sub)],
        lambda sub: shard.at[:, columns(2 + sub)],
        z, along_z, send, recv, 6,
    )
    halo.start()
    keep = pltpu.make_async_copy(shard, full.at[z, y], own)
    keep.start()
    keep.wait()
    first_y.relay()
    first_z.relay()
    first_y.finish()
    second_z = RingGather(
        lambda at, sub: full.at[at, :, :, columns(sub)],
        lambda sub: full.at[z, :, :, columns(sub)],
        z, along_z, send, recv, 12,
    )
    first_z.finish()
    second_y = RingGather(
        lambda at, sub: full.at[:, at, :, columns(2 + sub)],
        lambda sub: full.at[:, y, :, columns(2 + sub)],
        y, along_y, send, recv, 18,
    )
    second_z.relay()
    second_y.relay()
    second_z.finish()
    second_y.finish()
    halo.wait()


def gather_weights(shard, edge):
    full, edge_in = pl.pallas_call(
        gather_kernel,
        out_shape=(
            jax.ShapeDtypeStruct((SIDE, SIDE, ROWS, WIDE), shard.dtype),
            jax.ShapeDtypeStruct(edge.shape, edge.dtype),
        ),
        in_specs=[VM, VM],
        out_specs=(VM, VM),
        scratch_shapes=[DMA((25,)), DMA((25,)), DMA],
        compiler_params=params(1),
    )(shard, edge)
    return full.reshape(SIDE * SIDE * ROWS, WIDE), edge_in


class RingScatter:
    def __init__(self, block, load, held, passed, position, along, send, recv, first):
        self.block, self.load, self.held, self.passed = block, load, held, passed
        self.position, self.along = position, along
        self.send, self.recv, self.first = send, recv, first
        far, right, left = ahead(position, 2), ahead(position, 1), ahead(position, 3)
        self.direct = [
            self.copy(block(far, 0), 0, 1),
            self.copy(block(far, 1), 1, 3),
            self.copy(block(right, 1), 2, 1),
            self.copy(block(left, 0), 3, 3),
        ]
        for item in self.direct:
            item.start()

    def copy(self, source, slot, hop):
        return remote(
            source,
            self.held.at[slot],
            self.send.at[self.first + slot],
            self.recv.at[self.first + slot],
            self.along(hop),
        )

    def relay(self):
        right, left = ahead(self.position, 1), ahead(self.position, 3)
        self.direct[0].wait_recv()
        self.passed[0] = (self.held[0].astype(F32) + self.load(right, 0).astype(F32)).astype(BF16)
        one = self.copy(self.passed.at[0], 4, 1)
        one.start()
        self.direct[1].wait_recv()
        self.passed[1] = (self.held[1].astype(F32) + self.load(left, 1).astype(F32)).astype(BF16)
        two = self.copy(self.passed.at[1], 5, 3)
        two.start()
        self.relayed = [one, two]

    def total(self, sub):
        own = self.load(self.position, sub).astype(F32)
        if sub == 0:
            self.direct[3].wait_recv()
            self.relayed[0].wait_recv()
            return own + self.held[3].astype(F32) + self.held[4].astype(F32)
        self.direct[2].wait_recv()
        self.relayed[1].wait_recv()
        return own + self.held[2].astype(F32) + self.held[5].astype(F32)

    def finish(self):
        for item in self.direct + self.relayed:
            item.wait_send()


class PairSum:
    def __init__(self, part, out, half_in, over_out, over_in, send, recv, first):
        self.part, self.out = part, out
        self.half_in, self.over_out, self.over_in = half_in, over_out, over_in
        self.send, self.recv, self.first = send, recv, first
        me = lax.axis_index("tp")
        core, chip = lax.rem(me, 2), lax.div(me, 2)
        self.twin, self.across = {"tp": me + 1 - 2 * core}, {"tp": me + 2 - 4 * chip}
        size = part.shape[0] // 4

        def quarter(c, h):
            return pl.ds(pl.multiple_of((2 * c + h) * size, size), size)

        self.keep, self.give = quarter(core, chip), quarter(core, 1 - chip)
        self.sends = [
            self.copy(part.at[quarter(1 - core, 1 - chip)], half_in.at[0], 0, self.twin),
            self.copy(part.at[quarter(1 - core, chip)], half_in.at[1], 1, self.twin),
        ]

    def copy(self, source, target, slot, where):
        item = remote(
            source, target, self.send.at[self.first + slot], self.recv.at[self.first + slot], where
        )
        item.start()
        return item

    def cross(self):
        self.sends[0].wait_recv()
        self.over_out[...] = (
            self.part[self.give].astype(F32) + self.half_in[0].astype(F32)
        ).astype(BF16)
        self.sends.append(self.copy(self.over_out, self.over_in, 2, self.across))

    def close(self, base=None):
        self.sends[1].wait_recv()
        self.sends[2].wait_recv()
        total = self.part[self.keep].astype(F32) + self.half_in[1].astype(F32)
        total = total + self.over_in[...].astype(F32)
        if base is not None:
            total = total + base[self.keep].astype(F32)
        self.out[self.keep] = total.astype(BF16)
        mine = self.out.at[self.keep]
        self.sends.append(self.copy(mine, mine, 3, self.across))
        self.sends.append(self.copy(mine, mine, 4, self.twin))

    def relay(self):
        self.sends[3].wait_recv()
        other = self.out.at[self.give]
        self.sends.append(self.copy(other, other, 5, self.twin))

    def finish(self):
        self.sends[4].wait_recv()
        self.sends[5].wait_recv()
        for item in self.sends:
            item.wait_send()


def pair_scratch(rows, columns):
    return [
        pltpu.VMEM((2, rows // 4, columns), BF16),
        pltpu.VMEM((rows // 4, columns), BF16),
        pltpu.VMEM((rows // 4, columns), BF16),
    ]


def all_peers(along_y, along_z):
    me, partner = lax.axis_index("tp"), {"ctx": 1 - lax.axis_index("ctx")}
    hops = range(1, SIDE)
    tp_peers = [{"tp": ahead(me, hop)} for hop in hops]
    return [along_y(hop) for hop in hops], [along_z(hop) for hop in hops], partner, tp_peers


def spread(source, held, own, peers, send, recv, first):
    copies = [
        remote(source, held.at[own], send.at[first + hop], recv.at[first + hop], peer)
        for hop, peer in enumerate(peers)
    ]
    for item in copies:
        item.start()
    return copies


def fold(held, own, value, copies):
    held[own] = value
    for item in copies:
        item.wait_recv()
    return (held[0] + held[1]) + (held[2] + held[3])


def final_kernel(
    grads, small, part, branch, base, out, small_out, normed_out, mixed_out,
    held_z, held_y, held_2z, held_2y, pass_z, pass_y, pass_2z, pass_2y, mid_z, mid_y,
    own_bf, pair_in, small_y, small_z, small_c, small_t, small_now,
    half_0, over_out_0, over_in_0, half_1, over_out_1, over_in_1,
    send, recv, small_send, small_recv, tp_send, tp_recv
):
    z, y, along_y, along_z = place()
    tp = lax.axis_index("tp")
    y_peers, z_peers, partner, tp_peers = all_peers(along_y, along_z)
    greet(y_peers + z_peers + [partner] + tp_peers)
    quarter, half = WIDE // 4, WIDE // 2

    def columns(sub):
        return pl.ds(sub * quarter, quarter)

    normed = PairSum(part, normed_out, half_0, over_out_0, over_in_0, tp_send, tp_recv, 0)
    first_z = RingScatter(
        lambda at, sub: grads.at[at, :, :, columns(sub)],
        lambda at, sub: grads[at, :, :, columns(sub)],
        held_z, pass_z, z, along_z, send, recv, 0,
    )
    first_y = RingScatter(
        lambda at, sub: grads.at[:, at, :, columns(2 + sub)],
        lambda at, sub: grads[:, at, :, columns(2 + sub)],
        held_y, pass_y, y, along_y, send, recv, 6,
    )
    mixed = PairSum(branch, mixed_out, half_1, over_out_1, over_in_1, tp_send, tp_recv, 6)
    to_y = spread(small, small_y, y, y_peers, small_send, small_recv, 0)
    normed.cross()
    first_z.relay()
    first_y.relay()
    small_now[0] = fold(small_y, y, small[...], to_y)
    to_z = spread(small_now.at[0], small_z, z, z_peers, small_send, small_recv, 3)
    mixed.cross()
    normed.close()
    for sub in range(2):
        mid_z[:, :, sub * quarter : (sub + 1) * quarter] = first_z.total(sub).astype(BF16)
    second_y = RingScatter(
        lambda at, sub: mid_z.at[at, :, columns(sub)],
        lambda at, sub: mid_z[at, :, columns(sub)],
        held_2y, pass_2y, y, along_y, send, recv, 12,
    )
    for sub in range(2):
        mid_y[:, :, sub * quarter : (sub + 1) * quarter] = first_y.total(sub).astype(BF16)
    second_z = RingScatter(
        lambda at, sub: mid_y.at[at, :, columns(sub)],
        lambda at, sub: mid_y[at, :, columns(sub)],
        held_2z, pass_2z, z, along_z, send, recv, 18,
    )
    small_now[1] = fold(small_z, z, small_now[0], to_z)
    to_ctx = remote(small_now.at[1], small_c, small_send.at[6], small_recv.at[6], partner)
    to_ctx.start()
    second_y.relay()
    second_z.relay()
    mixed.close(base)
    for sub in range(2):
        own_bf[:, sub * quarter : (sub + 1) * quarter] = second_y.total(sub).astype(BF16)
    for sub in range(2):
        own_bf[:, half + sub * quarter : half + (sub + 1) * quarter] = second_z.total(sub).astype(
            BF16
        )
    pair = remote(own_bf, pair_in, send.at[24], recv.at[24], partner)
    pair.start()
    to_ctx.wait_recv()
    small_now[2] = small_now[1] + small_c[...]
    shared = pl.ds(16, 8)
    to_tp = spread(small_now.at[2, shared], small_t, tp, tp_peers, small_send, small_recv, 7)
    normed.relay()
    pair.wait_recv()
    out[...] = own_bf[...].astype(F32) + pair_in[...].astype(F32)
    small_out[0:16] = small_now[2, 0:16]
    small_out[16:24] = fold(small_t, tp, small_now[2, 16:24], to_tp)
    mixed.relay()
    normed.finish()
    mixed.finish()
    for item in (first_z, first_y, second_y, second_z):
        item.finish()
    for item in to_y + to_z + to_tp + [to_ctx, pair]:
        item.wait_send()


def final_sums(grads, small, part, branch, base):
    rows, columns = part.shape
    quarter = WIDE // 4
    return pl.pallas_call(
        final_kernel,
        out_shape=(
            jax.ShapeDtypeStruct((ROWS, WIDE), F32),
            jax.ShapeDtypeStruct(small.shape, F32),
            jax.ShapeDtypeStruct(part.shape, BF16),
            jax.ShapeDtypeStruct(part.shape, BF16),
        ),
        in_specs=[VM] * 5,
        out_specs=(VM,) * 4,
        scratch_shapes=[
            pltpu.VMEM((6, SIDE, ROWS, quarter), BF16),
            pltpu.VMEM((6, SIDE, ROWS, quarter), BF16),
            pltpu.VMEM((6, ROWS, quarter), BF16),
            pltpu.VMEM((6, ROWS, quarter), BF16),
            pltpu.VMEM((2, SIDE, ROWS, quarter), BF16),
            pltpu.VMEM((2, SIDE, ROWS, quarter), BF16),
            pltpu.VMEM((2, ROWS, quarter), BF16),
            pltpu.VMEM((2, ROWS, quarter), BF16),
            pltpu.VMEM((SIDE, ROWS, 2 * quarter), BF16),
            pltpu.VMEM((SIDE, ROWS, 2 * quarter), BF16),
            pltpu.VMEM((ROWS, WIDE), BF16),
            pltpu.VMEM((ROWS, WIDE), BF16),
            pltpu.VMEM((SIDE, *small.shape), F32),
            pltpu.VMEM((SIDE, *small.shape), F32),
            pltpu.VMEM(small.shape, F32),
            pltpu.VMEM((SIDE, 8, small.shape[1]), F32),
            pltpu.VMEM((3, *small.shape), F32),
            *pair_scratch(rows, columns),
            *pair_scratch(rows, columns),
            DMA((25,)),
            DMA((25,)),
            DMA((10,)),
            DMA((10,)),
            DMA((12,)),
            DMA((12,)),
        ],
        compiler_params=params(2),
    )(grads.reshape(SIDE, SIDE, ROWS, WIDE), small, part, branch, base)


def swap_ctx(value, ctx_to):
    return lax.ppermute(value, "ctx", [(1 - ctx_to, ctx_to)])


def sum_all_kernel(part, out, held, send, recv):
    me = lax.axis_index("tp")
    peers = [{"tp": ahead(me, hop)} for hop in range(1, SIDE)]
    greet(peers)
    copies = spread(part, held, me, peers, send, recv, 0)
    out[...] = fold(held, me, part[...], copies)
    for item in copies:
        item.wait_send()


def sum_all(part, ident):
    return pl.pallas_call(
        sum_all_kernel,
        out_shape=jax.ShapeDtypeStruct(part.shape, part.dtype),
        in_specs=[VM],
        out_specs=VM,
        scratch_shapes=[pltpu.VMEM((4, *part.shape), part.dtype), DMA((3,)), DMA((3,))],
        compiler_params=params(ident),
    )(part)


def state_sum_kernel(part, values, slopes, out, values_in, slopes_in, state_in, half, over_out, over_in,
                     send, recv):
    partner = {"ctx": 1 - lax.axis_index("ctx")}
    me = lax.axis_index("tp")
    core, chip = lax.rem(me, 2), lax.div(me, 2)
    greet([{"tp": me + 1 - 2 * core}, {"tp": me + 2 - 4 * chip}, partner])
    total = PairSum(part, out, half, over_out, over_in, send, recv, 0)
    early = [
        remote(values, values_in, send.at[6], recv.at[6], partner),
        remote(slopes, slopes_in, send.at[7], recv.at[7], partner),
    ]
    for item in early:
        item.start()
    total.cross()
    total.close()
    total.relay()
    total.finish()
    late = remote(out.at[0:16], state_in, send.at[8], recv.at[8], partner)
    late.start()
    for item in early + [late]:
        item.wait()


def state_sum(part, values, slopes):
    rows, columns = part.shape
    return pl.pallas_call(
        state_sum_kernel,
        out_shape=(
            jax.ShapeDtypeStruct(part.shape, BF16),
            jax.ShapeDtypeStruct(values.shape, values.dtype),
            jax.ShapeDtypeStruct(slopes.shape, slopes.dtype),
            jax.ShapeDtypeStruct((16, columns), BF16),
        ),
        in_specs=[VM] * 3,
        out_specs=(VM,) * 4,
        scratch_shapes=[*pair_scratch(rows, columns), DMA((9,)), DMA((9,))],
        compiler_params=params(7),
    )(part, values, slopes)


def matmul(left, right):
    return jnp.dot(left, right, preferred_element_type=jnp.float32)


def back_matmul(grad_rows, weight):
    return lax.dot_general(
        grad_rows, weight, (((1,), (1,)), ((), ())), preferred_element_type=jnp.float32
    )


def silu_grad(pre_act):
    sigmoid_val = jax.nn.sigmoid(pre_act)
    return sigmoid_val * (1.0 + pre_act * (1.0 - sigmoid_val))


def chain(entering, decay, fresh, order):
    carry, inputs = entering, {}
    for block in order:
        inputs[block] = carry
        carry = decay[block][:, None, None] * carry + fresh[block]
    return carry, jnp.stack([inputs[block] for block in sorted(inputs)])


def per_device(
    stream,
    norm_gain,
    w_gate,
    w_value,
    w_step,
    w_state,
    w_out,
    conv_value,
    conv_value_bias,
    conv_state,
    conv_state_bias,
    step_bias,
    decay_log,
    skip_gain,
    inner_gain,
    cotangent,
):
    tokens = stream.shape[1]
    local_heads = step_bias.shape[0]
    local_inner = inner_gain.shape[0]
    blocks = tokens // GROUP
    bfloat = jnp.bfloat16
    f32 = jnp.float32
    ctx = lax.axis_index("ctx")
    tp = lax.axis_index("tp")
    mix = local_inner + 2 * STATE
    thin = mix + local_inner
    shard = jnp.concatenate(
        [
            w_value,
            w_state,
            w_gate,
            w_step,
            norm_gain[:, None],
            jnp.zeros((ROWS, 128 - local_heads - 1), bfloat),
            w_out.T,
        ],
        axis=1,
    )
    full, edge = gather_weights(shard, stream[0, tokens - 16 :])
    projection = full[:, : thin + 128]
    out_t = full[:, thin + 128 :]
    gain_zero = full[:, thin + local_heads].astype(f32)[None]
    source = stream[0].astype(f32)

    def normalise(rows):
        scale = lax.rsqrt(jnp.mean(rows * rows, axis=-1, keepdims=True) + EPS)
        return scale, (rows * scale * gain_zero).astype(bfloat)

    scale_zero, normed = normalise(source)
    projected = matmul(normed, projection)
    conv_input = projected[:, :mix].astype(bfloat)
    gate_out = projected[:, mix:thin]
    step_raw = projected[:, thin : thin + local_heads]
    edge_normed = normalise(edge.astype(f32))[1]
    edge_rows = matmul(edge_normed, full[:, :mix])[13:]
    edge_rows = jnp.where(ctx == 0, 0.0, edge_rows).astype(bfloat)
    padded = jnp.concatenate([edge_rows, conv_input], axis=0).astype(f32)
    kernel = jnp.concatenate([conv_value, conv_state], axis=1)
    kernel_bias = jnp.concatenate([conv_value_bias, conv_state_bias])
    conv_sum = kernel_bias + sum(
        (kernel[offset] * padded[offset : offset + tokens] for offset in range(CONV))
    )
    activated = jax.nn.silu(conv_sum)
    values = activated[:, :local_inner].astype(bfloat).reshape(blocks, GROUP, local_heads, HEAD)
    keys_low = (
        activated[:, local_inner : local_inner + STATE].astype(bfloat).reshape(blocks, GROUP, STATE)
    )
    reads_low = activated[:, local_inner + STATE :].astype(bfloat).reshape(blocks, GROUP, STATE)
    step_val = jax.nn.softplus(step_raw + step_bias)
    decay_rate = jnp.exp(decay_log)
    log_rate = -decay_rate * step_val
    step_blocks = step_val.reshape(blocks, GROUP, local_heads).transpose(0, 2, 1)
    lower_mask = jnp.arange(GROUP)[:, None] >= jnp.arange(GROUP)[None, :]
    lower_ones = lower_mask.astype(f32)
    cum_log = jnp.einsum(
        "ts,csh->cht", lower_ones, log_rate.reshape(blocks, GROUP, local_heads), precision=HIGH
    )
    last_cum = cum_log[:, :, -1]
    decays = jnp.exp(jnp.where(lower_mask, cum_log[:, :, :, None] - cum_log[:, :, None, :], -1e30))
    inner_prod = jnp.einsum("ctn,csn->cts", reads_low, keys_low, preferred_element_type=f32)
    weights = inner_prod[:, None] * decays * step_blocks[:, :, None, :]
    weights_low = weights.astype(bfloat)
    local_out = jnp.einsum("chts,cshp->cthp", weights_low, values, preferred_element_type=f32)
    scales = step_blocks * jnp.exp(last_cum[:, :, None] - cum_log)
    scales_t = scales.transpose(0, 2, 1)
    values_f = values.astype(f32)
    weighted = (values_f * scales_t[..., None]).astype(bfloat)
    fresh_state = jnp.einsum("cshp,csn->chpn", weighted, keys_low, preferred_element_type=f32)
    block_decay = jnp.exp(last_cum)
    zero_state = jnp.zeros((local_heads, HEAD, STATE), f32)
    forward, backward = range(blocks), range(blocks - 1, -1, -1)
    device_state = chain(zero_state, block_decay, fresh_state, forward)[0]
    entering = jnp.where(ctx == 1, swap_ctx(device_state, 1), 0.0)
    states_in = chain(entering, block_decay, fresh_state, forward)[1]
    states_low = states_in.astype(bfloat)
    carried_pre = jnp.einsum("ctn,chpn->cthp", reads_low, states_low, preferred_element_type=f32)
    exp_cum = jnp.exp(cum_log).transpose(0, 2, 1)
    ssd_heads = (
        local_out + exp_cum[..., None] * carried_pre + skip_gain[None, None, :, None] * values_f
    )
    ssd_out = ssd_heads.reshape(tokens, local_inner)
    gate_act = jax.nn.silu(gate_out)
    gated = ssd_out * gate_act
    upstream = cotangent[0]
    grad_normal = matmul(upstream, out_t)
    scaled_grad = grad_normal * inner_gain
    sums = jnp.stack([jnp.sum(gated * gated, axis=1), jnp.sum(scaled_grad * gated, axis=1)])
    sums = sum_all(sums.reshape(2 * tokens // 128, 128), 4).reshape(2, tokens)
    square_sum, cross_sum = sums[0], sums[1]
    scale_one = lax.rsqrt(square_sum / INNER + EPS)[:, None]
    normal_out = (gated * scale_one * inner_gain).astype(bfloat)
    branch = back_matmul(normal_out, out_t).astype(bfloat)
    grad_w_out = matmul(upstream.T, normal_out)
    grad_inner_gain = jnp.sum(grad_normal * gated * scale_one, axis=0)
    grad_gated = (
        scale_one * scaled_grad
        - gated * (scale_one * scale_one * scale_one) * (cross_sum / INNER)[:, None]
    )
    grad_ssd = (grad_gated * gate_act).astype(bfloat)
    grad_gate = (grad_gated * ssd_out * silu_grad(gate_out)).astype(bfloat)
    grad_heads = grad_ssd.reshape(blocks, GROUP, local_heads, HEAD)
    grad_heads_f = grad_heads.astype(f32)
    grad_skip_gain = jnp.sum(grad_heads_f * values_f, axis=(0, 1, 3))
    grad_values = skip_gain[None, None, :, None] * grad_heads_f
    grad_weights = jnp.einsum("cthp,cshp->chts", grad_heads, values, preferred_element_type=f32)
    grad_values = grad_values + jnp.einsum(
        "chts,cthp->cshp", weights_low, grad_heads, preferred_element_type=f32
    )
    product = grad_weights * weights
    grad_cum = jnp.sum(product, axis=3) - jnp.sum(product, axis=2)
    grad_step = jnp.sum(grad_weights * inner_prod[:, None] * decays, axis=2)
    grad_inner = jnp.sum(grad_weights * decays * step_blocks[:, :, None, :], axis=1)
    grad_exp = grad_heads_f * exp_cum[..., None]
    grad_carried = grad_exp.astype(bfloat)
    grad_cum = grad_cum + jnp.sum(grad_exp * carried_pre, axis=3).transpose(0, 2, 1)
    grad_reads = jnp.einsum("cthp,chpn->ctn", grad_carried, states_low, preferred_element_type=f32)
    grad_state_read = jnp.einsum(
        "cthp,ctn->chpn", grad_carried, reads_low, preferred_element_type=f32
    )
    local_in = chain(zero_state, block_decay, grad_state_read, backward)[0]
    arriving = jnp.where(ctx == 0, swap_ctx(local_in, 0), 0.0)
    grad_state_out = chain(arriving, block_decay, grad_state_read, backward)[1]
    grad_last = jnp.sum(grad_state_out * states_in, axis=(2, 3)) * block_decay
    grad_fresh = grad_state_out.astype(bfloat)
    grad_weighted = jnp.einsum("csn,chpn->cshp", keys_low, grad_fresh, preferred_element_type=f32)
    grad_keys = jnp.einsum("cshp,chpn->csn", weighted, grad_fresh, preferred_element_type=f32)
    grad_values = grad_values + grad_weighted * scales_t[..., None]
    grad_scales = jnp.sum(grad_weighted * values_f, axis=3).transpose(0, 2, 1)
    grad_step = grad_step + grad_scales * jnp.exp(last_cum[:, :, None] - cum_log)
    spill_term = grad_scales * scales
    grad_last = grad_last + jnp.sum(spill_term, axis=2)
    last_flag = (jnp.arange(GROUP) == GROUP - 1).astype(f32)
    grad_cum = grad_cum - spill_term + grad_last[:, :, None] * last_flag
    keys_f = keys_low.astype(f32)
    reads_f = reads_low.astype(f32)
    grad_reads = grad_reads + jnp.einsum("cts,csn->ctn", grad_inner, keys_f, precision=HIGH)
    grad_keys = grad_keys + jnp.einsum("cts,ctn->csn", grad_inner, reads_f, precision=HIGH)
    grad_rate = jnp.einsum("ts,cht->chs", lower_ones, grad_cum, precision=HIGH)
    grad_step = grad_step - decay_rate[None, :, None] * grad_rate
    grad_decay_log = -decay_rate * jnp.sum(grad_rate * step_blocks, axis=(0, 2))
    grad_step_pre = grad_step.transpose(0, 2, 1).reshape(tokens, local_heads) * jax.nn.sigmoid(
        step_raw + step_bias
    )
    grad_step_bias = jnp.sum(grad_step_pre, axis=0)
    grad_step_low = grad_step_pre.astype(bfloat)
    state_grads = jnp.concatenate(
        [grad_keys.reshape(tokens, STATE), grad_reads.reshape(tokens, STATE)], axis=1
    )
    slopes = silu_grad(conv_sum)
    grad_values = grad_values.reshape(tokens, local_inner)
    state_total, values_next, slopes_next, state_next = state_sum(
        state_grads.astype(bfloat), grad_values[:16], slopes[:16]
    )
    grad_act = jnp.concatenate([grad_values, state_total.astype(f32)], axis=1)
    grad_conv = grad_act * slopes
    conv_next = jnp.concatenate([values_next, state_next.astype(f32)], axis=1) * slopes_next
    conv_next = jnp.where(ctx == 0, conv_next, 0.0)[: CONV - 1]
    grad_ahead = jnp.concatenate([grad_conv, conv_next], axis=0)
    grad_input = sum(
        kernel[offset] * grad_ahead[CONV - 1 - offset : CONV - 1 - offset + tokens]
        for offset in range(CONV)
    )
    grad_kernel = jnp.stack(
        [jnp.sum(grad_conv * padded[offset : offset + tokens], axis=0) for offset in range(CONV)]
    )
    grad_kernel_bias = jnp.sum(grad_conv, axis=0)
    grad_step_wide = jnp.pad(grad_step_low, ((0, 0), (0, 128 - local_heads)))
    grad_mix = grad_input.astype(bfloat)
    all_grads = jnp.concatenate([grad_mix, grad_gate, grad_step_wide], axis=1)
    grad_w = matmul(normed.T, all_grads)
    mine = (jnp.arange(tokens) // (tokens // 4) == tp)[:, None]
    state_mine = jnp.where(mine, grad_mix[:, local_inner:], 0)
    once = jnp.concatenate([grad_mix[:, :local_inner], state_mine, all_grads[:, mix:]], axis=1)
    part = back_matmul(once, projection)
    gain_part = jnp.sum(part * source * scale_zero, axis=0)
    packed = jnp.concatenate([grad_w, grad_w_out], axis=1).astype(bfloat)
    heads_row = jnp.concatenate([grad_step_bias, grad_decay_log, grad_skip_gain])
    small = jnp.concatenate(
        [
            grad_kernel[:, :local_inner],
            grad_kernel_bias[None, :local_inner],
            grad_inner_gain[None],
            jnp.pad(grad_kernel[:, local_inner:], ((0, 0), (0, local_inner - 2 * STATE))),
            jnp.pad(grad_kernel_bias[None, local_inner:], ((0, 0), (0, local_inner - 2 * STATE))),
            jnp.pad(heads_row[None], ((0, 4), (0, local_inner - 3 * local_heads))),
            jnp.pad(gain_part.reshape(2, local_inner), ((0, 6), (0, 0))),
        ],
        axis=0,
    )
    owned, totals, grad_normed, mixed_out = final_sums(
        packed, small, part.astype(bfloat), branch, stream[0]
    )
    grad_normed = grad_normed.astype(f32)
    scaled_zero = grad_normed * gain_zero
    grad_source = scale_zero * scaled_zero - source * (scale_zero * scale_zero * scale_zero) * (
        jnp.sum(scaled_zero * source, axis=1, keepdims=True) / D
    )
    d_stream = (upstream.astype(f32) + grad_source)[None]
    gain_total = totals[16:18].reshape(D)
    return (
        mixed_out[None],
        d_stream,
        lax.dynamic_slice_in_dim(gain_total, lax.axis_index("dp") * ROWS, ROWS),
        owned[:, mix:thin],
        owned[:, :local_inner],
        owned[:, thin : thin + local_heads],
        owned[:, local_inner:mix],
        owned[:, thin + 128 :].T,
        totals[:4, :local_inner],
        totals[4],
        totals[6:10, : 2 * STATE],
        totals[10, : 2 * STATE],
        totals[11, :local_heads],
        totals[11, local_heads : 2 * local_heads],
        totals[11, 2 * local_heads : 3 * local_heads],
        totals[5],
    )


def solution(mesh):
    in_specs = (
        P("dp", "ctx", None),
        P("dp"),
        P("dp", "tp"),
        P("dp", "tp"),
        P("dp", "tp"),
        P("dp", None),
        P("tp", "dp"),
        P(None, "tp"),
        P("tp"),
        P(),
        P(),
        P("tp"),
        P("tp"),
        P("tp"),
        P("tp"),
        P("dp", "ctx", None),
    )
    out_specs = (
        P("dp", "ctx", None),
        P("dp", "ctx", None),
        P("dp"),
        P("dp", "tp"),
        P("dp", "tp"),
        P("dp", "tp"),
        P("dp", None),
        P("tp", "dp"),
        P(None, "tp"),
        P("tp"),
        P(),
        P(),
        P("tp"),
        P("tp"),
        P("tp"),
        P("tp"),
    )
    return jax.shard_map(
        per_device, mesh=mesh, in_specs=in_specs, out_specs=out_specs, check_vma=False
    )
```

```python
import jax
import jax.numpy as jnp
from jax import lax
from jax.experimental import pallas as pl
from jax.experimental.pallas import tpu as pltpu
from jax.sharding import PartitionSpec as P

D = 768
HEAD = 64
STATE = 128
CONV = 4
GROUP = 256
INNER = 1536


EPS = 1e-05
HIGH = lax.Precision.HIGHEST


MESH = pl.DeviceIdType.MESH
VM = pl.BlockSpec(memory_space=pltpu.VMEM)
SIDE = 4
ROWS = 48
WIDE = 1536
DMA = pltpu.SemaphoreType.DMA
F32 = jnp.float32
BF16 = jnp.bfloat16


def params(ident, limit=40):
    return pltpu.CompilerParams(
        collective_id=ident, has_side_effects=True, vmem_limit_bytes=limit * 1024 * 1024
    )


def remote(source, target, send, recv, where):
    return pltpu.make_async_remote_copy(
        src_ref=source,
        dst_ref=target,
        send_sem=send,
        recv_sem=recv,
        device_id=where,
        device_id_type=MESH,
    )


def greet(peers):
    barrier = pltpu.get_barrier_semaphore()
    for where in peers:
        pl.semaphore_signal(barrier, inc=1, device_id=where, device_id_type=MESH)
    pl.semaphore_wait(barrier, len(peers))


def place():
    me = lax.axis_index("dp")
    z, y = lax.div(me, SIDE), lax.rem(me, SIDE)

    def along_y(hop):
        return {"dp": z * SIDE + lax.rem(y + hop, SIDE)}

    def along_z(hop):
        return {"dp": lax.rem(z + hop, SIDE) * SIDE + y}

    return z, y, along_y, along_z


def ahead(position, hop):
    return lax.rem(position + hop, SIDE)


class RingGather:
    def __init__(self, block, source, position, along, send, recv, first):
        self.block, self.position, self.along = block, position, along
        self.send, self.recv, self.first = send, recv, first
        self.direct = [
            self.copy(source(0), position, 0, 0, 1),
            self.copy(source(1), position, 1, 1, 3),
            self.copy(source(1), position, 1, 2, 1),
            self.copy(source(0), position, 0, 3, 3),
        ]
        for item in self.direct:
            item.start()

    def copy(self, source, position, sub, slot, hop):
        slot = self.first + slot
        return remote(
            source,
            self.block(position, sub),
            self.send.at[slot],
            self.recv.at[slot],
            self.along(hop),
        )

    def relay(self):
        left, right = ahead(self.position, 3), ahead(self.position, 1)
        self.direct[0].wait_recv()
        one = self.copy(self.block(left, 0), left, 0, 4, 1)
        one.start()
        self.direct[1].wait_recv()
        two = self.copy(self.block(right, 1), right, 1, 5, 3)
        two.start()
        self.relayed = [one, two]

    def finish(self):
        for item in self.direct[2:] + self.relayed:
            item.wait_recv()
        for item in self.direct + self.relayed:
            item.wait_send()


def gather_kernel(shard, edge, full, edge_in, send, recv, own):
    z, y, along_y, along_z = place()
    partner = {"ctx": 1 - lax.axis_index("ctx")}
    greet([along_y(1), along_y(3), along_z(1), along_z(3), partner])
    quarter = WIDE // 4

    def columns(sub):
        return pl.ds(sub * quarter, quarter)

    halo = remote(edge, edge_in, send.at[24], recv.at[24], partner)
    first_y = RingGather(
        lambda at, sub: full.at[z, at, :, columns(sub)],
        lambda sub: shard.at[:, columns(sub)],
        y, along_y, send, recv, 0,
    )
    first_z = RingGather(
        lambda at, sub: full.at[at, y, :, columns(2 + sub)],
        lambda sub: shard.at[:, columns(2 + sub)],
        z, along_z, send, recv, 6,
    )
    halo.start()
    keep = pltpu.make_async_copy(shard, full.at[z, y], own)
    keep.start()
    keep.wait()
    first_y.relay()
    first_z.relay()
    first_y.finish()
    second_z = RingGather(
        lambda at, sub: full.at[at, :, :, columns(sub)],
        lambda sub: full.at[z, :, :, columns(sub)],
        z, along_z, send, recv, 12,
    )
    first_z.finish()
    second_y = RingGather(
        lambda at, sub: full.at[:, at, :, columns(2 + sub)],
        lambda sub: full.at[:, y, :, columns(2 + sub)],
        y, along_y, send, recv, 18,
    )
    second_z.relay()
    second_y.relay()
    second_z.finish()
    second_y.finish()
    halo.wait()


def gather_weights(shard, edge):
    full, edge_in = pl.pallas_call(
        gather_kernel,
        out_shape=(
            jax.ShapeDtypeStruct((SIDE, SIDE, ROWS, WIDE), shard.dtype),
            jax.ShapeDtypeStruct(edge.shape, edge.dtype),
        ),
        in_specs=[VM, VM],
        out_specs=(VM, VM),
        scratch_shapes=[DMA((25,)), DMA((25,)), DMA],
        compiler_params=params(1),
    )(shard, edge)
    return full.reshape(SIDE * SIDE * ROWS, WIDE), edge_in


class RingScatter:
    def __init__(self, block, load, held, passed, position, along, send, recv, first):
        self.block, self.load, self.held, self.passed = block, load, held, passed
        self.position, self.along = position, along
        self.send, self.recv, self.first = send, recv, first
        far, right, left = ahead(position, 2), ahead(position, 1), ahead(position, 3)
        self.direct = [
            self.copy(block(far, 0), 0, 1),
            self.copy(block(far, 1), 1, 3),
            self.copy(block(right, 1), 2, 1),
            self.copy(block(left, 0), 3, 3),
        ]
        for item in self.direct:
            item.start()

    def copy(self, source, slot, hop):
        return remote(
            source,
            self.held.at[slot],
            self.send.at[self.first + slot],
            self.recv.at[self.first + slot],
            self.along(hop),
        )

    def relay(self):
        right, left = ahead(self.position, 1), ahead(self.position, 3)
        self.direct[0].wait_recv()
        self.passed[0] = (self.held[0].astype(F32) + self.load(right, 0).astype(F32)).astype(BF16)
        one = self.copy(self.passed.at[0], 4, 1)
        one.start()
        self.direct[1].wait_recv()
        self.passed[1] = (self.held[1].astype(F32) + self.load(left, 1).astype(F32)).astype(BF16)
        two = self.copy(self.passed.at[1], 5, 3)
        two.start()
        self.relayed = [one, two]

    def total(self, sub):
        own = self.load(self.position, sub).astype(F32)
        if sub == 0:
            self.direct[3].wait_recv()
            self.relayed[0].wait_recv()
            return own + self.held[3].astype(F32) + self.held[4].astype(F32)
        self.direct[2].wait_recv()
        self.relayed[1].wait_recv()
        return own + self.held[2].astype(F32) + self.held[5].astype(F32)

    def finish(self):
        for item in self.direct + self.relayed:
            item.wait_send()


class PairSum:
    def __init__(self, part, out, half_in, over_out, over_in, send, recv, first):
        self.part, self.out = part, out
        self.half_in, self.over_out, self.over_in = half_in, over_out, over_in
        self.send, self.recv, self.first = send, recv, first
        me = lax.axis_index("tp")
        core, chip = lax.rem(me, 2), lax.div(me, 2)
        self.twin, self.across = {"tp": me + 1 - 2 * core}, {"tp": me + 2 - 4 * chip}
        size = part.shape[0] // 4

        def quarter(c, h):
            return pl.ds(pl.multiple_of((2 * c + h) * size, size), size)

        self.keep, self.give = quarter(core, chip), quarter(core, 1 - chip)
        self.sends = [
            self.copy(part.at[quarter(1 - core, 1 - chip)], half_in.at[0], 0, self.twin),
            self.copy(part.at[quarter(1 - core, chip)], half_in.at[1], 1, self.twin),
        ]

    def copy(self, source, target, slot, where):
        item = remote(
            source, target, self.send.at[self.first + slot], self.recv.at[self.first + slot], where
        )
        item.start()
        return item

    def cross(self):
        self.sends[0].wait_recv()
        self.over_out[...] = (
            self.part[self.give].astype(F32) + self.half_in[0].astype(F32)
        ).astype(BF16)
        self.sends.append(self.copy(self.over_out, self.over_in, 2, self.across))

    def close(self, base=None):
        self.sends[1].wait_recv()
        self.sends[2].wait_recv()
        total = self.part[self.keep].astype(F32) + self.half_in[1].astype(F32)
        total = total + self.over_in[...].astype(F32)
        if base is not None:
            total = total + base[self.keep].astype(F32)
        self.out[self.keep] = total.astype(BF16)
        mine = self.out.at[self.keep]
        self.sends.append(self.copy(mine, mine, 3, self.across))
        self.sends.append(self.copy(mine, mine, 4, self.twin))

    def relay(self):
        self.sends[3].wait_recv()
        other = self.out.at[self.give]
        self.sends.append(self.copy(other, other, 5, self.twin))

    def finish(self):
        self.sends[4].wait_recv()
        self.sends[5].wait_recv()
        for item in self.sends:
            item.wait_send()


def pair_scratch(rows, columns):
    return [
        pltpu.VMEM((2, rows // 4, columns), BF16),
        pltpu.VMEM((rows // 4, columns), BF16),
        pltpu.VMEM((rows // 4, columns), BF16),
    ]


def all_peers(along_y, along_z):
    me, partner = lax.axis_index("tp"), {"ctx": 1 - lax.axis_index("ctx")}
    hops = range(1, SIDE)
    tp_peers = [{"tp": ahead(me, hop)} for hop in hops]
    return [along_y(hop) for hop in hops], [along_z(hop) for hop in hops], partner, tp_peers


def spread(source, held, own, peers, send, recv, first):
    copies = [
        remote(source, held.at[own], send.at[first + hop], recv.at[first + hop], peer)
        for hop, peer in enumerate(peers)
    ]
    for item in copies:
        item.start()
    return copies


def fold(held, own, value, copies):
    held[own] = value
    for item in copies:
        item.wait_recv()
    return (held[0] + held[1]) + (held[2] + held[3])


def final_kernel(
    grads, last_grads, small, part, branch, base, out, small_out, normed_out, mixed_out,
    held_z, held_y, held_2z, held_2y, pass_z, pass_y, pass_2z, pass_2y, mid_z, mid_y,
    own_bf, pair_in, small_y, small_z, small_c, small_t, small_now,
    half_0, over_out_0, over_in_0, half_1, over_out_1, over_in_1,
    send, recv, small_send, small_recv, tp_send, tp_recv
):
    z, y, along_y, along_z = place()
    tp = lax.axis_index("tp")
    y_peers, z_peers, partner, tp_peers = all_peers(along_y, along_z)
    greet(y_peers + z_peers + [partner] + tp_peers)
    quarter, half = WIDE // 4, WIDE // 2

    def columns(sub):
        return pl.ds(sub * quarter, quarter)

    normed = PairSum(part, normed_out, half_0, over_out_0, over_in_0, tp_send, tp_recv, 0)
    first_z = RingScatter(
        lambda at, sub: grads.at[at, :, :, columns(sub)],
        lambda at, sub: grads[at, :, :, columns(sub)],
        held_z, pass_z, z, along_z, send, recv, 0,
    )
    first_y = RingScatter(
        lambda at, sub: last_grads.at[:, at] if sub else grads.at[:, at, :, columns(2)],
        lambda at, sub: last_grads[:, at] if sub else grads[:, at, :, columns(2)],
        held_y, pass_y, y, along_y, send, recv, 6,
    )
    mixed = PairSum(branch, mixed_out, half_1, over_out_1, over_in_1, tp_send, tp_recv, 6)
    to_y = spread(small, small_y, y, y_peers, small_send, small_recv, 0)
    normed.cross()
    first_z.relay()
    first_y.relay()
    small_now[0] = fold(small_y, y, small[...], to_y)
    to_z = spread(small_now.at[0], small_z, z, z_peers, small_send, small_recv, 3)
    mixed.cross()
    normed.close()
    for sub in range(2):
        mid_z[:, :, sub * quarter : (sub + 1) * quarter] = first_z.total(sub).astype(BF16)
    second_y = RingScatter(
        lambda at, sub: mid_z.at[at, :, columns(sub)],
        lambda at, sub: mid_z[at, :, columns(sub)],
        held_2y, pass_2y, y, along_y, send, recv, 12,
    )
    for sub in range(2):
        mid_y[:, :, sub * quarter : (sub + 1) * quarter] = first_y.total(sub).astype(BF16)
    second_z = RingScatter(
        lambda at, sub: mid_y.at[at, :, columns(sub)],
        lambda at, sub: mid_y[at, :, columns(sub)],
        held_2z, pass_2z, z, along_z, send, recv, 18,
    )
    small_now[1] = fold(small_z, z, small_now[0], to_z)
    to_ctx = remote(small_now.at[1], small_c, small_send.at[6], small_recv.at[6], partner)
    to_ctx.start()
    second_y.relay()
    second_z.relay()
    mixed.close(base)
    for sub in range(2):
        own_bf[:, sub * quarter : (sub + 1) * quarter] = second_y.total(sub).astype(BF16)
    for sub in range(2):
        own_bf[:, half + sub * quarter : half + (sub + 1) * quarter] = second_z.total(sub).astype(
            BF16
        )
    pair = remote(own_bf, pair_in, send.at[24], recv.at[24], partner)
    pair.start()
    to_ctx.wait_recv()
    small_now[2] = small_now[1] + small_c[...]
    shared = pl.ds(16, 8)
    to_tp = spread(small_now.at[2, shared], small_t, tp, tp_peers, small_send, small_recv, 7)
    normed.relay()
    pair.wait_recv()
    out[...] = own_bf[...].astype(F32) + pair_in[...].astype(F32)
    small_out[0:16] = small_now[2, 0:16]
    small_out[16:24] = fold(small_t, tp, small_now[2, 16:24], to_tp)
    mixed.relay()
    normed.finish()
    mixed.finish()
    for item in (first_z, first_y, second_y, second_z):
        item.finish()
    for item in to_y + to_z + to_tp + [to_ctx, pair]:
        item.wait_send()


def final_sums(grads, last_grads, small, part, branch, base):
    rows, columns = part.shape
    quarter = WIDE // 4
    return pl.pallas_call(
        final_kernel,
        out_shape=(
            jax.ShapeDtypeStruct((ROWS, WIDE), F32),
            jax.ShapeDtypeStruct(small.shape, F32),
            jax.ShapeDtypeStruct(part.shape, BF16),
            jax.ShapeDtypeStruct(part.shape, BF16),
        ),
        in_specs=[VM] * 6,
        out_specs=(VM,) * 4,
        scratch_shapes=[
            pltpu.VMEM((6, SIDE, ROWS, quarter), BF16),
            pltpu.VMEM((6, SIDE, ROWS, quarter), BF16),
            pltpu.VMEM((6, ROWS, quarter), BF16),
            pltpu.VMEM((6, ROWS, quarter), BF16),
            pltpu.VMEM((2, SIDE, ROWS, quarter), BF16),
            pltpu.VMEM((2, SIDE, ROWS, quarter), BF16),
            pltpu.VMEM((2, ROWS, quarter), BF16),
            pltpu.VMEM((2, ROWS, quarter), BF16),
            pltpu.VMEM((SIDE, ROWS, 2 * quarter), BF16),
            pltpu.VMEM((SIDE, ROWS, 2 * quarter), BF16),
            pltpu.VMEM((ROWS, WIDE), BF16),
            pltpu.VMEM((ROWS, WIDE), BF16),
            pltpu.VMEM((SIDE, *small.shape), F32),
            pltpu.VMEM((SIDE, *small.shape), F32),
            pltpu.VMEM(small.shape, F32),
            pltpu.VMEM((SIDE, 8, small.shape[1]), F32),
            pltpu.VMEM((3, *small.shape), F32),
            *pair_scratch(rows, columns),
            *pair_scratch(rows, columns),
            DMA((25,)),
            DMA((25,)),
            DMA((10,)),
            DMA((10,)),
            DMA((12,)),
            DMA((12,)),
        ],
        compiler_params=params(2),
    )(
        grads.reshape(SIDE, SIDE, ROWS, 3 * quarter),
        last_grads.reshape(SIDE, SIDE, ROWS, quarter),
        small,
        part,
        branch,
        base,
    )


def sum_all_kernel(part, out, held, send, recv):
    me = lax.axis_index("tp")
    peers = [{"tp": ahead(me, hop)} for hop in range(1, SIDE)]
    greet(peers)
    copies = spread(part, held, me, peers, send, recv, 0)
    out[...] = fold(held, me, part[...], copies)
    for item in copies:
        item.wait_send()


def sum_all(part, ident):
    return pl.pallas_call(
        sum_all_kernel,
        out_shape=jax.ShapeDtypeStruct(part.shape, part.dtype),
        in_specs=[VM],
        out_specs=VM,
        scratch_shapes=[pltpu.VMEM((4, *part.shape), part.dtype), DMA((3,)), DMA((3,))],
        compiler_params=params(ident),
    )(part)


def state_sum_kernel(part, values, slopes, out, values_in, slopes_in, state_in, half, over_out, over_in,
                     send, recv):
    partner = {"ctx": 1 - lax.axis_index("ctx")}
    me = lax.axis_index("tp")
    core, chip = lax.rem(me, 2), lax.div(me, 2)
    greet([{"tp": me + 1 - 2 * core}, {"tp": me + 2 - 4 * chip}, partner])
    total = PairSum(part, out, half, over_out, over_in, send, recv, 0)
    early = [
        remote(values, values_in, send.at[6], recv.at[6], partner),
        remote(slopes, slopes_in, send.at[7], recv.at[7], partner),
    ]
    for item in early:
        item.start()
    total.cross()
    total.close()
    total.relay()
    total.finish()
    late = remote(out.at[0:16], state_in, send.at[8], recv.at[8], partner)
    late.start()
    for item in early + [late]:
        item.wait()


def state_sum(part, values, slopes):
    rows, columns = part.shape
    return pl.pallas_call(
        state_sum_kernel,
        out_shape=(
            jax.ShapeDtypeStruct(part.shape, BF16),
            jax.ShapeDtypeStruct(values.shape, values.dtype),
            jax.ShapeDtypeStruct(slopes.shape, slopes.dtype),
            jax.ShapeDtypeStruct((16, columns), BF16),
        ),
        in_specs=[VM] * 3,
        out_specs=(VM,) * 4,
        scratch_shapes=[*pair_scratch(rows, columns), DMA((9,)), DMA((9,))],
        compiler_params=params(7),
    )(part, values, slopes)


LOCAL = 384
MIX = LOCAL + 2 * STATE
THIN = MIX + LOCAL
PROJ = THIN + 128
PAIRS = 3


def dot(left, right, left_dim=1, right_dim=0, precision=None):
    return lax.dot_general(
        left,
        right,
        (((left_dim,), (right_dim,)), ((), ())),
        preferred_element_type=F32,
        precision=precision,
    )


def lanes(rows, columns=128):
    return lax.broadcasted_iota(jnp.int32, (rows, columns), 1)


def expand(per_head):
    first = lanes(per_head.shape[0]) < HEAD
    return jnp.concatenate(
        [
            jnp.where(first, per_head[:, 2 * j : 2 * j + 1], per_head[:, 2 * j + 1 : 2 * j + 2])
            for j in range(PAIRS)
        ],
        axis=1,
    )


def head_sums(wide):
    lane = lanes(wide.shape[0])
    total = jnp.zeros(lane.shape, F32)
    for j in range(PAIRS):
        pair = wide[:, 128 * j : 128 * j + 128]
        even = jnp.sum(jnp.where(lane < HEAD, pair, 0.0), axis=1, keepdims=True)
        odd = jnp.sum(jnp.where(lane < HEAD, 0.0, pair), axis=1, keepdims=True)
        total = jnp.where(lane == 2 * j, even, jnp.where(lane == 2 * j + 1, odd, total))
    return total


def by_head(row, states):
    return jnp.concatenate(
        [row[:, h : h + 1] * states[HEAD * h : HEAD * h + HEAD] for h in range(2 * PAIRS)], axis=0
    )


def lower():
    shape = (GROUP, GROUP)
    return lax.broadcasted_iota(jnp.int32, shape, 0) >= lax.broadcasted_iota(jnp.int32, shape, 1)


def decay_of(cum, cum_t, h, mask):
    return jnp.exp(jnp.where(mask, cum[:, h : h + 1] - cum_t[h : h + 1], -1e30))


def project_kernel(ctx, stream, edge, full, conv, heads, normed_o, pre_o, slope_o, vals_o, gate_o,
                   step_o, sig_o, cum_o, cum_t_o, step_t_o, fresh_o, state_o, gain_o, padded):
    step = pl.program_id(0)

    def normalise(rows):
        scale = lax.rsqrt(jnp.mean(rows * rows, axis=-1, keepdims=True) + EPS)
        return (rows * scale * gain_o[0:1]).astype(BF16)

    @pl.when(step == 0)
    def _():
        gain_o[...] = jnp.broadcast_to(full[:, THIN:PROJ].astype(F32).T[6:7], gain_o.shape)
        rows = dot(normalise(edge[...].astype(F32)), full[:, :MIX])
        rows = rows * jnp.where(ctx[0] == 1, 1.0, 0.0)
        padded[0:8] = rows[8:16].astype(BF16).astype(F32)
        state_o[...] = jnp.zeros_like(state_o)

    @pl.when(step > 0)
    def _():
        padded[0:8] = padded[GROUP : GROUP + 8]

    normed = normalise(stream[...].astype(F32))
    normed_o[...] = normed
    projected = dot(normed, full[:, :PROJ])
    gate_o[...] = projected[:, MIX:THIN]
    pre = projected[:, :MIX].astype(BF16)
    pre_o[...] = pre
    padded[8:] = pre.astype(F32)
    conv_sum = conv[4:5] + sum(conv[k : k + 1] * padded[5 + k : 5 + k + GROUP] for k in range(CONV))
    sig = jax.nn.sigmoid(conv_sum)
    slope_o[...] = sig * (1.0 + conv_sum * (1.0 - sig))
    vals = (conv_sum * sig).astype(BF16)
    vals_o[...] = vals
    live = lanes(GROUP) < 2 * PAIRS
    raw = jnp.where(live, projected[:, THIN:PROJ] + heads[0:1], 0.0)
    sig_o[...] = jnp.where(live, jax.nn.sigmoid(raw), 0.0)
    step_val = jnp.maximum(raw, 0.0) + jnp.log1p(jnp.exp(-jnp.abs(raw)))
    step_val = jnp.where(live, step_val, 0.0)
    step_o[...] = step_val
    log_rate = -jnp.exp(heads[1:2]) * step_val
    cum = dot(lower().astype(F32), log_rate, precision=HIGH)
    cum_o[...] = cum
    cum_t_o[0] = cum.T[0:8]
    step_t_o[0] = step_val.T[0:8]
    last = cum[GROUP - 1 :]
    scales = step_val * jnp.exp(last - cum)
    weighted = (vals[:, :LOCAL].astype(F32) * expand(scales)).astype(BF16)
    fresh = dot(weighted, vals[:, LOCAL : LOCAL + STATE], 0, 0)
    fresh_o[0] = fresh
    state_o[...] = by_head(jnp.exp(last), state_o[...]) + fresh


def inside_kernel(vals, cum, cum_t, step_t, heads, up, full, local_o, back_o):
    back_o[...] = dot(up[...], full[:, PROJ:])
    keys, reads = vals[:, LOCAL : LOCAL + STATE], vals[:, LOCAL + STATE :]
    inner = dot(reads, keys, 1, 1)
    mask, first = lower(), lanes(GROUP) < HEAD
    skip = expand(heads[2:3])
    for j in range(PAIRS):
        here = slice(128 * j, 128 * j + 128)
        pair = vals[:, here]
        outs = []
        for h in (2 * j, 2 * j + 1):
            weights = inner * decay_of(cum, cum_t[0], h, mask) * step_t[0, h : h + 1]
            outs.append(dot(weights.astype(BF16), pair))
        local_o[:, here] = jnp.where(first, outs[0], outs[1]) + skip[:, here] * pair.astype(F32)


def sum_row(wide):
    folded = wide[:, :128] + wide[:, 128:256] + wide[:, 256:]
    return jnp.sum(folded.T, axis=0, keepdims=True)


def output_kernel(vals, local, gate, fresh, cum, entering, back, gain, ssd_o, states_o, sums_o,
                  state):
    @pl.when(pl.program_id(0) == 0)
    def _():
        state[...] = entering[...]

    here = state[...]
    states_o[0] = here
    state[...] = by_head(jnp.exp(cum[GROUP - 1 :]), here) + fresh[0]
    carried = dot(vals[:, LOCAL + STATE :], here.astype(BF16), 1, 1)
    ssd = local[...] + expand(jnp.exp(cum[...])) * carried
    ssd_o[...] = ssd
    gated = ssd * (gate[...] * jax.nn.sigmoid(gate[...]))
    sums_o[0:1] = sum_row(gated * gated)
    sums_o[1:2] = sum_row(back[...] * gain[...] * gated)
    sums_o[2:8] = jnp.zeros((6, GROUP), F32)


def gates_kernel(ssd, gate, back, sums, gain, vals, cum, normal_o, dy_o, dgate_o, read_o, chain_o,
                 dgain_o):
    @pl.when(pl.program_id(0) == 0)
    def _():
        chain_o[...] = jnp.zeros_like(chain_o)
        dgain_o[...] = jnp.zeros_like(dgain_o)

    both = sums[...].T
    scale = lax.rsqrt(both[:, 0:1] / INNER + EPS)
    gate_val, ssd_val = gate[...], ssd[...]
    sig = jax.nn.sigmoid(gate_val)
    act = gate_val * sig
    gated = ssd_val * act
    normal_o[...] = (gated * scale * gain[...]).astype(BF16)
    grad_normal = back[...]
    dgain_o[0:1] += jnp.sum(grad_normal * gated * scale, axis=0, keepdims=True)
    dgated = scale * (grad_normal * gain[...]) - gated * (scale * scale * scale) * (
        both[:, 1:2] / INNER
    )
    dy = (dgated * act).astype(BF16)
    dy_o[...] = dy
    dgate_o[...] = (dgated * ssd_val * (sig * (1.0 + gate_val * (1.0 - sig)))).astype(BF16)
    carried = (dy.astype(F32) * expand(jnp.exp(cum[...]))).astype(BF16)
    read = dot(carried, vals[:, LOCAL + STATE :], 0, 0)
    read_o[0] = read
    chain_o[...] = by_head(jnp.exp(cum[GROUP - 1 :]), chain_o[...]) + read


def split_dot(wide, low, left_dim):
    high = wide.astype(BF16)
    rest = (wide - high.astype(F32)).astype(BF16)
    return dot(high, low, left_dim) + dot(rest, low, left_dim)


def blocks_kernel(dy, vals, cum, cum_t, step_val, step_t, normal, up, full, states, heads, dval_o,
                  dcum_o, dstep_o, dstate_o, branch_o, dout_o, skip_o, total, skips, rows):
    step = pl.program_id(0)

    @pl.when(step == 0)
    def _():
        total[...] = jnp.zeros_like(total)
        skips[...] = jnp.zeros_like(skips)
        rows[...] = jnp.zeros_like(rows)

    branch_o[...] = dot(normal[...], full[:, PROJ:], 1, 1).astype(BF16)
    total[...] += dot(up[...], normal[...], 0, 0)
    dy_f, values_f = dy[...].astype(F32), vals[:, :LOCAL].astype(F32)
    skips[0:1] += jnp.sum(dy_f * values_f, axis=0, keepdims=True)
    keys, reads = vals[:, LOCAL : LOCAL + STATE], vals[:, LOCAL + STATE :]
    inner = dot(reads, keys, 1, 1)
    mask, lane = lower(), lanes(GROUP)
    first = lane < HEAD
    skip = expand(heads[2:3])
    dinner = jnp.zeros((GROUP, GROUP), F32)
    dcum = jnp.zeros((GROUP, 128), F32)
    for j in range(PAIRS):
        here = slice(128 * j, 128 * j + 128)
        pair, dy_pair = values_f[:, here], dy[:, here]
        outs = []
        for h in (2 * j, 2 * j + 1):
            own = jnp.where(first if h % 2 == 0 else ~first, pair, 0.0).astype(BF16)
            decays = decay_of(cum, cum_t[0], h, mask)
            scaled = dot(dy_pair, own, 1, 1) * decays
            step_row = step_t[0, h : h + 1]
            product = scaled * inner
            rows[h : h + 1] = jnp.sum(product, axis=0, keepdims=True)
            dcum = jnp.where(
                lane == h, jnp.sum(product * step_row, axis=1, keepdims=True), dcum
            )
            dinner = dinner + scaled * step_row
            outs.append(dot((inner * decays * step_row).astype(BF16), dy_pair, 0, 0))
        dval_o[:, here] = jnp.where(first, outs[0], outs[1]) + skip[:, here] * dy_f[:, here]
    dstep = rows[...].T
    dstep_o[...] = dstep
    low = states[0].astype(BF16)
    grad_exp = dy_f * expand(jnp.exp(cum[...]))
    dcum_o[...] = dcum - dstep * step_val[...] + head_sums(grad_exp * dot(reads, low, 1, 1))
    dstate_o[:, :STATE] = split_dot(dinner, reads, 0)
    dstate_o[:, STATE:] = dot(grad_exp.astype(BF16), low) + split_dot(dinner, keys, 1)

    @pl.when(step == pl.num_programs(0) - 1)
    def _():
        dout_o[...] = total[...].astype(BF16)
        skip_o[...] = head_sums(skips[...])


def states_kernel(vals, cum, step_val, sig, states, read, arriving, heads, dval, dcum, dstep, dstate,
                  dval_o, state_o, low_o, heads_o, carry):
    @pl.when(pl.program_id(0) == 0)
    def _():
        carry[...] = arriving[...]
        heads_o[...] = jnp.zeros_like(heads_o)

    out = carry[...]
    last = cum[GROUP - 1 :]
    decay = jnp.exp(last)
    carry[...] = by_head(decay, out) + read[0]
    product = out * states[0]
    row = lanes(1)
    dlast = jnp.zeros((1, 128), F32)
    for h in range(2 * PAIRS):
        own = jnp.sum(product[HEAD * h : HEAD * h + HEAD], axis=0, keepdims=True)
        dlast = jnp.where(row == h, jnp.sum(own, axis=1, keepdims=True), dlast)
    dlast = dlast * decay
    fresh = out.astype(BF16)
    keys = vals[:, LOCAL : LOCAL + STATE]
    values_f = vals[:, :LOCAL].astype(F32)
    to_end = jnp.exp(last - cum[...])
    scales = step_val[...] * to_end
    wide = expand(scales)
    dweighted = dot(keys, fresh, 1, 1)
    dval_o[...] = dval[...] + dweighted * wide
    state_o[:, :STATE] = (
        dstate[:, :STATE] + dot((values_f * wide).astype(BF16), fresh)
    ).astype(BF16)
    state_o[:, STATE:] = dstate[:, STATE:].astype(BF16)
    dscales = head_sums(dweighted * values_f)
    spill = dscales * scales
    dlast = dlast + jnp.sum(spill, axis=0, keepdims=True)
    at_end = lax.broadcasted_iota(jnp.int32, (GROUP, 128), 0) == GROUP - 1
    full_cum = dcum[...] - spill + jnp.where(at_end, dlast, 0.0)
    drate = dot(lower().astype(F32), full_cum, 0, 0, precision=HIGH)
    rate = jnp.exp(heads[1:2])
    total_step = dstep[...] + dscales * to_end - rate * drate
    pre = total_step * sig[...]
    low_o[...] = pre.astype(BF16)
    heads_o[0:1] += jnp.sum(pre, axis=0, keepdims=True)
    heads_o[1:2] += -rate * jnp.sum(drate * step_val[...], axis=0, keepdims=True)


def weights_kernel(where, dval, state, slope, pre, dgate, dstep, normed, stream, full, gain, conv,
                   values_next, state_next, slope_next, dgain, heads, skip,
                   part_o, dw_o, small_o, padded, total):
    step = pl.program_id(0)
    block = pl.num_programs(0) - 1 - step

    @pl.when(step == 0)
    def _():
        small_o[...] = jnp.zeros_like(small_o)
        ahead_of = jnp.concatenate([values_next[0:8], state_next[...].astype(F32)[0:8]], axis=1)
        padded[GROUP:] = ahead_of * slope_next[0:8] * jnp.where(where[0] == 0, 1.0, 0.0)
        padded[GROUP:] = jnp.where(
            lax.broadcasted_iota(jnp.int32, (8, MIX), 0) < CONV - 1, padded[GROUP:], 0.0
        )
        total[...] = jnp.zeros_like(total)

    @pl.when(step > 0)
    def _():
        padded[GROUP:] = padded[0:8]

    grad = jnp.concatenate([dval[...], state[...].astype(F32)], axis=1) * slope[...]
    padded[0:GROUP] = grad
    pre_f = pre[...].astype(F32)
    dinput = jnp.zeros((GROUP, MIX), F32)
    for k in range(CONV):
        moved = padded[CONV - 1 - k : CONV - 1 - k + GROUP]
        dinput = dinput + conv[k : k + 1] * moved
        taps = jnp.sum(moved * pre_f, axis=0, keepdims=True)
        small_o[k : k + 1] += taps[:, :LOCAL]
        small_o[6 + k : 7 + k, : 2 * STATE] += taps[:, LOCAL:]
    bias = jnp.sum(grad, axis=0, keepdims=True)
    small_o[4:5] += bias[:, :LOCAL]
    small_o[10:11, : 2 * STATE] += bias[:, LOCAL:]
    low = dinput.astype(BF16)
    rest = [dgate[...], dstep[...]]
    total[...] += dot(normed[...], jnp.concatenate([low] + rest, axis=1), 0, 0)
    share = jnp.where(where[1] == block, 1.0, 0.0)
    once = (dinput[:, LOCAL:] * share).astype(BF16)
    part = dot(jnp.concatenate([low[:, :LOCAL], once] + rest, axis=1), full[:, :PROJ], 1, 1)
    part_o[...] = part.astype(BF16)
    source = stream[...].astype(F32)
    scale = lax.rsqrt(jnp.mean(source * source, axis=-1, keepdims=True) + EPS)
    dnorm = jnp.sum(part * source * scale, axis=0, keepdims=True)
    small_o[16:17] += dnorm[:, :LOCAL]
    small_o[17:18] += dnorm[:, LOCAL:]

    @pl.when(block == 0)
    def _():
        small_o[5:6] = dgain[0:1]
        small_o[11:12, :128] = heads[0:1]
        small_o[12:13, :128] = heads[1:2]
        small_o[13:14, :128] = skip[0:1]
        dw_o[...] = total[...].astype(BF16)


def stream_kernel(normed, stream, up, gain, out):
    source, grad = stream[...].astype(F32), normed[...].astype(F32)
    scale = lax.rsqrt(jnp.mean(source * source, axis=-1, keepdims=True) + EPS)
    scaled = grad * gain[0:1]
    inner = jnp.sum(scaled * source, axis=1, keepdims=True) / D
    out[...] = up[...].astype(F32) + (
        scale * scaled - source * (scale * scale * scale) * inner
    )


BLOCKS = 4


def tokens_spec(columns, backward=False):
    return pl.BlockSpec((GROUP, columns), (lambda g: (BLOCKS - 1 - g, 0)) if backward else (lambda g: (g, 0)))


def cube_spec(rows, columns, backward=False):
    return pl.BlockSpec(
        (1, rows, columns), (lambda g: (BLOCKS - 1 - g, 0, 0)) if backward else (lambda g: (g, 0, 0))
    )


def row_spec(rows, backward=False):
    return pl.BlockSpec((rows, GROUP), (lambda g: (0, BLOCKS - 1 - g)) if backward else (lambda g: (0, g)))


def whole(*shape):
    return pl.BlockSpec(shape, lambda g: (0,) * len(shape))


SCALARS = pl.BlockSpec(memory_space=pltpu.SMEM)


def on_blocks(kernel, ins, outs, scratch, operands):
    return pl.pallas_call(
        kernel,
        grid=(BLOCKS,),
        in_specs=ins,
        out_specs=tuple(spec for spec, shape, dtype in outs),
        out_shape=tuple(jax.ShapeDtypeStruct(shape, dtype) for spec, shape, dtype in outs),
        scratch_shapes=scratch,
        compiler_params=pltpu.CompilerParams(vmem_limit_bytes=48 * 1024 * 1024),
    )(*operands)


def per_device(
    stream,
    norm_gain,
    w_gate,
    w_value,
    w_step,
    w_state,
    w_out,
    conv_value,
    conv_value_bias,
    conv_state,
    conv_state_bias,
    step_bias,
    decay_log,
    skip_gain,
    inner_gain,
    cotangent,
):
    count = stream.shape[1]
    heads_here = step_bias.shape[0]
    ctx, tp = lax.axis_index("ctx"), lax.axis_index("tp")
    rows, up = stream[0], cotangent[0]
    shard = jnp.concatenate(
        [
            w_value,
            w_state,
            w_gate,
            w_step,
            norm_gain[:, None],
            jnp.zeros((ROWS, 128 - heads_here - 1), BF16),
            w_out.T,
        ],
        axis=1,
    )
    conv = jnp.concatenate(
        [
            jnp.concatenate([conv_value, conv_value_bias[None]], axis=0),
            jnp.concatenate([conv_state, conv_state_bias[None]], axis=0),
        ],
        axis=1,
    )
    conv = jnp.pad(conv, ((0, 3), (0, 0)))
    heads = jnp.pad(
        jnp.stack([step_bias, decay_log, skip_gain]), ((0, 5), (0, 128 - heads_here))
    )
    gain_one = inner_gain[None]
    where = jnp.stack([ctx, tp]).astype(jnp.int32)
    full, edge = gather_weights(shard, rows[count - 16 :])

    def tokens_out(columns, dtype=F32, backward=False):
        return (tokens_spec(columns, backward), (count, columns), dtype)

    def cube_out(size, columns, backward=False):
        return (cube_spec(size, columns, backward), (BLOCKS, size, columns), F32)

    def whole_out(size, columns, dtype=F32):
        return (whole(size, columns), (size, columns), dtype)

    full_spec, heads_spec = whole(D, WIDE), whole(8, 128)
    (
        normed, pre, slope, vals, gate, step_val, sig, cum, cum_t, step_t, fresh, leaving, gain_zero
    ) = on_blocks(
        project_kernel,
        [SCALARS, tokens_spec(D), whole(16, D), full_spec, whole(8, MIX), heads_spec],
        [
            tokens_out(D, BF16),
            tokens_out(MIX, BF16),
            tokens_out(MIX),
            tokens_out(MIX, BF16),
            tokens_out(LOCAL),
            tokens_out(128),
            tokens_out(128),
            tokens_out(128),
            cube_out(8, GROUP),
            cube_out(8, GROUP),
            cube_out(LOCAL, STATE),
            whole_out(LOCAL, STATE),
            whole_out(8, D),
        ],
        [pltpu.VMEM((GROUP + 8, MIX), F32)],
        (where, rows, edge, full, conv, heads),
    )
    entering = lax.ppermute(leaving, "ctx", [(0, 1)])
    local, back = on_blocks(
        inside_kernel,
        [
            tokens_spec(MIX),
            tokens_spec(128),
            cube_spec(8, GROUP),
            cube_spec(8, GROUP),
            heads_spec,
            tokens_spec(D),
            full_spec,
        ],
        [tokens_out(LOCAL), tokens_out(LOCAL)],
        [],
        (vals, cum, cum_t, step_t, heads, up, full),
    )
    ssd, states, sums = on_blocks(
        output_kernel,
        [
            tokens_spec(MIX),
            tokens_spec(LOCAL),
            tokens_spec(LOCAL),
            cube_spec(LOCAL, STATE),
            tokens_spec(128),
            whole(LOCAL, STATE),
            tokens_spec(LOCAL),
            whole(1, LOCAL),
        ],
        [tokens_out(LOCAL), cube_out(LOCAL, STATE), (row_spec(8), (8, count), F32)],
        [pltpu.VMEM((LOCAL, STATE), F32)],
        (vals, local, gate, fresh, cum, entering, back, gain_one),
    )
    sums = sum_all(sums, 4)
    normal, dy, dgate, read, returning, dgain = on_blocks(
        gates_kernel,
        [
            tokens_spec(LOCAL, True),
            tokens_spec(LOCAL, True),
            tokens_spec(LOCAL, True),
            row_spec(8, True),
            whole(1, LOCAL),
            tokens_spec(MIX, True),
            tokens_spec(128, True),
        ],
        [
            tokens_out(LOCAL, BF16, True),
            tokens_out(LOCAL, BF16, True),
            tokens_out(LOCAL, BF16, True),
            cube_out(LOCAL, STATE, True),
            whole_out(LOCAL, STATE),
            whole_out(8, LOCAL),
        ],
        [],
        (ssd, gate, back, sums, gain_one, vals, cum),
    )
    arriving = lax.ppermute(returning, "ctx", [(1, 0)])
    dval, dcum, dstep, dstate, branch, dout, skip = on_blocks(
        blocks_kernel,
        [
            tokens_spec(LOCAL),
            tokens_spec(MIX),
            tokens_spec(128),
            cube_spec(8, GROUP),
            tokens_spec(128),
            cube_spec(8, GROUP),
            tokens_spec(LOCAL),
            tokens_spec(D),
            full_spec,
            cube_spec(LOCAL, STATE),
            heads_spec,
        ],
        [
            tokens_out(LOCAL),
            tokens_out(128),
            tokens_out(128),
            tokens_out(2 * STATE),
            tokens_out(D, BF16),
            whole_out(D, LOCAL, BF16),
            whole_out(8, 128),
        ],
        [
            pltpu.VMEM((D, LOCAL), F32),
            pltpu.VMEM((8, LOCAL), F32),
            pltpu.VMEM((128, GROUP), F32),
        ],
        (dy, vals, cum, cum_t, step_val, step_t, normal, up, full, states, heads),
    )
    dval, state_part, dstep_low, head_rows = on_blocks(
        states_kernel,
        [
            tokens_spec(MIX, True),
            tokens_spec(128, True),
            tokens_spec(128, True),
            tokens_spec(128, True),
            cube_spec(LOCAL, STATE, True),
            cube_spec(LOCAL, STATE, True),
            whole(LOCAL, STATE),
            heads_spec,
            tokens_spec(LOCAL, True),
            tokens_spec(128, True),
            tokens_spec(128, True),
            tokens_spec(2 * STATE, True),
        ],
        [
            tokens_out(LOCAL, F32, True),
            tokens_out(2 * STATE, BF16, True),
            tokens_out(128, BF16, True),
            whole_out(8, 128),
        ],
        [pltpu.VMEM((LOCAL, STATE), F32)],
        (vals, cum, step_val, sig, states, read, arriving, heads, dval, dcum, dstep, dstate),
    )
    state_total, values_next, slope_next, state_next = state_sum(
        state_part, dval[:16], slope[:16]
    )
    part, dw, small = on_blocks(
        weights_kernel,
        [
            SCALARS,
            tokens_spec(LOCAL, True),
            tokens_spec(2 * STATE, True),
            tokens_spec(MIX, True),
            tokens_spec(MIX, True),
            tokens_spec(LOCAL, True),
            tokens_spec(128, True),
            tokens_spec(D, True),
            tokens_spec(D, True),
            full_spec,
            whole(8, D),
            whole(8, MIX),
            whole(16, LOCAL),
            whole(16, 2 * STATE),
            whole(16, MIX),
            whole(8, LOCAL),
            heads_spec,
            heads_spec,
        ],
        [tokens_out(D, BF16, True), whole_out(D, PROJ, BF16), whole_out(24, LOCAL)],
        [pltpu.VMEM((GROUP + 8, MIX), F32), pltpu.VMEM((D, PROJ), F32)],
        (
            where, dval, state_total, slope, pre, dgate, dstep_low, normed, rows, full, gain_zero,
            conv, values_next, state_next, slope_next, dgain, head_rows, skip,
        ),
    )
    owned, totals, dnormed, mixed = final_sums(dw, dout, small, part, branch, rows)
    (d_stream,) = on_blocks(
        stream_kernel,
        [tokens_spec(D), tokens_spec(D), tokens_spec(D), whole(8, D)],
        [tokens_out(D)],
        [],
        (dnormed, rows, up, gain_zero),
    )
    gain_total = totals[16:18].reshape(D)
    return (
        mixed[None],
        d_stream[None],
        lax.dynamic_slice_in_dim(gain_total, lax.axis_index("dp") * ROWS, ROWS),
        owned[:, MIX:THIN],
        owned[:, :LOCAL],
        owned[:, THIN : THIN + heads_here],
        owned[:, LOCAL:MIX],
        owned[:, PROJ:].T,
        totals[:4],
        totals[4],
        totals[6:10, : 2 * STATE],
        totals[10, : 2 * STATE],
        totals[11, :heads_here],
        totals[12, :heads_here],
        totals[13, :heads_here],
        totals[5],
    )


def solution(mesh):
    in_specs = (
        P("dp", "ctx", None),
        P("dp"),
        P("dp", "tp"),
        P("dp", "tp"),
        P("dp", "tp"),
        P("dp", None),
        P("tp", "dp"),
        P(None, "tp"),
        P("tp"),
        P(),
        P(),
        P("tp"),
        P("tp"),
        P("tp"),
        P("tp"),
        P("dp", "ctx", None),
    )
    out_specs = (
        P("dp", "ctx", None),
        P("dp", "ctx", None),
        P("dp"),
        P("dp", "tp"),
        P("dp", "tp"),
        P("dp", "tp"),
        P("dp", None),
        P("tp", "dp"),
        P(None, "tp"),
        P("tp"),
        P(),
        P(),
        P("tp"),
        P("tp"),
        P("tp"),
        P("tp"),
    )
    return jax.shard_map(
        per_device, mesh=mesh, in_specs=in_specs, out_specs=out_specs, check_vma=False
    )
```

```python
import types

import jax
import jax.numpy as jnp
from jax import lax
from jax.experimental import pallas as pl
from jax.experimental.pallas import tpu as pltpu
from jax.sharding import PartitionSpec as P

D = 768
HEAD = 64
STATE = 128
CONV = 4
GROUP = 256
INNER = 1536


EPS = 1e-05
HIGH = lax.Precision.HIGHEST


MESH = pl.DeviceIdType.MESH
VM = pl.BlockSpec(memory_space=pltpu.VMEM)
SIDE = 4
ROWS = 48
WIDE = 1536
LOCAL = 384
DMA = pltpu.SemaphoreType.DMA
F32 = jnp.float32
BF16 = jnp.bfloat16


def params(ident, limit=20):
    return pltpu.CompilerParams(
        collective_id=ident, has_side_effects=True, vmem_limit_bytes=limit * 1024 * 1024
    )


def remote(source, target, send, recv, where):
    return pltpu.make_async_remote_copy(
        src_ref=source,
        dst_ref=target,
        send_sem=send,
        recv_sem=recv,
        device_id=where,
        device_id_type=MESH,
    )


def greet(peers):
    barrier = pltpu.get_barrier_semaphore()
    for where in peers:
        pl.semaphore_signal(barrier, inc=1, device_id=where, device_id_type=MESH)
    pl.semaphore_wait(barrier, len(peers))


def place():
    me = lax.axis_index("dp")
    z, y = lax.div(me, SIDE), lax.rem(me, SIDE)

    def along_y(hop):
        return {"dp": z * SIDE + lax.rem(y + hop, SIDE)}

    def along_z(hop):
        return {"dp": lax.rem(z + hop, SIDE) * SIDE + y}

    return z, y, along_y, along_z


def ahead(position, hop):
    return lax.rem(position + hop, SIDE)


class Gather:
    def __init__(self, shard, full, first, y_first, send, recv, slot):
        z, y, along_y, along_z = place()
        columns = pl.ds(first, LOCAL)
        self.send, self.recv, self.slot = send, recv, slot
        if y_first:
            self.position, self.along, near = z, along_z, along_y
            self.block = lambda at, sub: full.at[at, pl.ds(2 * sub, 2), :, columns]
        else:
            self.position, self.along, near = y, along_y, along_z
            self.block = lambda at, sub: full.at[pl.ds(2 * sub, 2), at, :, columns]
        self.near = [
            remote(
                shard.at[:, columns],
                full.at[z, y, :, columns],
                send.at[slot + hop],
                recv.at[slot + hop],
                near(hop + 1),
            )
            for hop in range(3)
        ]
        for item in self.near:
            item.start()

    def copy(self, position, sub, slot, hop):
        item = remote(
            self.block(position, sub),
            self.block(position, sub),
            self.send.at[self.slot + slot],
            self.recv.at[self.slot + slot],
            self.along(hop),
        )
        item.start()
        return item

    def turn(self):
        for item in self.near:
            item.wait_recv()
        self.direct = [
            self.copy(self.position, 0, 3, 1),
            self.copy(self.position, 1, 4, 3),
            self.copy(self.position, 1, 5, 1),
            self.copy(self.position, 0, 6, 3),
        ]

    def relay(self):
        self.direct[0].wait_recv()
        one = self.copy(ahead(self.position, 3), 0, 7, 1)
        self.direct[1].wait_recv()
        two = self.copy(ahead(self.position, 1), 1, 8, 3)
        self.relayed = [one, two]

    def finish(self):
        for item in self.direct[2:] + self.relayed:
            item.wait_recv()

    def close(self):
        for item in self.near + self.direct + self.relayed:
            item.wait_send()


class RingScatter:
    def __init__(self, block, load, held, passed, position, along, send, recv, first):
        self.block, self.load, self.held, self.passed = block, load, held, passed
        self.position, self.along = position, along
        self.send, self.recv, self.first = send, recv, first
        far, right, left = ahead(position, 2), ahead(position, 1), ahead(position, 3)
        self.direct = [
            self.copy(block(far, 0), 0, 1),
            self.copy(block(far, 1), 1, 3),
            self.copy(block(right, 1), 2, 1),
            self.copy(block(left, 0), 3, 3),
        ]
        for item in self.direct:
            item.start()

    def copy(self, source, slot, hop):
        return remote(
            source,
            self.held.at[slot],
            self.send.at[self.first + slot],
            self.recv.at[self.first + slot],
            self.along(hop),
        )

    def relay(self):
        right, left = ahead(self.position, 1), ahead(self.position, 3)
        self.direct[0].wait_recv()
        self.passed[0] = (self.held[0].astype(F32) + self.load(right, 0).astype(F32)).astype(BF16)
        one = self.copy(self.passed.at[0], 4, 1)
        one.start()
        self.direct[1].wait_recv()
        self.passed[1] = (self.held[1].astype(F32) + self.load(left, 1).astype(F32)).astype(BF16)
        two = self.copy(self.passed.at[1], 5, 3)
        two.start()
        self.relayed = [one, two]

    def total(self, sub):
        own = self.load(self.position, sub).astype(F32)
        if sub == 0:
            self.direct[3].wait_recv()
            self.relayed[0].wait_recv()
            return own + self.held[3].astype(F32) + self.held[4].astype(F32)
        self.direct[2].wait_recv()
        self.relayed[1].wait_recv()
        return own + self.held[2].astype(F32) + self.held[5].astype(F32)

    def finish(self):
        for item in self.direct + self.relayed:
            item.wait_send()


class PairSum:
    def __init__(self, part, out, half_in, over_out, over_in, send, recv, first):
        self.part, self.out = part, out
        self.half_in, self.over_out, self.over_in = half_in, over_out, over_in
        self.send, self.recv, self.first = send, recv, first
        me = lax.axis_index("tp")
        core, chip = lax.rem(me, 2), lax.div(me, 2)
        self.twin, self.across = {"tp": me + 1 - 2 * core}, {"tp": me + 2 - 4 * chip}
        size = part.shape[0] // 4

        def quarter(c, h):
            return pl.ds(pl.multiple_of((2 * c + h) * size, size), size)

        self.keep, self.give = quarter(core, chip), quarter(core, 1 - chip)
        self.sends = [
            self.copy(part.at[quarter(1 - core, 1 - chip)], half_in.at[0], 0, self.twin),
            self.copy(part.at[quarter(1 - core, chip)], half_in.at[1], 1, self.twin),
        ]

    def copy(self, source, target, slot, where):
        item = remote(
            source, target, self.send.at[self.first + slot], self.recv.at[self.first + slot], where
        )
        item.start()
        return item

    def cross(self):
        self.sends[0].wait_recv()
        self.over_out[...] = (
            self.part[self.give].astype(F32) + self.half_in[0].astype(F32)
        ).astype(BF16)
        self.sends.append(self.copy(self.over_out, self.over_in, 2, self.across))

    def close(self, base=None):
        self.sends[1].wait_recv()
        self.sends[2].wait_recv()
        total = self.part[self.keep].astype(F32) + self.half_in[1].astype(F32)
        total = total + self.over_in[...].astype(F32)
        if base is not None:
            total = total + base[self.keep].astype(F32)
        self.out[self.keep] = total.astype(BF16)
        mine = self.out.at[self.keep]
        self.sends.append(self.copy(mine, mine, 3, self.across))
        self.sends.append(self.copy(mine, mine, 4, self.twin))

    def relay(self):
        self.sends[3].wait_recv()
        other = self.out.at[self.give]
        self.sends.append(self.copy(other, other, 5, self.twin))

    def finish(self):
        self.sends[4].wait_recv()
        self.sends[5].wait_recv()
        for item in self.sends:
            item.wait_send()


def pair_scratch(rows, columns):
    return [
        pltpu.VMEM((2, rows // 4, columns), BF16),
        pltpu.VMEM((rows // 4, columns), BF16),
        pltpu.VMEM((rows // 4, columns), BF16),
    ]


def all_peers(along_y, along_z):
    me, partner = lax.axis_index("tp"), {"ctx": 1 - lax.axis_index("ctx")}
    hops = range(1, SIDE)
    tp_peers = [{"tp": ahead(me, hop)} for hop in hops]
    return [along_y(hop) for hop in hops], [along_z(hop) for hop in hops], partner, tp_peers


def spread(source, held, own, peers, send, recv, first):
    copies = [
        remote(source, held.at[own], send.at[first + hop], recv.at[first + hop], peer)
        for hop, peer in enumerate(peers)
    ]
    for item in copies:
        item.start()
    return copies


def fold(held, own, value, copies):
    held[own] = value
    for item in copies:
        item.wait_recv()
    return (held[0] + held[1]) + (held[2] + held[3])


class WeightSum:
    def __init__(self, grads, z_first, scratch, send, recv, first):
        self.held, self.passed, self.mid, self.second = scratch
        z, y, along_y, along_z = place()
        self.grads, self.send, self.recv, self.first = grads, send, recv, first
        if z_first:
            block = lambda at, sub: grads.at[at, pl.ds(2 * sub, 2)]
            load = lambda at, sub: grads[at, pl.ds(2 * sub, 2)]
            self.later, self.along = y, along_y
            self.ring = RingScatter(block, load, self.held, self.passed, z, along_z, send, recv, first)
        else:
            block = lambda at, sub: grads.at[pl.ds(2 * sub, 2), at]
            load = lambda at, sub: grads[pl.ds(2 * sub, 2), at]
            self.later, self.along = z, along_z
            self.ring = RingScatter(block, load, self.held, self.passed, y, along_y, send, recv, first)

    def turn(self):
        for sub in range(2):
            self.mid[2 * sub : 2 * sub + 2] = self.ring.total(sub).astype(BF16)
        self.copies = []
        for hop in range(1, SIDE):
            slot = self.first + 5 + hop
            item = remote(
                self.mid.at[ahead(self.later, hop)],
                self.second.at[self.later],
                self.send.at[slot],
                self.recv.at[slot],
                self.along(hop),
            )
            item.start()
            self.copies.append(item)

    def total(self):
        self.second[self.later] = self.mid[self.later]
        for item in self.copies:
            item.wait_recv()
        held = [self.second[index].astype(F32) for index in range(SIDE)]
        return (held[0] + held[1]) + (held[2] + held[3])

    def finish(self):
        self.ring.finish()
        for item in self.copies:
            item.wait_send()


def weight_scratch():
    return [
        pltpu.VMEM((6, 2, ROWS, LOCAL), BF16),
        pltpu.VMEM((2, 2, ROWS, LOCAL), BF16),
        pltpu.VMEM((SIDE, ROWS, LOCAL), BF16),
        pltpu.VMEM((SIDE, ROWS, LOCAL), BF16),
    ]


BLOCKS = 4
LIMIT = 20
MIX = LOCAL + 2 * STATE
THIN = MIX + 128
PROJ = THIN + LOCAL
PAIRS = 3


def dot(left, right, left_dim=1, right_dim=0, precision=None):
    return lax.dot_general(
        left,
        right,
        (((left_dim,), (right_dim,)), ((), ())),
        preferred_element_type=F32,
        precision=precision,
    )


def lanes(rows, columns=128):
    return lax.broadcasted_iota(jnp.int32, (rows, columns), 1)


def expand(per_head):
    first = lanes(per_head.shape[0]) < HEAD
    return jnp.concatenate(
        [
            jnp.where(first, per_head[:, 2 * j : 2 * j + 1], per_head[:, 2 * j + 1 : 2 * j + 2])
            for j in range(PAIRS)
        ],
        axis=1,
    )


def head_sums(wide):
    lane = lanes(wide.shape[0])
    total = jnp.zeros(lane.shape, F32)
    for j in range(PAIRS):
        pair = wide[:, 128 * j : 128 * j + 128]
        even = jnp.sum(jnp.where(lane < HEAD, pair, 0.0), axis=1, keepdims=True)
        odd = jnp.sum(jnp.where(lane < HEAD, 0.0, pair), axis=1, keepdims=True)
        total = jnp.where(lane == 2 * j, even, jnp.where(lane == 2 * j + 1, odd, total))
    return total


def by_head(row, states):
    return jnp.concatenate(
        [row[:, h : h + 1] * states[HEAD * h : HEAD * h + HEAD] for h in range(2 * PAIRS)], axis=0
    )


def lower():
    shape = (GROUP, GROUP)
    return lax.broadcasted_iota(jnp.int32, shape, 0) >= lax.broadcasted_iota(jnp.int32, shape, 1)


def decay_of(cum, cum_t, h, mask):
    return jnp.exp(jnp.where(mask, cum[:, h : h + 1] - cum_t[h : h + 1], -1e30))


def project_kernel(step, ctx, stream, edge, full, conv, heads, normed_o, pre_o, slope_o, vals_o,
                   step_o, sig_o, cum_o, cum_t_o, step_t_o, fresh_o, state_o, gain_o, padded):

    def normalise(rows):
        scale = lax.rsqrt(jnp.mean(rows * rows, axis=-1, keepdims=True) + EPS)
        return (rows * scale * gain_o[0:1]).astype(BF16)

    @pl.when(step == 0)
    def _():
        gain_o[...] = jnp.broadcast_to(full[:, MIX:THIN].astype(F32).T[6:7], gain_o.shape)
        rows = dot(normalise(edge[...].astype(F32)), full[:, :MIX])
        rows = rows * jnp.where(ctx[0] == 1, 1.0, 0.0)
        padded[0:8] = rows[8:16].astype(BF16).astype(F32)
        state_o[...] = jnp.zeros_like(state_o)

    @pl.when(step > 0)
    def _():
        padded[0:8] = padded[GROUP : GROUP + 8]

    normed = normalise(stream[...].astype(F32))
    normed_o[...] = normed
    projected = dot(normed, full[:, :THIN])
    pre = projected[:, :MIX].astype(BF16)
    pre_o[...] = pre
    padded[8:] = pre.astype(F32)
    conv_sum = conv[4:5] + sum(conv[k : k + 1] * padded[5 + k : 5 + k + GROUP] for k in range(CONV))
    sig = jax.nn.sigmoid(conv_sum)
    slope_o[...] = sig * (1.0 + conv_sum * (1.0 - sig))
    vals = (conv_sum * sig).astype(BF16)
    vals_o[...] = vals
    live = lanes(GROUP) < 2 * PAIRS
    raw = jnp.where(live, projected[:, MIX:THIN] + heads[0:1], 0.0)
    sig_o[...] = jnp.where(live, jax.nn.sigmoid(raw), 0.0)
    step_val = jnp.maximum(raw, 0.0) + jnp.log1p(jnp.exp(-jnp.abs(raw)))
    step_val = jnp.where(live, step_val, 0.0)
    step_o[...] = step_val
    log_rate = -jnp.exp(heads[1:2]) * step_val
    cum = dot(lower().astype(F32), log_rate, precision=HIGH)
    cum_o[...] = cum
    cum_t_o[0] = cum.T[0:8]
    step_t_o[0] = step_val.T[0:8]
    last = cum[GROUP - 1 :]
    scales = step_val * jnp.exp(last - cum)
    weighted = (vals[:, :LOCAL].astype(F32) * expand(scales)).astype(BF16)
    fresh = dot(weighted, vals[:, LOCAL : LOCAL + STATE], 0, 0)
    fresh_o[0] = fresh
    state_o[...] = by_head(jnp.exp(last), state_o[...]) + fresh


def inside_kernel(step, vals, cum, cum_t, step_t, heads, up, normed, full, local_o, back_o, gate_o):
    gate_o[...] = dot(normed[...], full[:, THIN:PROJ])
    back_o[...] = dot(up[...], full[:, PROJ:])
    keys, reads = vals[:, LOCAL : LOCAL + STATE], vals[:, LOCAL + STATE :]
    inner = dot(reads, keys, 1, 1)
    mask, first = lower(), lanes(GROUP) < HEAD
    skip = expand(heads[2:3])
    for j in range(PAIRS):
        here = slice(128 * j, 128 * j + 128)
        pair = vals[:, here]
        outs = []
        for h in (2 * j, 2 * j + 1):
            weights = inner * decay_of(cum, cum_t[0], h, mask) * step_t[0, h : h + 1]
            outs.append(dot(weights.astype(BF16), pair))
        local_o[:, here] = jnp.where(first, outs[0], outs[1]) + skip[:, here] * pair.astype(F32)


def sum_row(wide):
    folded = wide[:, :128] + wide[:, 128:256] + wide[:, 256:]
    return jnp.sum(folded.T, axis=0, keepdims=True)


def output_kernel(step, vals, local, gate, fresh, cum, entering, back, gain, ssd_o, states_o, sums_o,
                  state):
    @pl.when(step == 0)
    def _():
        state[...] = entering[...]

    here = state[...]
    states_o[0] = here
    state[...] = by_head(jnp.exp(cum[GROUP - 1 :]), here) + fresh[0]
    carried = dot(vals[:, LOCAL + STATE :], here.astype(BF16), 1, 1)
    ssd = local[...] + expand(jnp.exp(cum[...])) * carried
    ssd_o[...] = ssd
    gated = ssd * (gate[...] * jax.nn.sigmoid(gate[...]))
    sums_o[0:1] = sum_row(gated * gated)
    sums_o[1:2] = sum_row(back[...] * gain[...] * gated)
    sums_o[2:8] = jnp.zeros((6, GROUP), F32)


def gates_kernel(step, ssd, gate, back, sums, gain, vals, cum, full, normal_o, dy_o, dgate_o, read_o,
                 chain_o, dgain_o, branch_o):
    @pl.when(step == 0)
    def _():
        chain_o[...] = jnp.zeros_like(chain_o)
        dgain_o[...] = jnp.zeros_like(dgain_o)

    both = sums[...].T
    scale = lax.rsqrt(both[:, 0:1] / INNER + EPS)
    gate_val, ssd_val = gate[...], ssd[...]
    sig = jax.nn.sigmoid(gate_val)
    act = gate_val * sig
    gated = ssd_val * act
    normal = (gated * scale * gain[...]).astype(BF16)
    normal_o[...] = normal
    branch_o[...] = dot(normal, full[:, PROJ:], 1, 1).astype(BF16)
    grad_normal = back[...]
    dgain_o[0:1] += jnp.sum(grad_normal * gated * scale, axis=0, keepdims=True)
    dgated = scale * (grad_normal * gain[...]) - gated * (scale * scale * scale) * (
        both[:, 1:2] / INNER
    )
    dy = (dgated * act).astype(BF16)
    dy_o[...] = dy
    dgate_o[...] = (dgated * ssd_val * (sig * (1.0 + gate_val * (1.0 - sig)))).astype(BF16)
    carried = (dy.astype(F32) * expand(jnp.exp(cum[...]))).astype(BF16)
    read = dot(carried, vals[:, LOCAL + STATE :], 0, 0)
    read_o[0] = read
    chain_o[...] = by_head(jnp.exp(cum[GROUP - 1 :]), chain_o[...]) + read


def split_dot(wide, low, left_dim):
    high = wide.astype(BF16)
    rest = (wide - high.astype(F32)).astype(BF16)
    return dot(high, low, left_dim) + dot(rest, low, left_dim)


def blocks_kernel(step, dy, vals, cum, cum_t, step_val, step_t, states, heads, dval_o, dcum_o, dstep_o,
                  dstate_o, skip_o, skips, rows):

    @pl.when(step == 0)
    def _():
        skips[...] = jnp.zeros_like(skips)
        rows[...] = jnp.zeros_like(rows)

    dy_f, values_f = dy[...].astype(F32), vals[:, :LOCAL].astype(F32)
    skips[0:1] += jnp.sum(dy_f * values_f, axis=0, keepdims=True)
    keys, reads = vals[:, LOCAL : LOCAL + STATE], vals[:, LOCAL + STATE :]
    inner = dot(reads, keys, 1, 1)
    mask, lane = lower(), lanes(GROUP)
    first = lane < HEAD
    skip = expand(heads[2:3])
    dinner = jnp.zeros((GROUP, GROUP), F32)
    dcum = jnp.zeros((GROUP, 128), F32)
    for j in range(PAIRS):
        here = slice(128 * j, 128 * j + 128)
        pair, dy_pair = values_f[:, here], dy[:, here]
        outs = []
        for h in (2 * j, 2 * j + 1):
            own = jnp.where(first if h % 2 == 0 else ~first, pair, 0.0).astype(BF16)
            decays = decay_of(cum, cum_t[0], h, mask)
            scaled = dot(dy_pair, own, 1, 1) * decays
            step_row = step_t[0, h : h + 1]
            product = scaled * inner
            rows[h : h + 1] = jnp.sum(product, axis=0, keepdims=True)
            dcum = jnp.where(
                lane == h, jnp.sum(product * step_row, axis=1, keepdims=True), dcum
            )
            dinner = dinner + scaled * step_row
            outs.append(dot((inner * decays * step_row).astype(BF16), dy_pair, 0, 0))
        dval_o[:, here] = jnp.where(first, outs[0], outs[1]) + skip[:, here] * dy_f[:, here]
    dstep = rows[...].T
    dstep_o[...] = dstep
    low = states[0].astype(BF16)
    grad_exp = dy_f * expand(jnp.exp(cum[...]))
    dcum_o[...] = dcum - dstep * step_val[...] + head_sums(grad_exp * dot(reads, low, 1, 1))
    dstate_o[:, :STATE] = split_dot(dinner, reads, 0)
    dstate_o[:, STATE:] = dot(grad_exp.astype(BF16), low) + split_dot(dinner, keys, 1)

    @pl.when(step == BLOCKS - 1)
    def _():
        skip_o[...] = head_sums(skips[...])


def states_kernel(step, vals, cum, step_val, sig, states, read, arriving, heads, dval, dcum, dstep, dstate,
                  dval_o, state_o, low_o, heads_o, carry):
    @pl.when(step == 0)
    def _():
        carry[...] = arriving[...]
        heads_o[...] = jnp.zeros_like(heads_o)

    out = carry[...]
    last = cum[GROUP - 1 :]
    decay = jnp.exp(last)
    carry[...] = by_head(decay, out) + read[0]
    product = out * states[0]
    row = lanes(1)
    dlast = jnp.zeros((1, 128), F32)
    for h in range(2 * PAIRS):
        own = jnp.sum(product[HEAD * h : HEAD * h + HEAD], axis=0, keepdims=True)
        dlast = jnp.where(row == h, jnp.sum(own, axis=1, keepdims=True), dlast)
    dlast = dlast * decay
    fresh = out.astype(BF16)
    keys = vals[:, LOCAL : LOCAL + STATE]
    values_f = vals[:, :LOCAL].astype(F32)
    to_end = jnp.exp(last - cum[...])
    scales = step_val[...] * to_end
    wide = expand(scales)
    dweighted = dot(keys, fresh, 1, 1)
    dval_o[...] = dval[...] + dweighted * wide
    state_o[:, :STATE] = (
        dstate[:, :STATE] + dot((values_f * wide).astype(BF16), fresh)
    ).astype(BF16)
    state_o[:, STATE:] = dstate[:, STATE:].astype(BF16)
    dscales = head_sums(dweighted * values_f)
    spill = dscales * scales
    dlast = dlast + jnp.sum(spill, axis=0, keepdims=True)
    at_end = lax.broadcasted_iota(jnp.int32, (GROUP, 128), 0) == GROUP - 1
    full_cum = dcum[...] - spill + jnp.where(at_end, dlast, 0.0)
    drate = dot(lower().astype(F32), full_cum, 0, 0, precision=HIGH)
    rate = jnp.exp(heads[1:2])
    total_step = dstep[...] + dscales * to_end - rate * drate
    pre = total_step * sig[...]
    low_o[...] = pre.astype(BF16)
    heads_o[0:1] += jnp.sum(pre, axis=0, keepdims=True)
    heads_o[1:2] += -rate * jnp.sum(drate * step_val[...], axis=0, keepdims=True)


def weights_kernel(step, where, dval, state, slope, pre, dgate, dstep, normed, stream, full, gain, conv,
                   values_next, state_next, slope_next, dgain, heads, skip,
                   part_o, dvalue_o, dstate_o, small_o, padded, total):
    block = BLOCKS - 1 - step

    @pl.when(step == 0)
    def _():
        small_o[...] = jnp.zeros_like(small_o)
        ahead_of = jnp.concatenate([values_next[0:8], state_next[...].astype(F32)[0:8]], axis=1)
        padded[GROUP:] = ahead_of * slope_next[0:8] * jnp.where(where[0] == 0, 1.0, 0.0)
        padded[GROUP:] = jnp.where(
            lax.broadcasted_iota(jnp.int32, (8, MIX), 0) < CONV - 1, padded[GROUP:], 0.0
        )
        total[...] = jnp.zeros_like(total)

    @pl.when(step > 0)
    def _():
        padded[GROUP:] = padded[0:8]

    grad = jnp.concatenate([dval[...], state[...].astype(F32)], axis=1) * slope[...]
    padded[0:GROUP] = grad
    pre_f = pre[...].astype(F32)
    dinput = jnp.zeros((GROUP, MIX), F32)
    for k in range(CONV):
        moved = padded[CONV - 1 - k : CONV - 1 - k + GROUP]
        dinput = dinput + conv[k : k + 1] * moved
        taps = jnp.sum(moved * pre_f, axis=0, keepdims=True)
        small_o[k : k + 1] += taps[:, :LOCAL]
        small_o[6 + k : 7 + k, : 2 * STATE] += taps[:, LOCAL:]
    bias = jnp.sum(grad, axis=0, keepdims=True)
    small_o[4:5] += bias[:, :LOCAL]
    small_o[10:11, : 2 * STATE] += bias[:, LOCAL:]
    low = dinput.astype(BF16)
    rest = [dstep[...], dgate[...]]
    total[...] += dot(normed[...], jnp.concatenate([low, dstep[...]], axis=1), 0, 0)
    share = jnp.where(where[1] == block, 1.0, 0.0)
    once = (dinput[:, LOCAL:] * share).astype(BF16)
    part = dot(jnp.concatenate([low[:, :LOCAL], once] + rest, axis=1), full[:, :PROJ], 1, 1)
    part_o[...] = part.astype(BF16)
    source = stream[...].astype(F32)
    scale = lax.rsqrt(jnp.mean(source * source, axis=-1, keepdims=True) + EPS)
    dnorm = jnp.sum(part * source * scale, axis=0, keepdims=True)
    small_o[16:17] += dnorm[:, :LOCAL]
    small_o[17:18] += dnorm[:, LOCAL:]

    @pl.when(block == 0)
    def _():
        small_o[5:6] = dgain[0:1]
        small_o[11:12, :128] = heads[0:1]
        small_o[12:13, :128] = heads[1:2]
        small_o[13:14, :128] = skip[0:1]
        dvalue_o[...] = gridded(total[:, :LOCAL])
        dstate_o[...] = gridded(total[:, LOCAL:])


def last_kernel(normed, stream, up, gain, branch, value, state, gate, small,
                out, mixed, value_o, state_o, step_o, gate_o, taps_o, state_taps_o):
    step = pl.program_id(0)
    source, grad = stream[...].astype(F32), normed[...].astype(F32)
    scale = lax.rsqrt(jnp.mean(source * source, axis=-1, keepdims=True) + EPS)
    scaled = grad * gain[0:1]
    inner = jnp.sum(scaled * source, axis=1, keepdims=True) / D
    out[...] = up[...].astype(F32) + (
        scale * scaled - source * (scale * scale * scale) * inner
    )

    mixed[...] = branch[...]

    @pl.when(step == 0)
    def _():
        value_o[...] = value[...]
        gate_o[...] = gate[...]
        state_o[...] = state[:, : 2 * STATE]
        step_o[...] = state[:, 2 * STATE : 2 * STATE + step_o.shape[1]]
        taps_o[...] = small[0:4]
        state_taps_o[...] = small[6:10, : 2 * STATE]


def finish(normed, stream, up, gain, branch, value, state, gate, small, heads_here):
    by_block = pl.BlockSpec((GROUP, D), lambda g: (g, 0))

    def all_of(*shape):
        return pl.BlockSpec(shape, lambda g: (0, 0))

    owned = (ROWS, LOCAL)
    small_shapes = [
        owned, (ROWS, 2 * STATE), (ROWS, heads_here), owned, (CONV, LOCAL), (CONV, 2 * STATE)
    ]
    return pl.pallas_call(
        last_kernel,
        grid=(BLOCKS,),
        in_specs=[
            by_block,
            by_block,
            by_block,
            all_of(8, D),
            by_block,
            all_of(*owned),
            all_of(*owned),
            all_of(*owned),
            all_of(24, LOCAL),
        ],
        out_specs=(by_block, by_block, *[all_of(*shape) for shape in small_shapes]),
        out_shape=(
            jax.ShapeDtypeStruct(stream.shape, F32),
            jax.ShapeDtypeStruct(stream.shape, BF16),
            *[jax.ShapeDtypeStruct(shape, F32) for shape in small_shapes],
        ),
        compiler_params=pltpu.CompilerParams(vmem_limit_bytes=LIMIT * 1024 * 1024),
    )(normed, stream, up, gain, branch, value, state, gate, small)


def place_of(step, backward):
    return (BLOCKS - 1 - step) if backward else step


def tokens_spec(columns, backward=False):
    def view(ref, step):
        start = pl.multiple_of(place_of(step, backward) * GROUP, GROUP)
        return ref.at[pl.ds(start, GROUP)]

    return view


def cube_spec(rows, columns, backward=False):
    return lambda ref, step: ref.at[pl.ds(place_of(step, backward), 1)]


def row_spec(rows, backward=False):
    def view(ref, step):
        start = pl.multiple_of(place_of(step, backward) * GROUP, GROUP)
        return ref.at[:, pl.ds(start, GROUP)]

    return view


def whole(*shape):
    return lambda ref, step: ref


class Flat:
    def __init__(self, ref):
        self.ref = ref

    def __getitem__(self, key):
        found = self.ref[:, :, :, key[1]]
        return found.reshape(D, found.shape[-1])


def gridded(total):
    return total.astype(BF16).reshape(SIDE, SIDE, ROWS, total.shape[-1])


def sweep(kernel, pairs, start=0, stop=BLOCKS):
    def step(index, carry):
        kernel(index, *[item[1](item[0], index) if type(item) is tuple else item for item in pairs])
        return carry

    lax.fori_loop(start, stop, step, 0)


COUNT = BLOCKS * GROUP
HALF = COUNT // 2
KEPT = dict(
    full=((SIDE, SIDE, ROWS, WIDE), BF16),
    edge_in=((16, D), BF16),
    normed=((COUNT, D), BF16),
    pre=((COUNT, MIX), BF16),
    slope=((COUNT, MIX), F32),
    vals=((COUNT, MIX), BF16),
    step_val=((COUNT, 128), F32),
    sig=((COUNT, 128), F32),
    cum=((COUNT, 128), F32),
    cum_t=((BLOCKS, 8, GROUP), F32),
    step_t=((BLOCKS, 8, GROUP), F32),
    fresh=((BLOCKS, LOCAL, STATE), F32),
    leaving=((LOCAL, STATE), F32),
    padded=((GROUP + 8, MIX), F32),
    entering=((LOCAL, STATE), F32),
    local=((COUNT, LOCAL), F32),
    back=((COUNT, LOCAL), F32),
    gate=((COUNT, LOCAL), F32),
    ssd=((COUNT, LOCAL), F32),
    states=((BLOCKS, LOCAL, STATE), F32),
    sums=((8, COUNT), F32),
    sums_all=((8, COUNT), F32),
    sums_in=((4, 8, COUNT), F32),
    state=((LOCAL, STATE), F32),
    normal=((COUNT, LOCAL), BF16),
    dy=((COUNT, LOCAL), BF16),
    dgate=((COUNT, LOCAL), BF16),
    read=((BLOCKS, LOCAL, STATE), F32),
    returning=((LOCAL, STATE), F32),
    arriving=((LOCAL, STATE), F32),
    dgain=((8, LOCAL), F32),
    branch=((COUNT, D), BF16),
    dout_w=((SIDE, SIDE, ROWS, LOCAL), BF16),
    dgate_w=((SIDE, SIDE, ROWS, LOCAL), BF16),
    dcum=((COUNT, 128), F32),
    dstep=((COUNT, 128), F32),
    dstate=((COUNT, 2 * STATE), F32),
    skip=((8, 128), F32),
    skips=((8, LOCAL), F32),
    rows=((128, GROUP), F32),
    state_part=((COUNT, 2 * STATE), BF16),
    state_total=((COUNT, 2 * STATE), BF16),
    half_in=((HALF, 2 * STATE), BF16),
    chip_sum=((HALF, 2 * STATE), BF16),
    over_in=((HALF, 2 * STATE), BF16),
    values_in=((16, LOCAL), F32),
    slopes_in=((16, MIX), F32),
    state_in=((16, 2 * STATE), BF16),
    dstep_low=((COUNT, 128), BF16),
    head_rows=((8, 128), F32),
    part=((COUNT, D), BF16),
    dvalue_w=((SIDE, SIDE, ROWS, LOCAL), BF16),
    dstate_w=((SIDE, SIDE, ROWS, LOCAL), BF16),
    small=((24, LOCAL), F32),
    total=((D, 2 * LOCAL), F32),
    own=((4, ROWS, LOCAL), BF16),
    own_in=((4, ROWS, LOCAL), BF16),
    small_y=((SIDE, 24, LOCAL), F32),
    small_z=((SIDE, 24, LOCAL), F32),
    small_c=((24, LOCAL), F32),
    small_t=((SIDE, 8, LOCAL), F32),
    small_now=((3, 24, LOCAL), F32),
)
for name in ("gate", "out", "value", "state"):
    KEPT["held_" + name] = ((6, 2, ROWS, LOCAL), BF16)
    KEPT["passed_" + name] = ((2, 2, ROWS, LOCAL), BF16)
    KEPT["mid_" + name] = ((SIDE, ROWS, LOCAL), BF16)
    KEPT["second_" + name] = ((SIDE, ROWS, LOCAL), BF16)
for name in ("mixed", "normed"):
    KEPT["half_" + name] = ((2, COUNT // 4, D), BF16)
    KEPT["over_out_" + name] = ((COUNT // 4, D), BF16)
    KEPT["over_in_" + name] = ((COUNT // 4, D), BF16)
SLOTS = 116


def block_kernel(shard, edge, stream, up, conv, heads, gain, value_out, state_out, gate_out,
                 w_out_out, small_out, normed_out, mixed_out, gain_zero, *kept):
    by_name = dict(zip(KEPT, kept))
    m = types.SimpleNamespace(**by_name)
    send, recv, own_sem = kept[len(KEPT) :]
    z, y, along_y, along_z = place()
    ctx, tp = lax.axis_index("ctx"), lax.axis_index("tp")
    core, chip = lax.rem(tp, 2), lax.div(tp, 2)
    y_peers, z_peers, partner, tp_peers = all_peers(along_y, along_z)
    twin, across = {"tp": tp + 1 - 2 * core}, {"tp": tp + 2 - 4 * chip}
    beyond = {"ctx": 1 - ctx, "tp": tp + 1 - 2 * core}
    greet(y_peers + z_peers + [partner, beyond] + tp_peers)
    open_sends = []

    def to(source, target, slot, where):
        item = remote(source, target, send.at[slot], recv.at[slot], where)
        item.start()
        open_sends.append(item)
        return item

    full = Flat(m.full)
    at = tokens_spec(1)
    back_at = tokens_spec(1, True)
    cube, back_cube = cube_spec(1, 1), cube_spec(1, 1, True)
    row, back_row = row_spec(8), row_spec(8, True)

    def f(ref):
        return (ref, at)

    def r(ref):
        return (ref, back_at)

    def fc(ref):
        return (ref, cube)

    def rc(ref):
        return (ref, back_cube)

    gathers = [
        Gather(shard, m.full, LOCAL * index, index % 2 == 0, send, recv, 9 * index)
        for index in range(4)
    ]
    halo = to(edge, m.edge_in, 36, partner)
    keep = pltpu.make_async_copy(shard, m.full.at[z, y], own_sem)
    keep.start()
    keep.wait()
    gathers[0].turn()
    gathers[1].turn()
    gathers[0].relay()
    gathers[1].relay()
    gathers[2].turn()
    gathers[3].turn()
    gathers[0].finish()
    gathers[1].finish()
    halo.wait_recv()
    project = [
        [ctx], (stream, at), m.edge_in, full, conv, heads, f(m.normed), f(m.pre), f(m.slope),
        f(m.vals), f(m.step_val), f(m.sig), f(m.cum), fc(m.cum_t), fc(m.step_t), fc(m.fresh),
        m.leaving, gain_zero, m.padded,
    ]
    sweep(project_kernel, project, 0, 2)
    gathers[2].relay()
    gathers[3].relay()
    sweep(project_kernel, project, 2, 4)
    entering = to(m.leaving, m.entering, 37, partner)
    gathers[2].finish()
    gathers[3].finish()
    sweep(
        inside_kernel,
        [
            f(m.vals), f(m.cum), fc(m.cum_t), fc(m.step_t), heads, (up, at), f(m.normed), full,
            f(m.local), f(m.back), f(m.gate),
        ],
    )
    entering.wait_recv()
    m.state[...] = m.entering[...] * jnp.where(ctx == 1, 1.0, 0.0)
    sweep(
        output_kernel,
        [
            f(m.vals), f(m.local), f(m.gate), fc(m.fresh), f(m.cum), m.state, f(m.back), gain,
            f(m.ssd), fc(m.states), (m.sums, row), m.state,
        ],
    )
    to_tp = spread(m.sums, m.sums_in, tp, tp_peers, send, recv, 38)
    m.sums_all[...] = fold(m.sums_in, tp, m.sums[...], to_tp)
    open_sends.extend(to_tp)
    sweep(
        gates_kernel,
        [
            r(m.ssd), r(m.gate), r(m.back), (m.sums_all, back_row), gain, r(m.vals), r(m.cum),
            full, r(m.normal), r(m.dy), r(m.dgate), rc(m.read), m.returning, m.dgain,
            r(m.branch),
        ],
    )
    arriving = to(m.returning, m.arriving, 41, partner)
    mixed = PairSum(
        m.branch, mixed_out, m.half_mixed, m.over_out_mixed, m.over_in_mixed,
        send, recv, 42,
    )
    m.dout_w[...] = gridded(dot(up[...], m.normal[...], 0, 0))
    m.dgate_w[...] = gridded(dot(m.normed[...], m.dgate[...], 0, 0))
    mixed.cross()

    def weight_sum(name, z_first, slot):
        scratch = [by_name[kind + name] for kind in ("held_", "passed_", "mid_", "second_")]
        return WeightSum(by_name["d" + name + "_w"], z_first, scratch, send, recv, slot)

    gate_sum, out_sum = weight_sum("gate", True, 48), weight_sum("out", False, 57)
    blocks = [
        f(m.dy), f(m.vals), f(m.cum), fc(m.cum_t), f(m.step_val), fc(m.step_t), fc(m.states), heads,
        f(m.local), f(m.dcum), f(m.dstep), f(m.dstate), m.skip, m.skips, m.rows,
    ]
    sweep(blocks_kernel, blocks, 0, 2)
    gate_sum.ring.relay()
    out_sum.ring.relay()
    sweep(blocks_kernel, blocks, 2, 4)
    mixed.close(stream)
    gate_sum.turn()
    out_sum.turn()
    arriving.wait_recv()
    m.state[...] = m.arriving[...] * jnp.where(ctx == 0, 1.0, 0.0)
    sweep(
        states_kernel,
        [
            r(m.vals), r(m.cum), r(m.step_val), r(m.sig), rc(m.states), rc(m.read), m.state,
            heads, r(m.local), r(m.dcum), r(m.dstep), r(m.dstate), r(m.ssd), r(m.state_part),
            r(m.dstep_low), m.head_rows, m.state,
        ],
    )
    mine = pl.ds(pl.multiple_of(core * HALF, HALF), HALF)
    theirs = pl.ds(pl.multiple_of((1 - core) * HALF, HALF), HALF)
    to_twin = to(m.state_part.at[theirs], m.half_in, 66, twin)
    early = [
        to(m.ssd.at[0:16], m.values_in, 67, partner),
        to(m.slope.at[0:16], m.slopes_in, 68, partner),
    ]
    to_twin.wait_recv()
    m.chip_sum[...] = (
        m.state_part[mine].astype(F32) + m.half_in[...].astype(F32)
    ).astype(BF16)
    over = to(m.chip_sum, m.over_in, 69, across)
    m.own[0] = gate_sum.total().astype(BF16)
    m.own[1] = out_sum.total().astype(BF16)
    mixed.relay()
    over.wait_recv()
    total = m.state_total
    total[mine] = (m.chip_sum[...].astype(F32) + m.over_in[...].astype(F32)).astype(BF16)
    back = to(total.at[mine], total.at[mine], 70, twin)
    head = total.at[0:16]
    late = remote(head, m.state_in, send.at[71], recv.at[71], partner)
    late_twin = remote(head, m.state_in, send.at[72], recv.at[71], beyond)

    @pl.when(core == 0)
    def _():
        late.start()
        late_twin.start()

    pair = to(m.own.at[0:2], m.own_in.at[0:2], 73, partner)
    back.wait_recv()
    late.wait_recv()
    for item in early:
        item.wait_recv()
    sweep(
        weights_kernel,
        [
            [ctx, tp], r(m.ssd), r(m.state_total), r(m.slope), r(m.pre), r(m.dgate),
            r(m.dstep_low), r(m.normed), (stream, back_at), full, gain_zero, conv, m.values_in,
            m.state_in, m.slopes_in, m.dgain, m.head_rows, m.skip, r(m.part),
            m.dvalue_w, m.dstate_w, m.small, m.padded, m.total,
        ],
    )
    normed = PairSum(
        m.part, normed_out, m.half_normed, m.over_out_normed, m.over_in_normed,
        send, recv, 74,
    )
    value_sum, state_sum = weight_sum("value", True, 80), weight_sum("state", False, 89)
    small_now, small_z, small_y = m.small_now, m.small_z, m.small_y
    to_y = spread(m.small, small_y, y, y_peers, send, recv, 98)
    normed.cross()
    value_sum.ring.relay()
    state_sum.ring.relay()
    small_now[0] = fold(small_y, y, m.small[...], to_y)
    to_z = spread(small_now.at[0], small_z, z, z_peers, send, recv, 101)
    value_sum.turn()
    state_sum.turn()
    small_now[1] = fold(small_z, z, small_now[0], to_z)
    to_ctx = to(small_now.at[1], m.small_c, 104, partner)
    normed.close()
    m.own[2] = value_sum.total().astype(BF16)
    m.own[3] = state_sum.total().astype(BF16)
    pair_late = to(m.own.at[2:4], m.own_in.at[2:4], 105, partner)
    to_ctx.wait_recv()
    small_now[2] = small_now[1] + m.small_c[...]
    to_all = spread(small_now.at[2, pl.ds(16, 8)], m.small_t, tp, tp_peers, send, recv, 106)
    normed.relay()
    pair.wait_recv()
    gate_out[...] = m.own[0].astype(F32) + m.own_in[0].astype(F32)
    w_out_out[...] = m.own[1].astype(F32) + m.own_in[1].astype(F32)
    pair_late.wait_recv()
    value_out[...] = m.own[2].astype(F32) + m.own_in[2].astype(F32)
    state_out[...] = m.own[3].astype(F32) + m.own_in[3].astype(F32)
    small_out[0:16] = small_now[2, 0:16]
    small_out[16:24] = fold(m.small_t, tp, small_now[2, 16:24], to_all)
    normed.finish()
    mixed.finish()
    for item in gathers:
        item.close()
    for item in (gate_sum, out_sum, value_sum, state_sum):
        item.finish()

    @pl.when(core == 0)
    def _():
        late.wait_send()
        late_twin.wait_send()

    for item in open_sends + to_y + to_z + to_all:
        item.wait_send()


def per_device(
    stream,
    norm_gain,
    w_gate,
    w_value,
    w_step,
    w_state,
    w_out,
    conv_value,
    conv_value_bias,
    conv_state,
    conv_state_bias,
    step_bias,
    decay_log,
    skip_gain,
    inner_gain,
    cotangent,
):
    count = stream.shape[1]
    heads_here = step_bias.shape[0]
    rows, up = stream[0], cotangent[0]
    shard = jnp.concatenate(
        [
            w_value,
            w_state,
            w_step,
            norm_gain[:, None],
            jnp.zeros((ROWS, 128 - heads_here - 1), BF16),
            w_gate,
            w_out.T,
        ],
        axis=1,
    )
    edge = rows[count - 16 :]
    conv = jnp.concatenate(
        [
            jnp.concatenate([conv_value, conv_value_bias[None]], axis=0),
            jnp.concatenate([conv_state, conv_state_bias[None]], axis=0),
        ],
        axis=1,
    )
    conv = jnp.pad(conv, ((0, 3), (0, 0)))
    heads = jnp.pad(
        jnp.stack([step_bias, decay_log, skip_gain]), ((0, 5), (0, 128 - heads_here))
    )
    gain_one = inner_gain[None]
    owned = jax.ShapeDtypeStruct((ROWS, LOCAL), F32)
    wide = jax.ShapeDtypeStruct((COUNT, D), BF16)
    own_value, own_state, own_gate, own_out, totals, dnormed, mixed, gain_zero = pl.pallas_call(
        block_kernel,
        in_specs=[VM] * 7,
        out_specs=(VM,) * 8,
        out_shape=(
            owned,
            owned,
            owned,
            owned,
            jax.ShapeDtypeStruct((24, LOCAL), F32),
            wide,
            wide,
            jax.ShapeDtypeStruct((8, D), F32),
        ),
        scratch_shapes=[
            *[pltpu.VMEM(shape, dtype) for shape, dtype in KEPT.values()],
            DMA((SLOTS,)),
            DMA((SLOTS,)),
            DMA,
        ],
        compiler_params=params(1, 56),
    )(shard, edge, rows, up, conv, heads, gain_one)
    d_stream, mixed, value_w, state_w, step_w, gate_w, taps, state_taps = finish(
        dnormed, rows, up, gain_zero, mixed, own_value, own_state, own_gate, totals, heads_here
    )
    gain_total = totals[16:18].reshape(D)
    return (
        mixed[None],
        d_stream[None],
        lax.dynamic_slice_in_dim(gain_total, lax.axis_index("dp") * ROWS, ROWS),
        gate_w,
        value_w,
        step_w,
        state_w,
        own_out.T,
        taps,
        totals[4],
        state_taps,
        totals[10, : 2 * STATE],
        totals[11, :heads_here],
        totals[12, :heads_here],
        totals[13, :heads_here],
        totals[5],
    )


def solution(mesh):
    in_specs = (
        P("dp", "ctx", None),
        P("dp"),
        P("dp", "tp"),
        P("dp", "tp"),
        P("dp", "tp"),
        P("dp", None),
        P("tp", "dp"),
        P(None, "tp"),
        P("tp"),
        P(),
        P(),
        P("tp"),
        P("tp"),
        P("tp"),
        P("tp"),
        P("dp", "ctx", None),
    )
    out_specs = (
        P("dp", "ctx", None),
        P("dp", "ctx", None),
        P("dp"),
        P("dp", "tp"),
        P("dp", "tp"),
        P("dp", "tp"),
        P("dp", None),
        P("tp", "dp"),
        P(None, "tp"),
        P("tp"),
        P(),
        P(),
        P("tp"),
        P("tp"),
        P("tp"),
        P("tp"),
    )
    return jax.shard_map(
        per_device, mesh=mesh, in_specs=in_specs, out_specs=out_specs, check_vma=False
    )
```

```python
import types

import jax
import jax.numpy as jnp
from jax import lax
from jax.experimental import pallas as pl
from jax.experimental.pallas import tpu as pltpu
from jax.sharding import PartitionSpec as P

D = 768
HEAD = 64
STATE = 128
CONV = 4
GROUP = 256
INNER = 1536


EPS = 1e-05
HIGH = lax.Precision.HIGHEST


MESH = pl.DeviceIdType.MESH
VM = pl.BlockSpec(memory_space=pltpu.VMEM)
SIDE = 4
ROWS = 48
WIDE = 1536
LOCAL = 384
DMA = pltpu.SemaphoreType.DMA
F32 = jnp.float32
BF16 = jnp.bfloat16


def params(ident, limit=20):
    return pltpu.CompilerParams(
        collective_id=ident, has_side_effects=True, vmem_limit_bytes=limit * 1024 * 1024
    )


def remote(source, target, send, recv, where):
    return pltpu.make_async_remote_copy(
        src_ref=source,
        dst_ref=target,
        send_sem=send,
        recv_sem=recv,
        device_id=where,
        device_id_type=MESH,
    )


def greet(peers):
    barrier = pltpu.get_barrier_semaphore()
    for where in peers:
        pl.semaphore_signal(barrier, inc=1, device_id=where, device_id_type=MESH)
    pl.semaphore_wait(barrier, len(peers))


def place():
    me = lax.axis_index("dp")
    z, y = lax.div(me, SIDE), lax.rem(me, SIDE)

    def along_y(hop):
        return {"dp": z * SIDE + lax.rem(y + hop, SIDE)}

    def along_z(hop):
        return {"dp": lax.rem(z + hop, SIDE) * SIDE + y}

    return z, y, along_y, along_z


def ahead(position, hop):
    return lax.rem(position + hop, SIDE)


class Gather:
    def __init__(self, shard, full, first, y_first, send, recv, slot):
        z, y, along_y, along_z = place()
        columns = pl.ds(first, LOCAL)
        self.send, self.recv, self.slot = send, recv, slot
        if y_first:
            self.position, self.along, near = z, along_z, along_y
            self.block = lambda at, sub: full.at[at, pl.ds(2 * sub, 2), :, columns]
        else:
            self.position, self.along, near = y, along_y, along_z
            self.block = lambda at, sub: full.at[pl.ds(2 * sub, 2), at, :, columns]
        self.near = [
            remote(
                shard.at[:, columns],
                full.at[z, y, :, columns],
                send.at[slot + hop],
                recv.at[slot + hop],
                near(hop + 1),
            )
            for hop in range(3)
        ]
        for item in self.near:
            item.start()

    def copy(self, position, sub, slot, hop):
        item = remote(
            self.block(position, sub),
            self.block(position, sub),
            self.send.at[self.slot + slot],
            self.recv.at[self.slot + slot],
            self.along(hop),
        )
        item.start()
        return item

    def turn(self):
        for item in self.near:
            item.wait_recv()
        self.direct = [
            self.copy(self.position, 0, 3, 1),
            self.copy(self.position, 1, 4, 3),
            self.copy(self.position, 1, 5, 1),
            self.copy(self.position, 0, 6, 3),
        ]

    def relay(self):
        self.direct[0].wait_recv()
        one = self.copy(ahead(self.position, 3), 0, 7, 1)
        self.direct[1].wait_recv()
        two = self.copy(ahead(self.position, 1), 1, 8, 3)
        self.relayed = [one, two]

    def finish(self):
        for item in self.direct[2:] + self.relayed:
            item.wait_recv()

    def close(self):
        for item in self.near + self.direct + self.relayed:
            item.wait_send()


class RingScatter:
    def __init__(self, block, load, held, passed, position, along, send, recv, first):
        self.block, self.load, self.held, self.passed = block, load, held, passed
        self.position, self.along = position, along
        self.send, self.recv, self.first = send, recv, first
        far, right, left = ahead(position, 2), ahead(position, 1), ahead(position, 3)
        self.direct = [
            self.copy(block(far, 0), 0, 1),
            self.copy(block(far, 1), 1, 3),
            self.copy(block(right, 1), 2, 1),
            self.copy(block(left, 0), 3, 3),
        ]
        for item in self.direct:
            item.start()

    def copy(self, source, slot, hop):
        return remote(
            source,
            self.held.at[slot],
            self.send.at[self.first + slot],
            self.recv.at[self.first + slot],
            self.along(hop),
        )

    def relay(self):
        right, left = ahead(self.position, 1), ahead(self.position, 3)
        self.direct[0].wait_recv()
        self.passed[0] = (self.held[0].astype(F32) + self.load(right, 0).astype(F32)).astype(BF16)
        one = self.copy(self.passed.at[0], 4, 1)
        one.start()
        self.direct[1].wait_recv()
        self.passed[1] = (self.held[1].astype(F32) + self.load(left, 1).astype(F32)).astype(BF16)
        two = self.copy(self.passed.at[1], 5, 3)
        two.start()
        self.relayed = [one, two]

    def total(self, sub):
        own = self.load(self.position, sub).astype(F32)
        if sub == 0:
            self.direct[3].wait_recv()
            self.relayed[0].wait_recv()
            return own + self.held[3].astype(F32) + self.held[4].astype(F32)
        self.direct[2].wait_recv()
        self.relayed[1].wait_recv()
        return own + self.held[2].astype(F32) + self.held[5].astype(F32)

    def finish(self):
        for item in self.direct + self.relayed:
            item.wait_send()


class PairSum:
    def __init__(self, part, out, half_in, over_out, over_in, send, recv, first):
        self.part, self.out = part, out
        self.half_in, self.over_out, self.over_in = half_in, over_out, over_in
        self.send, self.recv, self.first = send, recv, first
        me = lax.axis_index("tp")
        core, chip = lax.rem(me, 2), lax.div(me, 2)
        self.twin, self.across = {"tp": me + 1 - 2 * core}, {"tp": me + 2 - 4 * chip}
        size = part.shape[0] // 4

        def quarter(c, h):
            return pl.ds(pl.multiple_of((2 * c + h) * size, size), size)

        self.keep, self.give = quarter(core, chip), quarter(core, 1 - chip)
        self.sends = [
            self.copy(part.at[quarter(1 - core, 1 - chip)], half_in.at[0], 0, self.twin),
            self.copy(part.at[quarter(1 - core, chip)], half_in.at[1], 1, self.twin),
        ]

    def copy(self, source, target, slot, where):
        item = remote(
            source, target, self.send.at[self.first + slot], self.recv.at[self.first + slot], where
        )
        item.start()
        return item

    def cross(self):
        self.sends[0].wait_recv()
        self.over_out[...] = (
            self.part[self.give].astype(F32) + self.half_in[0].astype(F32)
        ).astype(BF16)
        self.sends.append(self.copy(self.over_out, self.over_in, 2, self.across))

    def close(self, base=None):
        self.sends[1].wait_recv()
        self.sends[2].wait_recv()
        total = self.part[self.keep].astype(F32) + self.half_in[1].astype(F32)
        total = total + self.over_in[...].astype(F32)
        if base is not None:
            total = total + base[self.keep].astype(F32)
        self.out[self.keep] = total.astype(BF16)
        mine = self.out.at[self.keep]
        self.sends.append(self.copy(mine, mine, 3, self.across))
        self.sends.append(self.copy(mine, mine, 4, self.twin))

    def relay(self):
        self.sends[3].wait_recv()
        other = self.out.at[self.give]
        self.sends.append(self.copy(other, other, 5, self.twin))

    def finish(self):
        self.sends[4].wait_recv()
        self.sends[5].wait_recv()
        for item in self.sends:
            item.wait_send()


def pair_scratch(rows, columns):
    return [
        pltpu.VMEM((2, rows // 4, columns), BF16),
        pltpu.VMEM((rows // 4, columns), BF16),
        pltpu.VMEM((rows // 4, columns), BF16),
    ]


def all_peers(along_y, along_z):
    me, partner = lax.axis_index("tp"), {"ctx": 1 - lax.axis_index("ctx")}
    hops = range(1, SIDE)
    tp_peers = [{"tp": ahead(me, hop)} for hop in hops]
    return [along_y(hop) for hop in hops], [along_z(hop) for hop in hops], partner, tp_peers


def spread(source, held, own, peers, send, recv, first):
    copies = [
        remote(source, held.at[own], send.at[first + hop], recv.at[first + hop], peer)
        for hop, peer in enumerate(peers)
    ]
    for item in copies:
        item.start()
    return copies


def fold(held, own, value, copies):
    held[own] = value
    for item in copies:
        item.wait_recv()
    return (held[0] + held[1]) + (held[2] + held[3])


class WeightSum:
    def __init__(self, grads, z_first, scratch, send, recv, first):
        self.held, self.passed, self.mid, self.second = scratch
        z, y, along_y, along_z = place()
        self.grads, self.send, self.recv, self.first = grads, send, recv, first
        if z_first:
            block = lambda at, sub: grads.at[at, pl.ds(2 * sub, 2)]
            load = lambda at, sub: grads[at, pl.ds(2 * sub, 2)]
            self.later, self.along = y, along_y
            self.ring = RingScatter(block, load, self.held, self.passed, z, along_z, send, recv, first)
        else:
            block = lambda at, sub: grads.at[pl.ds(2 * sub, 2), at]
            load = lambda at, sub: grads[pl.ds(2 * sub, 2), at]
            self.later, self.along = z, along_z
            self.ring = RingScatter(block, load, self.held, self.passed, y, along_y, send, recv, first)

    def turn(self):
        for sub in range(2):
            self.mid[2 * sub : 2 * sub + 2] = self.ring.total(sub).astype(BF16)
        self.copies = []
        for hop in range(1, SIDE):
            slot = self.first + 5 + hop
            item = remote(
                self.mid.at[ahead(self.later, hop)],
                self.second.at[self.later],
                self.send.at[slot],
                self.recv.at[slot],
                self.along(hop),
            )
            item.start()
            self.copies.append(item)

    def total(self):
        self.second[self.later] = self.mid[self.later]
        for item in self.copies:
            item.wait_recv()
        held = [self.second[index].astype(F32) for index in range(SIDE)]
        return (held[0] + held[1]) + (held[2] + held[3])

    def finish(self):
        self.ring.finish()
        for item in self.copies:
            item.wait_send()


def weight_scratch():
    return [
        pltpu.VMEM((6, 2, ROWS, LOCAL), BF16),
        pltpu.VMEM((2, 2, ROWS, LOCAL), BF16),
        pltpu.VMEM((SIDE, ROWS, LOCAL), BF16),
        pltpu.VMEM((SIDE, ROWS, LOCAL), BF16),
    ]


BLOCKS = 4
LIMIT = 20
MIX = LOCAL + 2 * STATE
THIN = MIX + 128
PROJ = THIN + LOCAL
PAIRS = 3


def dot(left, right, left_dim=1, right_dim=0, precision=None):
    return lax.dot_general(
        left,
        right,
        (((left_dim,), (right_dim,)), ((), ())),
        preferred_element_type=F32,
        precision=precision,
    )


def lanes(rows, columns=128):
    return lax.broadcasted_iota(jnp.int32, (rows, columns), 1)


def expand(per_head):
    first = lanes(per_head.shape[0]) < HEAD
    return jnp.concatenate(
        [
            jnp.where(first, per_head[:, 2 * j : 2 * j + 1], per_head[:, 2 * j + 1 : 2 * j + 2])
            for j in range(PAIRS)
        ],
        axis=1,
    )


def head_sums(wide):
    lane = lanes(wide.shape[0])
    total = jnp.zeros(lane.shape, F32)
    for j in range(PAIRS):
        pair = wide[:, 128 * j : 128 * j + 128]
        even = jnp.sum(jnp.where(lane < HEAD, pair, 0.0), axis=1, keepdims=True)
        odd = jnp.sum(jnp.where(lane < HEAD, 0.0, pair), axis=1, keepdims=True)
        total = jnp.where(lane == 2 * j, even, jnp.where(lane == 2 * j + 1, odd, total))
    return total


def by_head(row, states):
    return jnp.concatenate(
        [row[:, h : h + 1] * states[HEAD * h : HEAD * h + HEAD] for h in range(2 * PAIRS)], axis=0
    )


def lower():
    shape = (GROUP, GROUP)
    return lax.broadcasted_iota(jnp.int32, shape, 0) >= lax.broadcasted_iota(jnp.int32, shape, 1)


def decay_of(cum, cum_t, h, mask):
    return jnp.exp(jnp.where(mask, cum[:, h : h + 1] - cum_t[h : h + 1], -1e30))


def project_kernel(step, ctx, stream, edge, full, conv, heads, normed_o, pre_o, slope_o, vals_o,
                   step_o, sig_o, cum_o, cum_t_o, step_t_o, fresh_o, state_o, gain_o, padded):

    def normalise(rows):
        scale = lax.rsqrt(jnp.mean(rows * rows, axis=-1, keepdims=True) + EPS)
        return (rows * scale * gain_o[0:1]).astype(BF16)

    @pl.when(step == 0)
    def _():
        gain_o[...] = jnp.broadcast_to(full[:, MIX:THIN].astype(F32).T[6:7], gain_o.shape)
        rows = dot(normalise(edge[...].astype(F32)), full[:, :MIX])
        rows = rows * jnp.where(ctx[0] == 1, 1.0, 0.0)
        padded[0:8] = rows[8:16].astype(BF16).astype(F32)
        state_o[...] = jnp.zeros_like(state_o)

    @pl.when(step > 0)
    def _():
        padded[0:8] = padded[GROUP : GROUP + 8]

    normed = normalise(stream[...].astype(F32))
    normed_o[...] = normed
    projected = dot(normed, full[:, :THIN])
    pre = projected[:, :MIX].astype(BF16)
    pre_o[...] = pre
    padded[8:] = pre.astype(F32)
    conv_sum = conv[4:5] + sum(conv[k : k + 1] * padded[5 + k : 5 + k + GROUP] for k in range(CONV))
    sig = jax.nn.sigmoid(conv_sum)
    slope_o[...] = sig * (1.0 + conv_sum * (1.0 - sig))
    vals = (conv_sum * sig).astype(BF16)
    vals_o[...] = vals
    live = lanes(GROUP) < 2 * PAIRS
    raw = jnp.where(live, projected[:, MIX:THIN] + heads[0:1], 0.0)
    sig_o[...] = jnp.where(live, jax.nn.sigmoid(raw), 0.0)
    step_val = jnp.maximum(raw, 0.0) + jnp.log1p(jnp.exp(-jnp.abs(raw)))
    step_val = jnp.where(live, step_val, 0.0)
    step_o[...] = step_val
    log_rate = -jnp.exp(heads[1:2]) * step_val
    cum = dot(lower().astype(F32), log_rate, precision=HIGH)
    cum_o[...] = cum
    cum_t_o[0] = cum.T[0:8]
    step_t_o[0] = step_val.T[0:8]
    last = cum[GROUP - 1 :]
    scales = step_val * jnp.exp(last - cum)
    weighted = (vals[:, :LOCAL].astype(F32) * expand(scales)).astype(BF16)
    fresh = dot(weighted, vals[:, LOCAL : LOCAL + STATE], 0, 0)
    fresh_o[0] = fresh
    state_o[...] = by_head(jnp.exp(last), state_o[...]) + fresh


def inside_kernel(step, vals, cum, cum_t, step_t, heads, up, normed, full, local_o, back_o, gate_o):
    gate_o[...] = dot(normed[...], full[:, THIN:PROJ])
    back_o[...] = dot(up[...], full[:, PROJ:])
    keys, reads = vals[:, LOCAL : LOCAL + STATE], vals[:, LOCAL + STATE :]
    inner = dot(reads, keys, 1, 1)
    mask, first = lower(), lanes(GROUP) < HEAD
    skip = expand(heads[2:3])
    for j in range(PAIRS):
        here = slice(128 * j, 128 * j + 128)
        pair = vals[:, here]
        outs = []
        for h in (2 * j, 2 * j + 1):
            weights = inner * decay_of(cum, cum_t[0], h, mask) * step_t[0, h : h + 1]
            outs.append(dot(weights.astype(BF16), pair))
        local_o[:, here] = jnp.where(first, outs[0], outs[1]) + skip[:, here] * pair.astype(F32)


def sum_row(wide):
    folded = wide[:, :128] + wide[:, 128:256] + wide[:, 256:]
    return jnp.sum(folded.T, axis=0, keepdims=True)


def output_kernel(step, vals, local, gate, fresh, cum, entering, back, gain, ssd_o, states_o, sums_o,
                  state):
    @pl.when(step == 0)
    def _():
        state[...] = entering[...]

    here = state[...]
    states_o[0] = here
    state[...] = by_head(jnp.exp(cum[GROUP - 1 :]), here) + fresh[0]
    carried = dot(vals[:, LOCAL + STATE :], here.astype(BF16), 1, 1)
    ssd = local[...] + expand(jnp.exp(cum[...])) * carried
    ssd_o[...] = ssd
    gated = ssd * (gate[...] * jax.nn.sigmoid(gate[...]))
    sums_o[0:1] = sum_row(gated * gated)
    sums_o[1:2] = sum_row(back[...] * gain[...] * gated)
    sums_o[2:8] = jnp.zeros((6, GROUP), F32)


def gates_kernel(step, ssd, gate, back, sums, gain, vals, cum, full, normal_o, dy_o, dgate_o, read_o,
                 chain_o, dgain_o, branch_o):
    @pl.when(step == 0)
    def _():
        chain_o[...] = jnp.zeros_like(chain_o)
        dgain_o[...] = jnp.zeros_like(dgain_o)

    both = sums[...].T
    scale = lax.rsqrt(both[:, 0:1] / INNER + EPS)
    gate_val, ssd_val = gate[...], ssd[...]
    sig = jax.nn.sigmoid(gate_val)
    act = gate_val * sig
    gated = ssd_val * act
    normal = (gated * scale * gain[...]).astype(BF16)
    normal_o[...] = normal
    branch_o[...] = dot(normal, full[:, PROJ:], 1, 1).astype(BF16)
    grad_normal = back[...]
    dgain_o[0:1] += jnp.sum(grad_normal * gated * scale, axis=0, keepdims=True)
    dgated = scale * (grad_normal * gain[...]) - gated * (scale * scale * scale) * (
        both[:, 1:2] / INNER
    )
    dy = (dgated * act).astype(BF16)
    dy_o[...] = dy
    dgate_o[...] = (dgated * ssd_val * (sig * (1.0 + gate_val * (1.0 - sig)))).astype(BF16)
    carried = (dy.astype(F32) * expand(jnp.exp(cum[...]))).astype(BF16)
    read = dot(carried, vals[:, LOCAL + STATE :], 0, 0)
    read_o[0] = read
    chain_o[...] = by_head(jnp.exp(cum[GROUP - 1 :]), chain_o[...]) + read


def split_dot(wide, low, left_dim):
    high = wide.astype(BF16)
    rest = (wide - high.astype(F32)).astype(BF16)
    return dot(high, low, left_dim) + dot(rest, low, left_dim)


def blocks_kernel(step, dy, vals, cum, cum_t, step_val, step_t, states, heads, dval_o, dcum_o, dstep_o,
                  dstate_o, skip_o, skips, rows):

    @pl.when(step == 0)
    def _():
        skips[...] = jnp.zeros_like(skips)
        rows[...] = jnp.zeros_like(rows)

    dy_f, values_f = dy[...].astype(F32), vals[:, :LOCAL].astype(F32)
    skips[0:1] += jnp.sum(dy_f * values_f, axis=0, keepdims=True)
    keys, reads = vals[:, LOCAL : LOCAL + STATE], vals[:, LOCAL + STATE :]
    inner = dot(reads, keys, 1, 1)
    mask, lane = lower(), lanes(GROUP)
    first = lane < HEAD
    skip = expand(heads[2:3])
    dinner = jnp.zeros((GROUP, GROUP), F32)
    dcum = jnp.zeros((GROUP, 128), F32)
    for j in range(PAIRS):
        here = slice(128 * j, 128 * j + 128)
        pair, dy_pair = values_f[:, here], dy[:, here]
        outs = []
        for h in (2 * j, 2 * j + 1):
            own = jnp.where(first if h % 2 == 0 else ~first, pair, 0.0).astype(BF16)
            decays = decay_of(cum, cum_t[0], h, mask)
            scaled = dot(dy_pair, own, 1, 1) * decays
            step_row = step_t[0, h : h + 1]
            product = scaled * inner
            rows[h : h + 1] = jnp.sum(product, axis=0, keepdims=True)
            dcum = jnp.where(
                lane == h, jnp.sum(product * step_row, axis=1, keepdims=True), dcum
            )
            dinner = dinner + scaled * step_row
            outs.append(dot((inner * decays * step_row).astype(BF16), dy_pair, 0, 0))
        dval_o[:, here] = jnp.where(first, outs[0], outs[1]) + skip[:, here] * dy_f[:, here]
    dstep = rows[...].T
    dstep_o[...] = dstep
    low = states[0].astype(BF16)
    grad_exp = dy_f * expand(jnp.exp(cum[...]))
    dcum_o[...] = dcum - dstep * step_val[...] + head_sums(grad_exp * dot(reads, low, 1, 1))
    dstate_o[:, :STATE] = split_dot(dinner, reads, 0)
    dstate_o[:, STATE:] = dot(grad_exp.astype(BF16), low) + split_dot(dinner, keys, 1)

    @pl.when(step == BLOCKS - 1)
    def _():
        skip_o[...] = head_sums(skips[...])


def states_kernel(step, vals, cum, step_val, sig, states, read, arriving, heads, dval, dcum, dstep, dstate,
                  dval_o, state_o, low_o, heads_o, carry):
    @pl.when(step == 0)
    def _():
        carry[...] = arriving[...]
        heads_o[...] = jnp.zeros_like(heads_o)

    out = carry[...]
    last = cum[GROUP - 1 :]
    decay = jnp.exp(last)
    carry[...] = by_head(decay, out) + read[0]
    product = out * states[0]
    row = lanes(1)
    dlast = jnp.zeros((1, 128), F32)
    for h in range(2 * PAIRS):
        own = jnp.sum(product[HEAD * h : HEAD * h + HEAD], axis=0, keepdims=True)
        dlast = jnp.where(row == h, jnp.sum(own, axis=1, keepdims=True), dlast)
    dlast = dlast * decay
    fresh = out.astype(BF16)
    keys = vals[:, LOCAL : LOCAL + STATE]
    values_f = vals[:, :LOCAL].astype(F32)
    to_end = jnp.exp(last - cum[...])
    scales = step_val[...] * to_end
    wide = expand(scales)
    dweighted = dot(keys, fresh, 1, 1)
    dval_o[...] = dval[...] + dweighted * wide
    state_o[:, :STATE] = (
        dstate[:, :STATE] + dot((values_f * wide).astype(BF16), fresh)
    ).astype(BF16)
    state_o[:, STATE:] = dstate[:, STATE:].astype(BF16)
    dscales = head_sums(dweighted * values_f)
    spill = dscales * scales
    dlast = dlast + jnp.sum(spill, axis=0, keepdims=True)
    at_end = lax.broadcasted_iota(jnp.int32, (GROUP, 128), 0) == GROUP - 1
    full_cum = dcum[...] - spill + jnp.where(at_end, dlast, 0.0)
    drate = dot(lower().astype(F32), full_cum, 0, 0, precision=HIGH)
    rate = jnp.exp(heads[1:2])
    total_step = dstep[...] + dscales * to_end - rate * drate
    pre = total_step * sig[...]
    low_o[...] = pre.astype(BF16)
    heads_o[0:1] += jnp.sum(pre, axis=0, keepdims=True)
    heads_o[1:2] += -rate * jnp.sum(drate * step_val[...], axis=0, keepdims=True)


def next_rows(block, extra):
    keep = lax.broadcasted_iota(jnp.int32, block.shape, 0) < CONV - 1
    return jnp.where(keep, block * extra, 0.0)


def value_kernel(step, where, dval, slope, pre, dgate, dstep, normed, full, conv, values_next,
                 slope_next, part_o, dvalue_o, small_o, padded, total):
    @pl.when(step == 0)
    def _():
        small_o[...] = jnp.zeros_like(small_o)
        own = values_next[0:8] * slope_next[0:8, :LOCAL]
        padded[GROUP:, :LOCAL] = next_rows(own, jnp.where(where[0] == 0, 1.0, 0.0))
        total[...] = jnp.zeros_like(total)

    @pl.when(step > 0)
    def _():
        padded[GROUP:, :LOCAL] = padded[0:8, :LOCAL]

    grad = dval[...] * slope[:, :LOCAL]
    padded[0:GROUP, :LOCAL] = grad
    pre_f = pre[:, :LOCAL].astype(F32)
    dinput = jnp.zeros((GROUP, LOCAL), F32)
    for k in range(CONV):
        moved = padded[CONV - 1 - k : CONV - 1 - k + GROUP, :LOCAL]
        dinput = dinput + conv[k : k + 1, :LOCAL] * moved
        small_o[k : k + 1] += jnp.sum(moved * pre_f, axis=0, keepdims=True)
    small_o[4:5] += jnp.sum(grad, axis=0, keepdims=True)
    low = dinput.astype(BF16)
    total[...] += dot(normed[...], jnp.concatenate([low, dstep[...]], axis=1), 0, 0)
    part_o[...] = dot(low, full[:, :LOCAL], 1, 1) + dot(
        jnp.concatenate([dstep[...], dgate[...]], axis=1), full[:, MIX:PROJ], 1, 1
    )

    @pl.when(step == BLOCKS - 1)
    def _():
        dvalue_o[...] = gridded(total[:, :LOCAL])


def maps_kernel(step, where, state, slope, pre, normed, stream, full, conv, state_next, slope_next,
                dgain, heads, skip, part_in, part_o, dstate_o, small_o, padded, total, thin):
    block = BLOCKS - 1 - step

    @pl.when(step == 0)
    def _():
        own = state_next[...].astype(F32)[0:8] * slope_next[0:8, LOCAL:]
        padded[GROUP:, LOCAL:] = next_rows(own, jnp.where(where[0] == 0, 1.0, 0.0))
        total[...] = jnp.zeros_like(total)

    @pl.when(step > 0)
    def _():
        padded[GROUP:, LOCAL:] = padded[0:8, LOCAL:]

    grad = state[...].astype(F32) * slope[:, LOCAL:]
    padded[0:GROUP, LOCAL:] = grad
    pre_f = pre[:, LOCAL:].astype(F32)
    dinput = jnp.zeros((GROUP, 2 * STATE), F32)
    for k in range(CONV):
        moved = padded[CONV - 1 - k : CONV - 1 - k + GROUP, LOCAL:]
        dinput = dinput + conv[k : k + 1, LOCAL:] * moved
        small_o[6 + k : 7 + k, : 2 * STATE] += jnp.sum(moved * pre_f, axis=0, keepdims=True)
    small_o[10:11, : 2 * STATE] += jnp.sum(grad, axis=0, keepdims=True)
    total[...] += dot(normed[...], dinput.astype(BF16), 0, 0)
    once = (dinput * jnp.where(where[1] == block, 1.0, 0.0)).astype(BF16)
    part = part_in[...] + dot(once, full[:, LOCAL:MIX], 1, 1)
    part_o[...] = part.astype(BF16)
    source = stream[...].astype(F32)
    scale = lax.rsqrt(jnp.mean(source * source, axis=-1, keepdims=True) + EPS)
    dnorm = jnp.sum(part * source * scale, axis=0, keepdims=True)
    small_o[16:17] += dnorm[:, :LOCAL]
    small_o[17:18] += dnorm[:, LOCAL:]

    @pl.when(block == 0)
    def _():
        small_o[5:6] = dgain[0:1]
        small_o[11:12, :128] = heads[0:1]
        small_o[12:13, :128] = heads[1:2]
        small_o[13:14, :128] = skip[0:1]
        dstate_o[...] = gridded(jnp.concatenate([total[...], thin[:, LOCAL:]], axis=1))


def last_kernel(normed, stream, up, gain, branch, value, state, gate, small,
                out, mixed, value_o, state_o, step_o, gate_o, taps_o, state_taps_o):
    step = pl.program_id(0)
    source, grad = stream[...].astype(F32), normed[...].astype(F32)
    scale = lax.rsqrt(jnp.mean(source * source, axis=-1, keepdims=True) + EPS)
    scaled = grad * gain[0:1]
    inner = jnp.sum(scaled * source, axis=1, keepdims=True) / D
    out[...] = up[...].astype(F32) + (
        scale * scaled - source * (scale * scale * scale) * inner
    )

    mixed[...] = branch[...]

    @pl.when(step == 0)
    def _():
        value_o[...] = value[...]
        gate_o[...] = gate[...]
        state_o[...] = state[:, : 2 * STATE]
        step_o[...] = state[:, 2 * STATE : 2 * STATE + step_o.shape[1]]
        taps_o[...] = small[0:4]
        state_taps_o[...] = small[6:10, : 2 * STATE]


def finish(normed, stream, up, gain, branch, value, state, gate, small, heads_here):
    by_block = pl.BlockSpec((GROUP, D), lambda g: (g, 0))

    def all_of(*shape):
        return pl.BlockSpec(shape, lambda g: (0, 0))

    owned = (ROWS, LOCAL)
    small_shapes = [
        owned, (ROWS, 2 * STATE), (ROWS, heads_here), owned, (CONV, LOCAL), (CONV, 2 * STATE)
    ]
    return pl.pallas_call(
        last_kernel,
        grid=(BLOCKS,),
        in_specs=[
            by_block,
            by_block,
            by_block,
            all_of(8, D),
            by_block,
            all_of(*owned),
            all_of(*owned),
            all_of(*owned),
            all_of(24, LOCAL),
        ],
        out_specs=(by_block, by_block, *[all_of(*shape) for shape in small_shapes]),
        out_shape=(
            jax.ShapeDtypeStruct(stream.shape, F32),
            jax.ShapeDtypeStruct(stream.shape, BF16),
            *[jax.ShapeDtypeStruct(shape, F32) for shape in small_shapes],
        ),
        compiler_params=pltpu.CompilerParams(vmem_limit_bytes=60 * 1024 * 1024),
    )(normed, stream, up, gain, branch, value, state, gate, small)


def place_of(step, backward):
    return (BLOCKS - 1 - step) if backward else step


def tokens_spec(columns, backward=False):
    def view(ref, step):
        start = pl.multiple_of(place_of(step, backward) * GROUP, GROUP)
        return ref.at[pl.ds(start, GROUP)]

    return view


def cube_spec(rows, columns, backward=False):
    return lambda ref, step: ref.at[pl.ds(place_of(step, backward), 1)]


def row_spec(rows, backward=False):
    def view(ref, step):
        start = pl.multiple_of(place_of(step, backward) * GROUP, GROUP)
        return ref.at[:, pl.ds(start, GROUP)]

    return view


def whole(*shape):
    return lambda ref, step: ref


class Flat:
    def __init__(self, ref):
        self.ref = ref

    def __getitem__(self, key):
        found = self.ref[:, :, :, key[1]]
        return found.reshape(D, found.shape[-1])


def gridded(total):
    return total.astype(BF16).reshape(SIDE, SIDE, ROWS, total.shape[-1])


def sweep(kernel, pairs, start=0, stop=BLOCKS):
    def step(index, carry):
        kernel(index, *[item[1](item[0], index) if type(item) is tuple else item for item in pairs])
        return carry

    lax.fori_loop(start, stop, step, 0)


COUNT = BLOCKS * GROUP
HALF = COUNT // 2
KEPT = dict(
    full=((SIDE, SIDE, ROWS, WIDE), BF16),
    edge_in=((16, D), BF16),
    conv=((8, MIX), F32),
    heads=((8, 128), F32),
    gain=((1, LOCAL), F32),
    normed=((COUNT, D), BF16),
    pre=((COUNT, MIX), BF16),
    slope=((COUNT, MIX), F32),
    vals=((COUNT, MIX), BF16),
    step_val=((COUNT, 128), F32),
    sig=((COUNT, 128), F32),
    cum=((COUNT, 128), F32),
    cum_t=((BLOCKS, 8, GROUP), F32),
    step_t=((BLOCKS, 8, GROUP), F32),
    fresh=((BLOCKS, LOCAL, STATE), F32),
    leaving=((LOCAL, STATE), F32),
    padded=((GROUP + 8, MIX), F32),
    entering=((LOCAL, STATE), F32),
    local=((COUNT, LOCAL), F32),
    back=((COUNT, LOCAL), F32),
    gate=((COUNT, LOCAL), F32),
    ssd=((COUNT, LOCAL), F32),
    states=((BLOCKS, LOCAL, STATE), F32),
    sums=((8, COUNT), F32),
    sums_all=((8, COUNT), F32),
    sums_in=((4, 8, COUNT), F32),
    state=((LOCAL, STATE), F32),
    normal=((COUNT, LOCAL), BF16),
    dy=((COUNT, LOCAL), BF16),
    dgate=((COUNT, LOCAL), BF16),
    read=((BLOCKS, LOCAL, STATE), F32),
    returning=((LOCAL, STATE), F32),
    arriving=((LOCAL, STATE), F32),
    dgain=((8, LOCAL), F32),
    branch=((COUNT, D), BF16),
    dout_w=((SIDE, SIDE, ROWS, LOCAL), BF16),
    dgate_w=((SIDE, SIDE, ROWS, LOCAL), BF16),
    dcum=((COUNT, 128), F32),
    dstep=((COUNT, 128), F32),
    dstate=((COUNT, 2 * STATE), F32),
    skip=((8, 128), F32),
    skips=((8, LOCAL), F32),
    rows=((128, GROUP), F32),
    state_part=((COUNT, 2 * STATE), BF16),
    state_total=((COUNT, 2 * STATE), BF16),
    half_in=((HALF, 2 * STATE), BF16),
    chip_sum=((HALF, 2 * STATE), BF16),
    over_in=((HALF, 2 * STATE), BF16),
    values_in=((16, LOCAL), F32),
    slopes_in=((16, MIX), F32),
    state_in=((16, 2 * STATE), BF16),
    dstep_low=((COUNT, 128), BF16),
    head_rows=((8, 128), F32),
    part=((COUNT, D), BF16),
    dvalue_w=((SIDE, SIDE, ROWS, LOCAL), BF16),
    dstate_w=((SIDE, SIDE, ROWS, LOCAL), BF16),
    small=((24, LOCAL), F32),
    total=((D, LOCAL + 128), F32),
    total_maps=((D, 2 * STATE), F32),
    part_sum=((COUNT, D), F32),
    own=((4, ROWS, LOCAL), BF16),
    own_in=((4, ROWS, LOCAL), BF16),
    small_y=((SIDE, 24, LOCAL), F32),
    small_z=((SIDE, 24, LOCAL), F32),
    small_c=((24, LOCAL), F32),
    small_t=((SIDE, 8, LOCAL), F32),
    small_now=((3, 24, LOCAL), F32),
)
for name in ("gate", "out", "value", "state"):
    KEPT["held_" + name] = ((6, 2, ROWS, LOCAL), BF16)
    KEPT["passed_" + name] = ((2, 2, ROWS, LOCAL), BF16)
    KEPT["mid_" + name] = ((SIDE, ROWS, LOCAL), BF16)
    KEPT["second_" + name] = ((SIDE, ROWS, LOCAL), BF16)
for name in ("mixed", "normed"):
    KEPT["half_" + name] = ((2, COUNT // 4, D), BF16)
    KEPT["over_out_" + name] = ((COUNT // 4, D), BF16)
    KEPT["over_in_" + name] = ((COUNT // 4, D), BF16)
SLOTS = 116


def block_kernel(shard, stream, up, taps_value, taps_state, singles, value_out, state_out, gate_out,
                 w_out_out, small_out, normed_out, mixed_out, gain_zero, *kept):
    by_name = dict(zip(KEPT, kept))
    m = types.SimpleNamespace(**by_name)
    send, recv, own_sem = kept[len(KEPT) :]
    z, y, along_y, along_z = place()
    ctx, tp = lax.axis_index("ctx"), lax.axis_index("tp")
    core, chip = lax.rem(tp, 2), lax.div(tp, 2)
    y_peers, z_peers, partner, tp_peers = all_peers(along_y, along_z)
    twin, across = {"tp": tp + 1 - 2 * core}, {"tp": tp + 2 - 4 * chip}
    beyond = {"ctx": 1 - ctx, "tp": tp + 1 - 2 * core}
    greet(y_peers + z_peers + [partner, beyond] + tp_peers)
    open_sends = []
    conv, heads, gain = m.conv, m.heads, m.gain
    conv[0:4, :LOCAL] = taps_value[...]
    conv[0:4, LOCAL:] = taps_state[...]
    conv[4:5] = singles[:, :MIX]
    gain[...] = singles[:, MIX : MIX + LOCAL]
    for index in range(3):
        first = MIX + LOCAL + 128 * index
        heads[index : index + 1] = singles[:, first : first + 128]

    def to(source, target, slot, where):
        item = remote(source, target, send.at[slot], recv.at[slot], where)
        item.start()
        open_sends.append(item)
        return item

    full = Flat(m.full)
    at = tokens_spec(1)
    back_at = tokens_spec(1, True)
    cube, back_cube = cube_spec(1, 1), cube_spec(1, 1, True)
    row, back_row = row_spec(8), row_spec(8, True)

    def f(ref):
        return (ref, at)

    def r(ref):
        return (ref, back_at)

    def fc(ref):
        return (ref, cube)

    def rc(ref):
        return (ref, back_cube)

    gathers = [
        Gather(shard, m.full, LOCAL * index, index % 2 == 0, send, recv, 9 * index)
        for index in range(4)
    ]
    halo = to(stream.at[pl.ds(COUNT - 16, 16)], m.edge_in, 36, partner)
    keep = pltpu.make_async_copy(shard, m.full.at[z, y], own_sem)
    keep.start()
    keep.wait()
    gathers[0].turn()
    gathers[1].turn()
    gathers[0].relay()
    gathers[1].relay()
    gathers[2].turn()
    gathers[3].turn()
    gathers[0].finish()
    gathers[1].finish()
    halo.wait_recv()
    project = [
        [ctx], (stream, at), m.edge_in, full, conv, heads, f(m.normed), f(m.pre), f(m.slope),
        f(m.vals), f(m.step_val), f(m.sig), f(m.cum), fc(m.cum_t), fc(m.step_t), fc(m.fresh),
        m.leaving, gain_zero, m.padded,
    ]
    sweep(project_kernel, project, 0, 2)
    gathers[2].relay()
    gathers[3].relay()
    sweep(project_kernel, project, 2, 4)
    entering = to(m.leaving, m.entering, 37, partner)
    gathers[2].finish()
    gathers[3].finish()
    sweep(
        inside_kernel,
        [
            f(m.vals), f(m.cum), fc(m.cum_t), fc(m.step_t), heads, (up, at), f(m.normed), full,
            f(m.local), f(m.back), f(m.gate),
        ],
    )
    entering.wait_recv()
    m.state[...] = m.entering[...] * jnp.where(ctx == 1, 1.0, 0.0)
    sweep(
        output_kernel,
        [
            f(m.vals), f(m.local), f(m.gate), fc(m.fresh), f(m.cum), m.state, f(m.back), gain,
            f(m.ssd), fc(m.states), (m.sums, row), m.state,
        ],
    )
    to_tp = spread(m.sums, m.sums_in, tp, tp_peers, send, recv, 38)
    m.sums_all[...] = fold(m.sums_in, tp, m.sums[...], to_tp)
    open_sends.extend(to_tp)
    sweep(
        gates_kernel,
        [
            r(m.ssd), r(m.gate), r(m.back), (m.sums_all, back_row), gain, r(m.vals), r(m.cum),
            full, r(m.normal), r(m.dy), r(m.dgate), rc(m.read), m.returning, m.dgain,
            r(m.branch),
        ],
    )
    arriving = to(m.returning, m.arriving, 41, partner)
    mixed = PairSum(
        m.branch, mixed_out, m.half_mixed, m.over_out_mixed, m.over_in_mixed,
        send, recv, 42,
    )
    m.dout_w[...] = gridded(dot(up[...], m.normal[...], 0, 0))
    m.dgate_w[...] = gridded(dot(m.normed[...], m.dgate[...], 0, 0))
    mixed.cross()

    def weight_sum(name, z_first, slot):
        scratch = [by_name[kind + name] for kind in ("held_", "passed_", "mid_", "second_")]
        return WeightSum(by_name["d" + name + "_w"], z_first, scratch, send, recv, slot)

    gate_sum, out_sum = weight_sum("gate", True, 48), weight_sum("out", False, 57)
    blocks = [
        f(m.dy), f(m.vals), f(m.cum), fc(m.cum_t), f(m.step_val), fc(m.step_t), fc(m.states), heads,
        f(m.local), f(m.dcum), f(m.dstep), f(m.dstate), m.skip, m.skips, m.rows,
    ]
    sweep(blocks_kernel, blocks, 0, 2)
    gate_sum.ring.relay()
    out_sum.ring.relay()
    sweep(blocks_kernel, blocks, 2, 4)
    mixed.close(stream)
    gate_sum.turn()
    out_sum.turn()
    arriving.wait_recv()
    m.state[...] = m.arriving[...] * jnp.where(ctx == 0, 1.0, 0.0)
    sweep(
        states_kernel,
        [
            r(m.vals), r(m.cum), r(m.step_val), r(m.sig), rc(m.states), rc(m.read), m.state,
            heads, r(m.local), r(m.dcum), r(m.dstep), r(m.dstate), r(m.ssd), r(m.state_part),
            r(m.dstep_low), m.head_rows, m.state,
        ],
    )
    mine = pl.ds(pl.multiple_of(core * HALF, HALF), HALF)
    theirs = pl.ds(pl.multiple_of((1 - core) * HALF, HALF), HALF)
    to_twin = to(m.state_part.at[theirs], m.half_in, 66, twin)
    early = [
        to(m.ssd.at[0:16], m.values_in, 67, partner),
        to(m.slope.at[0:16], m.slopes_in, 68, partner),
    ]
    to_twin.wait_recv()
    m.chip_sum[...] = (
        m.state_part[mine].astype(F32) + m.half_in[...].astype(F32)
    ).astype(BF16)
    over = to(m.chip_sum, m.over_in, 69, across)
    m.own[0] = gate_sum.total().astype(BF16)
    m.own[1] = out_sum.total().astype(BF16)
    mixed.relay()
    for item in early:
        item.wait_recv()
    values = [
        [ctx], r(m.ssd), r(m.slope), r(m.pre), r(m.dgate), r(m.dstep_low), r(m.normed), full, conv,
        m.values_in, m.slopes_in, r(m.part_sum), m.dvalue_w, m.small, m.padded, m.total,
    ]
    sweep(value_kernel, values, 0, 3)
    over.wait_recv()
    total = m.state_total
    total[mine] = (m.chip_sum[...].astype(F32) + m.over_in[...].astype(F32)).astype(BF16)
    back = to(total.at[mine], total.at[mine], 70, twin)
    head = total.at[0:16]
    late = remote(head, m.state_in, send.at[71], recv.at[71], partner)
    late_twin = remote(head, m.state_in, send.at[72], recv.at[71], beyond)

    @pl.when(core == 0)
    def _():
        late.start()
        late_twin.start()

    pair = to(m.own.at[0:2], m.own_in.at[0:2], 73, partner)
    sweep(value_kernel, values, 3, 4)
    value_sum = weight_sum("value", True, 80)
    back.wait_recv()
    late.wait_recv()
    sweep(
        maps_kernel,
        [
            [ctx, tp], r(m.state_total), r(m.slope), r(m.pre), r(m.normed), (stream, back_at), full,
            conv, m.state_in, m.slopes_in, m.dgain, m.head_rows, m.skip, r(m.part_sum), r(m.part),
            m.dstate_w, m.small, m.padded, m.total_maps, m.total,
        ],
    )
    normed = PairSum(
        m.part, normed_out, m.half_normed, m.over_out_normed, m.over_in_normed,
        send, recv, 74,
    )
    state_sum = weight_sum("state", False, 89)
    small_now, small_z, small_y = m.small_now, m.small_z, m.small_y
    to_y = spread(m.small, small_y, y, y_peers, send, recv, 98)
    normed.cross()
    value_sum.ring.relay()
    state_sum.ring.relay()
    small_now[0] = fold(small_y, y, m.small[...], to_y)
    to_z = spread(small_now.at[0], small_z, z, z_peers, send, recv, 101)
    value_sum.turn()
    state_sum.turn()
    small_now[1] = fold(small_z, z, small_now[0], to_z)
    to_ctx = to(small_now.at[1], m.small_c, 104, partner)
    normed.close()
    m.own[2] = value_sum.total().astype(BF16)
    m.own[3] = state_sum.total().astype(BF16)
    pair_late = to(m.own.at[2:4], m.own_in.at[2:4], 105, partner)
    to_ctx.wait_recv()
    small_now[2] = small_now[1] + m.small_c[...]
    to_all = spread(small_now.at[2, pl.ds(16, 8)], m.small_t, tp, tp_peers, send, recv, 106)
    normed.relay()
    pair.wait_recv()
    gate_out[...] = m.own[0].astype(F32) + m.own_in[0].astype(F32)
    w_out_out[...] = m.own[1].astype(F32) + m.own_in[1].astype(F32)
    pair_late.wait_recv()
    value_out[...] = m.own[2].astype(F32) + m.own_in[2].astype(F32)
    state_out[...] = m.own[3].astype(F32) + m.own_in[3].astype(F32)
    small_out[0:16] = small_now[2, 0:16]
    small_out[16:24] = fold(m.small_t, tp, small_now[2, 16:24], to_all)
    normed.finish()
    mixed.finish()
    for item in gathers:
        item.close()
    for item in (gate_sum, out_sum, value_sum, state_sum):
        item.finish()

    @pl.when(core == 0)
    def _():
        late.wait_send()
        late_twin.wait_send()

    for item in open_sends + to_y + to_z + to_all:
        item.wait_send()


def per_device(
    stream,
    norm_gain,
    w_gate,
    w_value,
    w_step,
    w_state,
    w_out,
    conv_value,
    conv_value_bias,
    conv_state,
    conv_state_bias,
    step_bias,
    decay_log,
    skip_gain,
    inner_gain,
    cotangent,
):
    count = stream.shape[1]
    heads_here = step_bias.shape[0]
    rows, up = stream[0], cotangent[0]
    shard = jnp.concatenate(
        [
            w_value,
            w_state,
            w_step,
            norm_gain[:, None],
            jnp.zeros((ROWS, 128 - heads_here - 1), BF16),
            w_gate,
            w_out.T,
        ],
        axis=1,
    )
    spare = jnp.zeros((128 - heads_here,), F32)
    singles = jnp.concatenate(
        [
            conv_value_bias, conv_state_bias, inner_gain, step_bias, spare, decay_log, spare,
            skip_gain, spare,
        ]
    )[None]
    taps_value, taps_state = conv_value, conv_state
    owned = jax.ShapeDtypeStruct((ROWS, LOCAL), F32)
    wide = jax.ShapeDtypeStruct((COUNT, D), BF16)
    own_value, own_state, own_gate, own_out, totals, dnormed, mixed, gain_zero = pl.pallas_call(
        block_kernel,
        in_specs=[VM] * 6,
        out_specs=(VM,) * 8,
        out_shape=(
            owned,
            owned,
            owned,
            owned,
            jax.ShapeDtypeStruct((24, LOCAL), F32),
            wide,
            wide,
            jax.ShapeDtypeStruct((8, D), F32),
        ),
        scratch_shapes=[
            *[pltpu.VMEM(shape, dtype) for shape, dtype in KEPT.values()],
            DMA((SLOTS,)),
            DMA((SLOTS,)),
            DMA,
        ],
        compiler_params=params(1, 56),
    )(shard, rows, up, taps_value, taps_state, singles)
    d_stream, mixed, value_w, state_w, step_w, gate_w, taps, state_taps = finish(
        dnormed, rows, up, gain_zero, mixed, own_value, own_state, own_gate, totals, heads_here
    )
    gain_total = totals[16:18].reshape(D)
    return (
        mixed[None],
        d_stream[None],
        lax.dynamic_slice_in_dim(gain_total, lax.axis_index("dp") * ROWS, ROWS),
        gate_w,
        value_w,
        step_w,
        state_w,
        own_out.T,
        taps,
        totals[4],
        state_taps,
        totals[10, : 2 * STATE],
        totals[11, :heads_here],
        totals[12, :heads_here],
        totals[13, :heads_here],
        totals[5],
    )


def solution(mesh):
    in_specs = (
        P("dp", "ctx", None),
        P("dp"),
        P("dp", "tp"),
        P("dp", "tp"),
        P("dp", "tp"),
        P("dp", None),
        P("tp", "dp"),
        P(None, "tp"),
        P("tp"),
        P(),
        P(),
        P("tp"),
        P("tp"),
        P("tp"),
        P("tp"),
        P("dp", "ctx", None),
    )
    out_specs = (
        P("dp", "ctx", None),
        P("dp", "ctx", None),
        P("dp"),
        P("dp", "tp"),
        P("dp", "tp"),
        P("dp", "tp"),
        P("dp", None),
        P("tp", "dp"),
        P(None, "tp"),
        P("tp"),
        P(),
        P(),
        P("tp"),
        P("tp"),
        P("tp"),
        P("tp"),
    )
    return jax.shard_map(
        per_device, mesh=mesh, in_specs=in_specs, out_specs=out_specs, check_vma=False
    )
```

```python
import types

import jax
import jax.numpy as jnp
from jax import lax
from jax.experimental import pallas as pl
from jax.experimental.pallas import tpu as pltpu
from jax.sharding import PartitionSpec as P

D = 768
HEAD = 64
STATE = 128
CONV = 4
GROUP = 256
INNER = 1536


EPS = 1e-05
HIGH = lax.Precision.HIGHEST


MESH = pl.DeviceIdType.MESH
VM = pl.BlockSpec(memory_space=pltpu.VMEM)
SIDE = 4
ROWS = 48
WIDE = 1536
LOCAL = 384
DMA = pltpu.SemaphoreType.DMA
F32 = jnp.float32
BF16 = jnp.bfloat16


def params(ident, limit=20):
    return pltpu.CompilerParams(
        collective_id=ident, has_side_effects=True, vmem_limit_bytes=limit * 1024 * 1024
    )


def remote(source, target, send, recv, where):
    return pltpu.make_async_remote_copy(
        src_ref=source,
        dst_ref=target,
        send_sem=send,
        recv_sem=recv,
        device_id=where,
        device_id_type=MESH,
    )


def greet(peers):
    barrier = pltpu.get_barrier_semaphore()
    for where in peers:
        pl.semaphore_signal(barrier, inc=1, device_id=where, device_id_type=MESH)
    pl.semaphore_wait(barrier, len(peers))


def place():
    me = lax.axis_index("dp")
    z, y = lax.div(me, SIDE), lax.rem(me, SIDE)

    def along_y(hop):
        return {"dp": z * SIDE + lax.rem(y + hop, SIDE)}

    def along_z(hop):
        return {"dp": lax.rem(z + hop, SIDE) * SIDE + y}

    return z, y, along_y, along_z


def ahead(position, hop):
    return lax.rem(position + hop, SIDE)


class Gather:
    def __init__(self, shard, full, first, y_first, send, recv, slot):
        z, y, along_y, along_z = place()
        columns = pl.ds(first, LOCAL)
        self.send, self.recv, self.slot = send, recv, slot
        if y_first:
            self.position, self.along, near = z, along_z, along_y
            self.block = lambda at, sub: full.at[at, pl.ds(2 * sub, 2), :, columns]
        else:
            self.position, self.along, near = y, along_y, along_z
            self.block = lambda at, sub: full.at[pl.ds(2 * sub, 2), at, :, columns]
        self.near = [
            remote(
                shard.at[:, columns],
                full.at[z, y, :, columns],
                send.at[slot + hop],
                recv.at[slot + hop],
                near(hop + 1),
            )
            for hop in range(3)
        ]
        for item in self.near:
            item.start()

    def copy(self, position, sub, slot, hop):
        item = remote(
            self.block(position, sub),
            self.block(position, sub),
            self.send.at[self.slot + slot],
            self.recv.at[self.slot + slot],
            self.along(hop),
        )
        item.start()
        return item

    def turn(self):
        for item in self.near:
            item.wait_recv()
        self.direct = [
            self.copy(self.position, 0, 3, 1),
            self.copy(self.position, 1, 4, 3),
            self.copy(self.position, 1, 5, 1),
            self.copy(self.position, 0, 6, 3),
        ]

    def relay(self):
        self.direct[0].wait_recv()
        one = self.copy(ahead(self.position, 3), 0, 7, 1)
        self.direct[1].wait_recv()
        two = self.copy(ahead(self.position, 1), 1, 8, 3)
        self.relayed = [one, two]

    def finish(self):
        for item in self.direct[2:] + self.relayed:
            item.wait_recv()

    def close(self):
        for item in self.near + self.direct + self.relayed:
            item.wait_send()


class RingScatter:
    def __init__(self, block, load, held, passed, position, along, send, recv, first):
        self.block, self.load, self.held, self.passed = block, load, held, passed
        self.position, self.along = position, along
        self.send, self.recv, self.first = send, recv, first
        far, right, left = ahead(position, 2), ahead(position, 1), ahead(position, 3)
        self.direct = [
            self.copy(block(far, 0), 0, 1),
            self.copy(block(far, 1), 1, 3),
            self.copy(block(right, 1), 2, 1),
            self.copy(block(left, 0), 3, 3),
        ]
        for item in self.direct:
            item.start()

    def copy(self, source, slot, hop):
        return remote(
            source,
            self.held.at[slot],
            self.send.at[self.first + slot],
            self.recv.at[self.first + slot],
            self.along(hop),
        )

    def relay(self):
        right, left = ahead(self.position, 1), ahead(self.position, 3)
        self.direct[0].wait_recv()
        self.passed[0] = (self.held[0].astype(F32) + self.load(right, 0).astype(F32)).astype(BF16)
        one = self.copy(self.passed.at[0], 4, 1)
        one.start()
        self.direct[1].wait_recv()
        self.passed[1] = (self.held[1].astype(F32) + self.load(left, 1).astype(F32)).astype(BF16)
        two = self.copy(self.passed.at[1], 5, 3)
        two.start()
        self.relayed = [one, two]

    def total(self, sub):
        own = self.load(self.position, sub).astype(F32)
        if sub == 0:
            self.direct[3].wait_recv()
            self.relayed[0].wait_recv()
            return own + self.held[3].astype(F32) + self.held[4].astype(F32)
        self.direct[2].wait_recv()
        self.relayed[1].wait_recv()
        return own + self.held[2].astype(F32) + self.held[5].astype(F32)

    def finish(self):
        for item in self.direct + self.relayed:
            item.wait_send()


class PairSum:
    def __init__(self, part, out, half_in, over_out, over_in, send, recv, first):
        self.part, self.out = part, out
        self.half_in, self.over_out, self.over_in = half_in, over_out, over_in
        self.send, self.recv, self.first = send, recv, first
        me = lax.axis_index("tp")
        core, chip = lax.rem(me, 2), lax.div(me, 2)
        self.twin, self.across = {"tp": me + 1 - 2 * core}, {"tp": me + 2 - 4 * chip}
        size = part.shape[0] // 4

        def quarter(c, h):
            return pl.ds(pl.multiple_of((2 * c + h) * size, size), size)

        self.keep, self.give = quarter(core, chip), quarter(core, 1 - chip)
        self.sends = [
            self.copy(part.at[quarter(1 - core, 1 - chip)], half_in.at[0], 0, self.twin),
            self.copy(part.at[quarter(1 - core, chip)], half_in.at[1], 1, self.twin),
        ]

    def copy(self, source, target, slot, where):
        item = remote(
            source, target, self.send.at[self.first + slot], self.recv.at[self.first + slot], where
        )
        item.start()
        return item

    def cross(self):
        self.sends[0].wait_recv()
        self.over_out[...] = (
            self.part[self.give].astype(F32) + self.half_in[0].astype(F32)
        ).astype(BF16)
        self.sends.append(self.copy(self.over_out, self.over_in, 2, self.across))

    def close(self, base=None):
        self.sends[1].wait_recv()
        self.sends[2].wait_recv()
        total = self.part[self.keep].astype(F32) + self.half_in[1].astype(F32)
        total = total + self.over_in[...].astype(F32)
        if base is not None:
            total = total + base[self.keep].astype(F32)
        self.out[self.keep] = total.astype(BF16)
        mine = self.out.at[self.keep]
        self.sends.append(self.copy(mine, mine, 3, self.across))
        self.sends.append(self.copy(mine, mine, 4, self.twin))

    def relay(self):
        self.sends[3].wait_recv()
        other = self.out.at[self.give]
        self.sends.append(self.copy(other, other, 5, self.twin))

    def finish(self):
        self.sends[4].wait_recv()
        self.sends[5].wait_recv()
        for item in self.sends:
            item.wait_send()


def pair_scratch(rows, columns):
    return [
        pltpu.VMEM((2, rows // 4, columns), BF16),
        pltpu.VMEM((rows // 4, columns), BF16),
        pltpu.VMEM((rows // 4, columns), BF16),
    ]


def all_peers(along_y, along_z):
    me, partner = lax.axis_index("tp"), {"ctx": 1 - lax.axis_index("ctx")}
    hops = range(1, SIDE)
    tp_peers = [{"tp": ahead(me, hop)} for hop in hops]
    return [along_y(hop) for hop in hops], [along_z(hop) for hop in hops], partner, tp_peers


def spread(source, held, own, peers, send, recv, first):
    copies = [
        remote(source, held.at[own], send.at[first + hop], recv.at[first + hop], peer)
        for hop, peer in enumerate(peers)
    ]
    for item in copies:
        item.start()
    return copies


def fold(held, own, value, copies):
    held[own] = value
    for item in copies:
        item.wait_recv()
    return (held[0] + held[1]) + (held[2] + held[3])


class WeightSum:
    def __init__(self, grads, z_first, scratch, send, recv, first):
        self.held, self.passed, self.mid, self.second = scratch
        z, y, along_y, along_z = place()
        self.grads, self.send, self.recv, self.first = grads, send, recv, first
        if z_first:
            block = lambda at, sub: grads.at[at, pl.ds(2 * sub, 2)]
            load = lambda at, sub: grads[at, pl.ds(2 * sub, 2)]
            self.later, self.along = y, along_y
            self.ring = RingScatter(block, load, self.held, self.passed, z, along_z, send, recv, first)
        else:
            block = lambda at, sub: grads.at[pl.ds(2 * sub, 2), at]
            load = lambda at, sub: grads[pl.ds(2 * sub, 2), at]
            self.later, self.along = z, along_z
            self.ring = RingScatter(block, load, self.held, self.passed, y, along_y, send, recv, first)

    def turn(self):
        for sub in range(2):
            self.mid[2 * sub : 2 * sub + 2] = self.ring.total(sub).astype(BF16)
        self.copies = []
        for hop in range(1, SIDE):
            slot = self.first + 5 + hop
            item = remote(
                self.mid.at[ahead(self.later, hop)],
                self.second.at[self.later],
                self.send.at[slot],
                self.recv.at[slot],
                self.along(hop),
            )
            item.start()
            self.copies.append(item)

    def total(self):
        self.second[self.later] = self.mid[self.later]
        for item in self.copies:
            item.wait_recv()
        held = [self.second[index].astype(F32) for index in range(SIDE)]
        return (held[0] + held[1]) + (held[2] + held[3])

    def finish(self):
        self.ring.finish()
        for item in self.copies:
            item.wait_send()


def weight_scratch():
    return [
        pltpu.VMEM((6, 2, ROWS, LOCAL), BF16),
        pltpu.VMEM((2, 2, ROWS, LOCAL), BF16),
        pltpu.VMEM((SIDE, ROWS, LOCAL), BF16),
        pltpu.VMEM((SIDE, ROWS, LOCAL), BF16),
    ]


BLOCKS = 4
LIMIT = 20
MIX = LOCAL + 2 * STATE
THIN = MIX + 128
PROJ = THIN + LOCAL
PAIRS = 3


def dot(left, right, left_dim=1, right_dim=0, precision=None):
    return lax.dot_general(
        left,
        right,
        (((left_dim,), (right_dim,)), ((), ())),
        preferred_element_type=F32,
        precision=precision,
    )


def lanes(rows, columns=128):
    return lax.broadcasted_iota(jnp.int32, (rows, columns), 1)


def expand(per_head):
    first = lanes(per_head.shape[0]) < HEAD
    return jnp.concatenate(
        [
            jnp.where(first, per_head[:, 2 * j : 2 * j + 1], per_head[:, 2 * j + 1 : 2 * j + 2])
            for j in range(PAIRS)
        ],
        axis=1,
    )


def head_sums(wide):
    lane = lanes(wide.shape[0])
    total = jnp.zeros(lane.shape, F32)
    for j in range(PAIRS):
        pair = wide[:, 128 * j : 128 * j + 128]
        even = jnp.sum(jnp.where(lane < HEAD, pair, 0.0), axis=1, keepdims=True)
        odd = jnp.sum(jnp.where(lane < HEAD, 0.0, pair), axis=1, keepdims=True)
        total = jnp.where(lane == 2 * j, even, jnp.where(lane == 2 * j + 1, odd, total))
    return total


def by_head(row, states):
    return jnp.concatenate(
        [row[:, h : h + 1] * states[HEAD * h : HEAD * h + HEAD] for h in range(2 * PAIRS)], axis=0
    )


def lower():
    shape = (GROUP, GROUP)
    return lax.broadcasted_iota(jnp.int32, shape, 0) >= lax.broadcasted_iota(jnp.int32, shape, 1)


def decay_of(cum, cum_t, h, mask):
    return jnp.exp(jnp.where(mask, cum[:, h : h + 1] - cum_t[h : h + 1], -1e30))


def project_kernel(step, ctx, stream, edge, full, conv, heads, normed_o, pre_o, slope_o, vals_o,
                   step_o, sig_o, cum_o, cum_t_o, step_t_o, fresh_o, state_o, gain_o, padded):

    def normalise(rows):
        scale = lax.rsqrt(jnp.mean(rows * rows, axis=-1, keepdims=True) + EPS)
        return (rows * scale * gain_o[0:1]).astype(BF16)

    @pl.when(step == 0)
    def _():
        gain_o[...] = jnp.broadcast_to(full[:, MIX:THIN].astype(F32).T[6:7], gain_o.shape)
        rows = dot(normalise(edge[...].astype(F32)), full[:, :MIX])
        rows = rows * jnp.where(ctx[0] == 1, 1.0, 0.0)
        padded[0:8] = rows[8:16].astype(BF16).astype(F32)
        state_o[...] = jnp.zeros_like(state_o)

    @pl.when(step > 0)
    def _():
        padded[0:8] = padded[GROUP : GROUP + 8]

    normed = normalise(stream[...].astype(F32))
    normed_o[...] = normed
    projected = dot(normed, full[:, :THIN])
    pre = projected[:, :MIX].astype(BF16)
    pre_o[...] = pre
    padded[8:] = pre.astype(F32)
    conv_sum = conv[4:5] + sum(conv[k : k + 1] * padded[5 + k : 5 + k + GROUP] for k in range(CONV))
    sig = jax.nn.sigmoid(conv_sum)
    slope_o[...] = sig * (1.0 + conv_sum * (1.0 - sig))
    vals = (conv_sum * sig).astype(BF16)
    vals_o[...] = vals
    live = lanes(GROUP) < 2 * PAIRS
    raw = jnp.where(live, projected[:, MIX:THIN] + heads[0:1], 0.0)
    sig_o[...] = jnp.where(live, jax.nn.sigmoid(raw), 0.0)
    step_val = jnp.maximum(raw, 0.0) + jnp.log1p(jnp.exp(-jnp.abs(raw)))
    step_val = jnp.where(live, step_val, 0.0)
    step_o[...] = step_val
    log_rate = -jnp.exp(heads[1:2]) * step_val
    cum = dot(lower().astype(F32), log_rate, precision=HIGH)
    cum_o[...] = cum
    cum_t_o[0] = cum.T[0:8]
    step_t_o[0] = step_val.T[0:8]
    last = cum[GROUP - 1 :]
    scales = step_val * jnp.exp(last - cum)
    weighted = (vals[:, :LOCAL].astype(F32) * expand(scales)).astype(BF16)
    fresh = dot(weighted, vals[:, LOCAL : LOCAL + STATE], 0, 0)
    fresh_o[0] = fresh
    state_o[...] = by_head(jnp.exp(last), state_o[...]) + fresh


def inside_kernel(step, vals, cum, cum_t, step_t, heads, up, normed, full, local_o, back_o, gate_o):
    gate_o[...] = dot(normed[...], full[:, THIN:PROJ])
    back_o[...] = dot(up[...], full[:, PROJ:])
    keys, reads = vals[:, LOCAL : LOCAL + STATE], vals[:, LOCAL + STATE :]
    inner = dot(reads, keys, 1, 1)
    mask, first = lower(), lanes(GROUP) < HEAD
    skip = expand(heads[2:3])
    for j in range(PAIRS):
        here = slice(128 * j, 128 * j + 128)
        pair = vals[:, here]
        outs = []
        for h in (2 * j, 2 * j + 1):
            weights = inner * decay_of(cum, cum_t[0], h, mask) * step_t[0, h : h + 1]
            outs.append(dot(weights.astype(BF16), pair))
        local_o[:, here] = jnp.where(first, outs[0], outs[1]) + skip[:, here] * pair.astype(F32)


def sum_row(wide):
    folded = wide[:, :128] + wide[:, 128:256] + wide[:, 256:]
    return jnp.sum(folded.T, axis=0, keepdims=True)


def output_kernel(step, vals, local, gate, fresh, cum, entering, back, gain, ssd_o, states_o, sums_o,
                  state):
    @pl.when(step == 0)
    def _():
        state[...] = entering[...]

    here = state[...]
    states_o[0] = here
    state[...] = by_head(jnp.exp(cum[GROUP - 1 :]), here) + fresh[0]
    carried = dot(vals[:, LOCAL + STATE :], here.astype(BF16), 1, 1)
    ssd = local[...] + expand(jnp.exp(cum[...])) * carried
    ssd_o[...] = ssd
    gated = ssd * (gate[...] * jax.nn.sigmoid(gate[...]))
    sums_o[0:1] = sum_row(gated * gated)
    sums_o[1:2] = sum_row(back[...] * gain[...] * gated)
    sums_o[2:8] = jnp.zeros((6, GROUP), F32)


def gates_kernel(step, ssd, gate, back, sums, gain, vals, cum, full, normal_o, dy_o, dgate_o, read_o,
                 chain_o, dgain_o, branch_o):
    @pl.when(step == 0)
    def _():
        chain_o[...] = jnp.zeros_like(chain_o)
        dgain_o[...] = jnp.zeros_like(dgain_o)

    both = sums[...].T
    scale = lax.rsqrt(both[:, 0:1] / INNER + EPS)
    gate_val, ssd_val = gate[...], ssd[...]
    sig = jax.nn.sigmoid(gate_val)
    act = gate_val * sig
    gated = ssd_val * act
    normal = (gated * scale * gain[...]).astype(BF16)
    normal_o[...] = normal
    branch_o[...] = dot(normal, full[:, PROJ:], 1, 1).astype(BF16)
    grad_normal = back[...]
    dgain_o[0:1] += jnp.sum(grad_normal * gated * scale, axis=0, keepdims=True)
    dgated = scale * (grad_normal * gain[...]) - gated * (scale * scale * scale) * (
        both[:, 1:2] / INNER
    )
    dy = (dgated * act).astype(BF16)
    dy_o[...] = dy
    dgate_o[...] = (dgated * ssd_val * (sig * (1.0 + gate_val * (1.0 - sig)))).astype(BF16)
    carried = (dy.astype(F32) * expand(jnp.exp(cum[...]))).astype(BF16)
    read = dot(carried, vals[:, LOCAL + STATE :], 0, 0)
    read_o[0] = read
    chain_o[...] = by_head(jnp.exp(cum[GROUP - 1 :]), chain_o[...]) + read


def split_dot(wide, low, left_dim):
    high = wide.astype(BF16)
    rest = (wide - high.astype(F32)).astype(BF16)
    return dot(high, low, left_dim) + dot(rest, low, left_dim)


def blocks_kernel(step, dy, vals, cum, cum_t, step_val, step_t, states, heads, dval_o, dcum_o, dstep_o,
                  dstate_o, skip_o, skips, rows):

    @pl.when(step == 0)
    def _():
        skips[...] = jnp.zeros_like(skips)
        rows[...] = jnp.zeros_like(rows)

    dy_f, values_f = dy[...].astype(F32), vals[:, :LOCAL].astype(F32)
    skips[0:1] += jnp.sum(dy_f * values_f, axis=0, keepdims=True)
    keys, reads = vals[:, LOCAL : LOCAL + STATE], vals[:, LOCAL + STATE :]
    inner = dot(reads, keys, 1, 1)
    mask, lane = lower(), lanes(GROUP)
    first = lane < HEAD
    skip = expand(heads[2:3])
    dinner = jnp.zeros((GROUP, GROUP), F32)
    dcum = jnp.zeros((GROUP, 128), F32)
    for j in range(PAIRS):
        here = slice(128 * j, 128 * j + 128)
        pair, dy_pair = values_f[:, here], dy[:, here]
        outs = []
        for h in (2 * j, 2 * j + 1):
            own = jnp.where(first if h % 2 == 0 else ~first, pair, 0.0).astype(BF16)
            decays = decay_of(cum, cum_t[0], h, mask)
            scaled = dot(dy_pair, own, 1, 1) * decays
            step_row = step_t[0, h : h + 1]
            product = scaled * inner
            rows[h : h + 1] = jnp.sum(product, axis=0, keepdims=True)
            dcum = jnp.where(
                lane == h, jnp.sum(product * step_row, axis=1, keepdims=True), dcum
            )
            dinner = dinner + scaled * step_row
            outs.append(dot((inner * decays * step_row).astype(BF16), dy_pair, 0, 0))
        dval_o[:, here] = jnp.where(first, outs[0], outs[1]) + skip[:, here] * dy_f[:, here]
    dstep = rows[...].T
    dstep_o[...] = dstep
    low = states[0].astype(BF16)
    grad_exp = dy_f * expand(jnp.exp(cum[...]))
    dcum_o[...] = dcum - dstep * step_val[...] + head_sums(grad_exp * dot(reads, low, 1, 1))
    dstate_o[:, :STATE] = split_dot(dinner, reads, 0)
    dstate_o[:, STATE:] = dot(grad_exp.astype(BF16), low) + split_dot(dinner, keys, 1)

    @pl.when(step == BLOCKS - 1)
    def _():
        skip_o[...] = head_sums(skips[...])


def states_kernel(step, vals, cum, step_val, sig, states, read, arriving, heads, dval, dcum, dstep, dstate,
                  dval_o, state_o, low_o, heads_o, carry):
    @pl.when(step == 0)
    def _():
        carry[...] = arriving[...]
        heads_o[...] = jnp.zeros_like(heads_o)

    out = carry[...]
    last = cum[GROUP - 1 :]
    decay = jnp.exp(last)
    carry[...] = by_head(decay, out) + read[0]
    product = out * states[0]
    row = lanes(1)
    dlast = jnp.zeros((1, 128), F32)
    for h in range(2 * PAIRS):
        own = jnp.sum(product[HEAD * h : HEAD * h + HEAD], axis=0, keepdims=True)
        dlast = jnp.where(row == h, jnp.sum(own, axis=1, keepdims=True), dlast)
    dlast = dlast * decay
    fresh = out.astype(BF16)
    keys = vals[:, LOCAL : LOCAL + STATE]
    values_f = vals[:, :LOCAL].astype(F32)
    to_end = jnp.exp(last - cum[...])
    scales = step_val[...] * to_end
    wide = expand(scales)
    dweighted = dot(keys, fresh, 1, 1)
    dval_o[...] = dval[...] + dweighted * wide
    state_o[:, :STATE] = (
        dstate[:, :STATE] + dot((values_f * wide).astype(BF16), fresh)
    ).astype(BF16)
    state_o[:, STATE:] = dstate[:, STATE:].astype(BF16)
    dscales = head_sums(dweighted * values_f)
    spill = dscales * scales
    dlast = dlast + jnp.sum(spill, axis=0, keepdims=True)
    at_end = lax.broadcasted_iota(jnp.int32, (GROUP, 128), 0) == GROUP - 1
    full_cum = dcum[...] - spill + jnp.where(at_end, dlast, 0.0)
    drate = dot(lower().astype(F32), full_cum, 0, 0, precision=HIGH)
    rate = jnp.exp(heads[1:2])
    total_step = dstep[...] + dscales * to_end - rate * drate
    pre = total_step * sig[...]
    low_o[...] = pre.astype(BF16)
    heads_o[0:1] += jnp.sum(pre, axis=0, keepdims=True)
    heads_o[1:2] += -rate * jnp.sum(drate * step_val[...], axis=0, keepdims=True)


def next_rows(block, extra):
    keep = lax.broadcasted_iota(jnp.int32, block.shape, 0) < CONV - 1
    return jnp.where(keep, block * extra, 0.0)


def value_kernel(step, where, dval, slope, pre, dgate, dstep, normed, full, conv, values_next,
                 slope_next, part_o, dvalue_o, small_o, padded, total):
    @pl.when(step == 0)
    def _():
        small_o[...] = jnp.zeros_like(small_o)
        own = values_next[0:8] * slope_next[0:8, :LOCAL]
        padded[GROUP:, :LOCAL] = next_rows(own, jnp.where(where[0] == 0, 1.0, 0.0))
        total[...] = jnp.zeros_like(total)

    @pl.when(step > 0)
    def _():
        padded[GROUP:, :LOCAL] = padded[0:8, :LOCAL]

    grad = dval[...] * slope[:, :LOCAL]
    padded[0:GROUP, :LOCAL] = grad
    pre_f = pre[:, :LOCAL].astype(F32)
    dinput = jnp.zeros((GROUP, LOCAL), F32)
    for k in range(CONV):
        moved = padded[CONV - 1 - k : CONV - 1 - k + GROUP, :LOCAL]
        dinput = dinput + conv[k : k + 1, :LOCAL] * moved
        small_o[k : k + 1] += jnp.sum(moved * pre_f, axis=0, keepdims=True)
    small_o[4:5] += jnp.sum(grad, axis=0, keepdims=True)
    low = dinput.astype(BF16)
    total[...] += dot(normed[...], jnp.concatenate([low, dstep[...]], axis=1), 0, 0)
    part_o[...] = dot(low, full[:, :LOCAL], 1, 1) + dot(
        jnp.concatenate([dstep[...], dgate[...]], axis=1), full[:, MIX:PROJ], 1, 1
    )

    @pl.when(step == BLOCKS - 1)
    def _():
        dvalue_o[...] = gridded(total[:, :LOCAL])


def maps_kernel(step, where, state, slope, pre, normed, stream, full, conv, state_next, slope_next,
                dgain, heads, skip, part_in, part_o, dstate_o, small_o, padded, total, thin):
    block = BLOCKS - 1 - step

    @pl.when(step == 0)
    def _():
        own = state_next[...].astype(F32)[0:8] * slope_next[0:8, LOCAL:]
        padded[GROUP:, LOCAL:] = next_rows(own, jnp.where(where[0] == 0, 1.0, 0.0))
        total[...] = jnp.zeros_like(total)

    @pl.when(step > 0)
    def _():
        padded[GROUP:, LOCAL:] = padded[0:8, LOCAL:]

    grad = state[...].astype(F32) * slope[:, LOCAL:]
    padded[0:GROUP, LOCAL:] = grad
    pre_f = pre[:, LOCAL:].astype(F32)
    dinput = jnp.zeros((GROUP, 2 * STATE), F32)
    for k in range(CONV):
        moved = padded[CONV - 1 - k : CONV - 1 - k + GROUP, LOCAL:]
        dinput = dinput + conv[k : k + 1, LOCAL:] * moved
        small_o[6 + k : 7 + k, : 2 * STATE] += jnp.sum(moved * pre_f, axis=0, keepdims=True)
    small_o[10:11, : 2 * STATE] += jnp.sum(grad, axis=0, keepdims=True)
    total[...] += dot(normed[...], dinput.astype(BF16), 0, 0)
    once = (dinput * jnp.where(where[1] == block, 1.0, 0.0)).astype(BF16)
    part = part_in[...] + dot(once, full[:, LOCAL:MIX], 1, 1)
    part_o[...] = part.astype(BF16)
    source = stream[...].astype(F32)
    scale = lax.rsqrt(jnp.mean(source * source, axis=-1, keepdims=True) + EPS)
    dnorm = jnp.sum(part * source * scale, axis=0, keepdims=True)
    small_o[16:17] += dnorm[:, :LOCAL]
    small_o[17:18] += dnorm[:, LOCAL:]

    @pl.when(block == 0)
    def _():
        small_o[5:6] = dgain[0:1]
        small_o[11:12, :128] = heads[0:1]
        small_o[12:13, :128] = heads[1:2]
        small_o[13:14, :128] = skip[0:1]
        dstate_o[...] = gridded(jnp.concatenate([total[...], thin[:, LOCAL:]], axis=1))


def last_kernel(normed, stream, up, gain, branch, value, state, gate, last, small,
                out, mixed, value_o, state_o, step_o, gate_o, taps_o, state_taps_o, last_o, bias_o,
                state_bias_o, inner_o, step_bias_o, decay_o, skip_o):
    step = pl.program_id(0)
    source, grad = stream[...].astype(F32), normed[...].astype(F32)
    scale = lax.rsqrt(jnp.mean(source * source, axis=-1, keepdims=True) + EPS)
    scaled = grad * gain[0:1]
    inner = jnp.sum(scaled * source, axis=1, keepdims=True) / D
    out[...] = up[...].astype(F32) + (
        scale * scaled - source * (scale * scale * scale) * inner
    )

    mixed[...] = branch[...]

    @pl.when(step == 0)
    def _():
        value_o[...] = value[...]
        gate_o[...] = gate[...]
        state_o[...] = state[:, : 2 * STATE]
        step_o[...] = state[:, 2 * STATE : 2 * STATE + step_o.shape[1]]
        taps_o[...] = small[0:4]
        state_taps_o[...] = small[6:10, : 2 * STATE]
        last_o[...] = last[...]
        bias_o[...] = small[4, :]
        state_bias_o[...] = small[10, : 2 * STATE]
        inner_o[...] = small[5, :]
        step_bias_o[...] = small[11, : step_bias_o.shape[0]]
        decay_o[...] = small[12, : decay_o.shape[0]]
        skip_o[...] = small[13, : skip_o.shape[0]]


def finish(normed, stream, up, gain, branch, value, state, gate, last, small, heads_here):
    by_block = pl.BlockSpec((GROUP, D), lambda g: (g, 0))

    def all_of(*shape):
        return pl.BlockSpec(shape, lambda g: (0,) * len(shape))

    owned = (ROWS, LOCAL)
    small_shapes = [
        owned, (ROWS, 2 * STATE), (ROWS, heads_here), owned, (CONV, LOCAL), (CONV, 2 * STATE),
        owned, (LOCAL,), (2 * STATE,), (LOCAL,), (heads_here,), (heads_here,), (heads_here,),
    ]
    return pl.pallas_call(
        last_kernel,
        grid=(BLOCKS,),
        in_specs=[
            by_block,
            by_block,
            by_block,
            all_of(8, D),
            by_block,
            all_of(*owned),
            all_of(*owned),
            all_of(*owned),
            all_of(*owned),
            all_of(24, LOCAL),
        ],
        out_specs=(by_block, by_block, *[all_of(*shape) for shape in small_shapes]),
        out_shape=(
            jax.ShapeDtypeStruct(stream.shape, F32),
            jax.ShapeDtypeStruct(stream.shape, BF16),
            *[jax.ShapeDtypeStruct(shape, F32) for shape in small_shapes],
        ),
        compiler_params=pltpu.CompilerParams(vmem_limit_bytes=60 * 1024 * 1024),
    )(normed, stream, up, gain, branch, value, state, gate, last, small)


def place_of(step, backward):
    return (BLOCKS - 1 - step) if backward else step


def tokens_spec(columns, backward=False):
    def view(ref, step):
        start = pl.multiple_of(place_of(step, backward) * GROUP, GROUP)
        return ref.at[pl.ds(start, GROUP)]

    return view


def cube_spec(rows, columns, backward=False):
    return lambda ref, step: ref.at[pl.ds(place_of(step, backward), 1)]


def row_spec(rows, backward=False):
    def view(ref, step):
        start = pl.multiple_of(place_of(step, backward) * GROUP, GROUP)
        return ref.at[:, pl.ds(start, GROUP)]

    return view


def whole(*shape):
    return lambda ref, step: ref


class Flat:
    def __init__(self, ref):
        self.ref = ref

    def __getitem__(self, key):
        found = self.ref[:, :, :, key[1]]
        return found.reshape(D, found.shape[-1])


def gridded(total):
    return total.astype(BF16).reshape(SIDE, SIDE, ROWS, total.shape[-1])


def sweep(kernel, pairs, start=0, stop=BLOCKS):
    def step(index, carry):
        kernel(index, *[item[1](item[0], index) if type(item) is tuple else item for item in pairs])
        return carry

    lax.fori_loop(start, stop, step, 0)


COUNT = BLOCKS * GROUP
HALF = COUNT // 2
KEPT = dict(
    full=((SIDE, SIDE, ROWS, WIDE), BF16),
    edge_in=((16, D), BF16),
    conv=((8, MIX), F32),
    heads=((8, 128), F32),
    gain=((1, LOCAL), F32),
    normed=((COUNT, D), BF16),
    pre=((COUNT, MIX), BF16),
    slope=((COUNT, MIX), F32),
    vals=((COUNT, MIX), BF16),
    step_val=((COUNT, 128), F32),
    sig=((COUNT, 128), F32),
    cum=((COUNT, 128), F32),
    cum_t=((BLOCKS, 8, GROUP), F32),
    step_t=((BLOCKS, 8, GROUP), F32),
    fresh=((BLOCKS, LOCAL, STATE), F32),
    leaving=((LOCAL, STATE), F32),
    padded=((GROUP + 8, MIX), F32),
    entering=((LOCAL, STATE), F32),
    local=((COUNT, LOCAL), F32),
    back=((COUNT, LOCAL), F32),
    gate=((COUNT, LOCAL), F32),
    ssd=((COUNT, LOCAL), F32),
    states=((BLOCKS, LOCAL, STATE), F32),
    sums=((8, COUNT), F32),
    sums_all=((8, COUNT), F32),
    sums_in=((4, 8, COUNT), F32),
    state=((LOCAL, STATE), F32),
    normal=((COUNT, LOCAL), BF16),
    dy=((COUNT, LOCAL), BF16),
    dgate=((COUNT, LOCAL), BF16),
    read=((BLOCKS, LOCAL, STATE), F32),
    returning=((LOCAL, STATE), F32),
    arriving=((LOCAL, STATE), F32),
    dgain=((8, LOCAL), F32),
    branch=((COUNT, D), BF16),
    dout_w=((SIDE, SIDE, ROWS, LOCAL), BF16),
    dgate_w=((SIDE, SIDE, ROWS, LOCAL), BF16),
    dcum=((COUNT, 128), F32),
    dstep=((COUNT, 128), F32),
    dstate=((COUNT, 2 * STATE), F32),
    skip=((8, 128), F32),
    skips=((8, LOCAL), F32),
    rows=((128, GROUP), F32),
    state_part=((COUNT, 2 * STATE), BF16),
    state_total=((COUNT, 2 * STATE), BF16),
    half_in=((HALF, 2 * STATE), BF16),
    chip_sum=((HALF, 2 * STATE), BF16),
    over_in=((HALF, 2 * STATE), BF16),
    values_in=((16, LOCAL), F32),
    slopes_in=((16, MIX), F32),
    state_in=((16, 2 * STATE), BF16),
    dstep_low=((COUNT, 128), BF16),
    head_rows=((8, 128), F32),
    part=((COUNT, D), BF16),
    dvalue_w=((SIDE, SIDE, ROWS, LOCAL), BF16),
    dstate_w=((SIDE, SIDE, ROWS, LOCAL), BF16),
    small=((24, LOCAL), F32),
    total=((D, LOCAL + 128), F32),
    total_maps=((D, 2 * STATE), F32),
    part_sum=((COUNT, D), F32),
    own=((4, ROWS, LOCAL), BF16),
    own_in=((4, ROWS, LOCAL), BF16),
    small_y=((SIDE, 24, LOCAL), F32),
    small_z=((SIDE, 24, LOCAL), F32),
    small_c=((24, LOCAL), F32),
    small_t=((SIDE, 8, LOCAL), F32),
    small_now=((3, 24, LOCAL), F32),
)
for name in ("gate", "out", "value", "state"):
    KEPT["held_" + name] = ((6, 2, ROWS, LOCAL), BF16)
    KEPT["passed_" + name] = ((2, 2, ROWS, LOCAL), BF16)
    KEPT["mid_" + name] = ((SIDE, ROWS, LOCAL), BF16)
    KEPT["second_" + name] = ((SIDE, ROWS, LOCAL), BF16)
for name in ("mixed", "normed"):
    KEPT["half_" + name] = ((2, COUNT // 4, D), BF16)
    KEPT["over_out_" + name] = ((COUNT // 4, D), BF16)
    KEPT["over_in_" + name] = ((COUNT // 4, D), BF16)
SLOTS = 116


def block_kernel(shard, stream, up, taps_value, taps_state, singles, value_out, state_out, gate_out,
                 w_out_out, small_out, normed_out, mixed_out, gain_zero, *kept):
    by_name = dict(zip(KEPT, kept))
    m = types.SimpleNamespace(**by_name)
    send, recv, own_sem = kept[len(KEPT) :]
    z, y, along_y, along_z = place()
    ctx, tp = lax.axis_index("ctx"), lax.axis_index("tp")
    core, chip = lax.rem(tp, 2), lax.div(tp, 2)
    y_peers, z_peers, partner, tp_peers = all_peers(along_y, along_z)
    twin, across = {"tp": tp + 1 - 2 * core}, {"tp": tp + 2 - 4 * chip}
    beyond = {"ctx": 1 - ctx, "tp": tp + 1 - 2 * core}
    greet(y_peers + z_peers + [partner, beyond] + tp_peers)
    open_sends = []
    conv, heads, gain = m.conv, m.heads, m.gain
    conv[0:4, :LOCAL] = taps_value[...]
    conv[0:4, LOCAL:] = taps_state[...]
    conv[4:5] = singles[:, :MIX]
    gain[...] = singles[:, MIX : MIX + LOCAL]
    for index in range(3):
        first = MIX + LOCAL + 128 * index
        heads[index : index + 1] = singles[:, first : first + 128]

    def to(source, target, slot, where):
        item = remote(source, target, send.at[slot], recv.at[slot], where)
        item.start()
        open_sends.append(item)
        return item

    full = Flat(m.full)
    at = tokens_spec(1)
    back_at = tokens_spec(1, True)
    cube, back_cube = cube_spec(1, 1), cube_spec(1, 1, True)
    row, back_row = row_spec(8), row_spec(8, True)

    def f(ref):
        return (ref, at)

    def r(ref):
        return (ref, back_at)

    def fc(ref):
        return (ref, cube)

    def rc(ref):
        return (ref, back_cube)

    gathers = [
        Gather(shard, m.full, LOCAL * index, index % 2 == 0, send, recv, 9 * index)
        for index in range(4)
    ]
    halo = to(stream.at[pl.ds(COUNT - 16, 16)], m.edge_in, 36, partner)
    keep = pltpu.make_async_copy(shard, m.full.at[z, y], own_sem)
    keep.start()
    keep.wait()
    gathers[0].turn()
    gathers[1].turn()
    gathers[0].relay()
    gathers[1].relay()
    gathers[2].turn()
    gathers[3].turn()
    gathers[0].finish()
    gathers[1].finish()
    halo.wait_recv()
    project = [
        [ctx], (stream, at), m.edge_in, full, conv, heads, f(m.normed), f(m.pre), f(m.slope),
        f(m.vals), f(m.step_val), f(m.sig), f(m.cum), fc(m.cum_t), fc(m.step_t), fc(m.fresh),
        m.leaving, gain_zero, m.padded,
    ]
    sweep(project_kernel, project, 0, 2)
    gathers[2].relay()
    gathers[3].relay()
    sweep(project_kernel, project, 2, 4)
    entering = to(m.leaving, m.entering, 37, partner)
    gathers[2].finish()
    gathers[3].finish()
    sweep(
        inside_kernel,
        [
            f(m.vals), f(m.cum), fc(m.cum_t), fc(m.step_t), heads, (up, at), f(m.normed), full,
            f(m.local), f(m.back), f(m.gate),
        ],
    )
    entering.wait_recv()
    m.state[...] = m.entering[...] * jnp.where(ctx == 1, 1.0, 0.0)
    sweep(
        output_kernel,
        [
            f(m.vals), f(m.local), f(m.gate), fc(m.fresh), f(m.cum), m.state, f(m.back), gain,
            f(m.ssd), fc(m.states), (m.sums, row), m.state,
        ],
    )
    to_tp = spread(m.sums, m.sums_in, tp, tp_peers, send, recv, 38)
    m.sums_all[...] = fold(m.sums_in, tp, m.sums[...], to_tp)
    open_sends.extend(to_tp)
    sweep(
        gates_kernel,
        [
            r(m.ssd), r(m.gate), r(m.back), (m.sums_all, back_row), gain, r(m.vals), r(m.cum),
            full, r(m.normal), r(m.dy), r(m.dgate), rc(m.read), m.returning, m.dgain,
            r(m.branch),
        ],
    )
    arriving = to(m.returning, m.arriving, 41, partner)
    mixed = PairSum(
        m.branch, mixed_out, m.half_mixed, m.over_out_mixed, m.over_in_mixed,
        send, recv, 42,
    )
    m.dout_w[...] = gridded(dot(up[...], m.normal[...], 0, 0))
    m.dgate_w[...] = gridded(dot(m.normed[...], m.dgate[...], 0, 0))
    mixed.cross()

    def weight_sum(name, z_first, slot):
        scratch = [by_name[kind + name] for kind in ("held_", "passed_", "mid_", "second_")]
        return WeightSum(by_name["d" + name + "_w"], z_first, scratch, send, recv, slot)

    gate_sum, out_sum = weight_sum("gate", True, 48), weight_sum("out", False, 57)
    blocks = [
        f(m.dy), f(m.vals), f(m.cum), fc(m.cum_t), f(m.step_val), fc(m.step_t), fc(m.states), heads,
        f(m.local), f(m.dcum), f(m.dstep), f(m.dstate), m.skip, m.skips, m.rows,
    ]
    sweep(blocks_kernel, blocks, 0, 2)
    gate_sum.ring.relay()
    out_sum.ring.relay()
    sweep(blocks_kernel, blocks, 2, 4)
    mixed.close(stream)
    gate_sum.turn()
    out_sum.turn()
    arriving.wait_recv()
    m.state[...] = m.arriving[...] * jnp.where(ctx == 0, 1.0, 0.0)
    sweep(
        states_kernel,
        [
            r(m.vals), r(m.cum), r(m.step_val), r(m.sig), rc(m.states), rc(m.read), m.state,
            heads, r(m.local), r(m.dcum), r(m.dstep), r(m.dstate), r(m.ssd), r(m.state_part),
            r(m.dstep_low), m.head_rows, m.state,
        ],
    )
    mine = pl.ds(pl.multiple_of(core * HALF, HALF), HALF)
    theirs = pl.ds(pl.multiple_of((1 - core) * HALF, HALF), HALF)
    to_twin = to(m.state_part.at[theirs], m.half_in, 66, twin)
    early = [
        to(m.ssd.at[0:16], m.values_in, 67, partner),
        to(m.slope.at[0:16], m.slopes_in, 68, partner),
    ]
    to_twin.wait_recv()
    m.chip_sum[...] = (
        m.state_part[mine].astype(F32) + m.half_in[...].astype(F32)
    ).astype(BF16)
    over = to(m.chip_sum, m.over_in, 69, across)
    m.own[0] = gate_sum.total().astype(BF16)
    m.own[1] = out_sum.total().astype(BF16)
    mixed.relay()
    for item in early:
        item.wait_recv()
    values = [
        [ctx], r(m.ssd), r(m.slope), r(m.pre), r(m.dgate), r(m.dstep_low), r(m.normed), full, conv,
        m.values_in, m.slopes_in, r(m.part_sum), m.dvalue_w, m.small, m.padded, m.total,
    ]
    sweep(value_kernel, values, 0, 3)
    over.wait_recv()
    total = m.state_total
    total[mine] = (m.chip_sum[...].astype(F32) + m.over_in[...].astype(F32)).astype(BF16)
    back = to(total.at[mine], total.at[mine], 70, twin)
    head = total.at[0:16]
    late = remote(head, m.state_in, send.at[71], recv.at[71], partner)
    late_twin = remote(head, m.state_in, send.at[72], recv.at[71], beyond)

    @pl.when(core == 0)
    def _():
        late.start()
        late_twin.start()

    pair = to(m.own.at[0:2], m.own_in.at[0:2], 73, partner)
    sweep(value_kernel, values, 3, 4)
    value_sum = weight_sum("value", True, 80)
    back.wait_recv()
    late.wait_recv()
    sweep(
        maps_kernel,
        [
            [ctx, tp], r(m.state_total), r(m.slope), r(m.pre), r(m.normed), (stream, back_at), full,
            conv, m.state_in, m.slopes_in, m.dgain, m.head_rows, m.skip, r(m.part_sum), r(m.part),
            m.dstate_w, m.small, m.padded, m.total_maps, m.total,
        ],
    )
    normed = PairSum(
        m.part, normed_out, m.half_normed, m.over_out_normed, m.over_in_normed,
        send, recv, 74,
    )
    state_sum = weight_sum("state", False, 89)
    small_now, small_z, small_y = m.small_now, m.small_z, m.small_y
    to_y = spread(m.small, small_y, y, y_peers, send, recv, 98)
    normed.cross()
    value_sum.ring.relay()
    state_sum.ring.relay()
    small_now[0] = fold(small_y, y, m.small[...], to_y)
    to_z = spread(small_now.at[0], small_z, z, z_peers, send, recv, 101)
    value_sum.turn()
    state_sum.turn()
    small_now[1] = fold(small_z, z, small_now[0], to_z)
    to_ctx = to(small_now.at[1], m.small_c, 104, partner)
    normed.close()
    m.own[2] = value_sum.total().astype(BF16)
    m.own[3] = state_sum.total().astype(BF16)
    pair_late = to(m.own.at[2:4], m.own_in.at[2:4], 105, partner)
    to_ctx.wait_recv()
    small_now[2] = small_now[1] + m.small_c[...]
    to_all = spread(small_now.at[2, pl.ds(16, 8)], m.small_t, tp, tp_peers, send, recv, 106)
    normed.relay()
    pair.wait_recv()
    gate_out[...] = m.own[0].astype(F32) + m.own_in[0].astype(F32)
    w_out_out[...] = m.own[1].astype(F32) + m.own_in[1].astype(F32)
    pair_late.wait_recv()
    value_out[...] = m.own[2].astype(F32) + m.own_in[2].astype(F32)
    state_out[...] = m.own[3].astype(F32) + m.own_in[3].astype(F32)
    small_out[0:16] = small_now[2, 0:16]
    small_out[16:24] = fold(m.small_t, tp, small_now[2, 16:24], to_all)
    normed.finish()
    mixed.finish()
    for item in gathers:
        item.close()
    for item in (gate_sum, out_sum, value_sum, state_sum):
        item.finish()

    @pl.when(core == 0)
    def _():
        late.wait_send()
        late_twin.wait_send()

    for item in open_sends + to_y + to_z + to_all:
        item.wait_send()


def per_device(
    stream,
    norm_gain,
    w_gate,
    w_value,
    w_step,
    w_state,
    w_out,
    conv_value,
    conv_value_bias,
    conv_state,
    conv_state_bias,
    step_bias,
    decay_log,
    skip_gain,
    inner_gain,
    cotangent,
):
    count = stream.shape[1]
    heads_here = step_bias.shape[0]
    rows, up = stream[0], cotangent[0]
    shard = jnp.concatenate(
        [
            w_value,
            w_state,
            w_step,
            norm_gain[:, None],
            jnp.zeros((ROWS, 128 - heads_here - 1), BF16),
            w_gate,
            w_out.T,
        ],
        axis=1,
    )
    spare = jnp.zeros((128 - heads_here,), F32)
    singles = jnp.concatenate(
        [
            conv_value_bias, conv_state_bias, inner_gain, step_bias, spare, decay_log, spare,
            skip_gain, spare,
        ]
    )[None]
    taps_value, taps_state = conv_value, conv_state
    owned = jax.ShapeDtypeStruct((ROWS, LOCAL), F32)
    wide = jax.ShapeDtypeStruct((COUNT, D), BF16)
    own_value, own_state, own_gate, own_out, totals, dnormed, mixed, gain_zero = pl.pallas_call(
        block_kernel,
        in_specs=[VM] * 6,
        out_specs=(VM,) * 8,
        out_shape=(
            owned,
            owned,
            owned,
            owned,
            jax.ShapeDtypeStruct((24, LOCAL), F32),
            wide,
            wide,
            jax.ShapeDtypeStruct((8, D), F32),
        ),
        scratch_shapes=[
            *[pltpu.VMEM(shape, dtype) for shape, dtype in KEPT.values()],
            DMA((SLOTS,)),
            DMA((SLOTS,)),
            DMA,
        ],
        compiler_params=params(1, 56),
    )(shard, rows, up, taps_value, taps_state, singles)
    (
        d_stream, mixed, value_w, state_w, step_w, gate_w, taps, state_taps, out_w, bias,
        state_bias, inner_w, step_bias_w, decay_w, skip_w,
    ) = finish(
        dnormed, rows, up, gain_zero, mixed, own_value, own_state, own_gate, own_out, totals,
        heads_here,
    )
    gain_total = totals[16:18].reshape(D)
    return (
        mixed[None],
        d_stream[None],
        lax.dynamic_slice_in_dim(gain_total, lax.axis_index("dp") * ROWS, ROWS),
        gate_w,
        value_w,
        step_w,
        state_w,
        out_w.T,
        taps,
        bias,
        state_taps,
        state_bias,
        step_bias_w,
        decay_w,
        skip_w,
        inner_w,
    )


def solution(mesh):
    in_specs = (
        P("dp", "ctx", None),
        P("dp"),
        P("dp", "tp"),
        P("dp", "tp"),
        P("dp", "tp"),
        P("dp", None),
        P("tp", "dp"),
        P(None, "tp"),
        P("tp"),
        P(),
        P(),
        P("tp"),
        P("tp"),
        P("tp"),
        P("tp"),
        P("dp", "ctx", None),
    )
    out_specs = (
        P("dp", "ctx", None),
        P("dp", "ctx", None),
        P("dp"),
        P("dp", "tp"),
        P("dp", "tp"),
        P("dp", "tp"),
        P("dp", None),
        P("tp", "dp"),
        P(None, "tp"),
        P("tp"),
        P(),
        P(),
        P("tp"),
        P("tp"),
        P("tp"),
        P("tp"),
    )
    return jax.shard_map(
        per_device, mesh=mesh, in_specs=in_specs, out_specs=out_specs, check_vma=False
    )
```
